32 devices in a mesh: region: 8 (over z, x), neuron: 4 (over y, core).
Axes of the slice: x: 2, y: 2, z: 4, core: 2. Of those that a mesh axis runs over, the one named last changes fastest.
Arguments:
- counts: bfloat16 [8, 5120, 1024], P('region', 'neuron'), may hold values from 0 to 3, as said below
- latents: bfloat16 [64, 1024], P(None, 'neuron'), may hold values from -5 to 5
- loadings: bfloat16 [8, 64, 5120], P('region', None, 'neuron'), may hold values from -0.75 to 0.75
- bias: float32 [8, 5120], P('region', 'neuron'), may hold values from -3 to 3
- delays: int32 [8, 64], P('region'), may hold values from 0 to 128
- recorded: int32 [8], P('region'), may hold values from 256 to 1024, as said below
Outputs:
- grad_latents: float32 [64, 1024], P(None, 'neuron')
- grad_loadings: float32 [8, 64, 5120], P('region', None, 'neuron')
- grad_bias: float32 [8, 5120], P('region', 'neuron')
The draws below stay inside these ranges and needn't reach their ends.
Inputs may be any that keep to these rules, and one draw needn't show every extreme that they name: At least one region is recorded over all 1024 bins. `counts`: whole numbers.
All inputs are finite; a program needn't handle non-finite values.
Results may differ from the reference program's by a relative error of at most 0.0021.
Values may be sent and summed in bfloat16 or wider, within the bound.
No kernel may reach another device: no remote copies, remote signals or barrier semaphores. Data moves between devices by JAX's collectives and lax.ppermute only.
A program may use at most 64 MiB of HBM per device.

```python
import jax
import jax.numpy as jnp
from jax import lax

L = 64
REGIONS = 8
NEURONS = 5120
TIME = 1024
DELAY_MAX = 128


def draw_recorded(key, part):
    first_key, second_key = jax.random.split(jax.random.fold_in(key, 17))
    full = jax.random.randint(first_key, (), 0, REGIONS)
    spans = jax.random.randint(second_key, (REGIONS,), TIME // 4, TIME + 1)
    return jnp.where(jnp.arange(REGIONS) == full, TIME, spans).astype(jnp.int32)


def draw_counts(key, part):
    values = jax.random.randint(jax.random.fold_in(key, 29), (REGIONS, NEURONS, TIME), 0, 4)
    return values.astype(jnp.float32).astype(jnp.bfloat16)


def with_ends(drawn, own_key, smallest, largest):
    place = [jax.random.randint(jax.random.fold_in(own_key, axis), (), 0, length) for axis, length in enumerate(drawn.shape)]
    main_axis = drawn.shape.index(max(drawn.shape))
    next_to = place[:main_axis] + [(place[main_axis] + 1) % drawn.shape[main_axis]] + place[main_axis + 1:]
    return drawn.at[tuple(place)].set(smallest).at[tuple(next_to)].set(largest)


def block_scale(rng, extent, cuts, smallest, top_value):
    factor_of = 1.0
    for axis_at, parts in cuts:
        steps = jax.random.uniform(jax.random.fold_in(jax.random.fold_in(rng, 6), axis_at), (parts,), jnp.float32, smallest / len(cuts), top_value / len(cuts))
        factor_of = factor_of * jnp.repeat(jnp.exp(steps), extent[axis_at] // parts).reshape((-1,) + (1,) * (len(extent) - 1 - axis_at))
    return factor_of


def normal_values(stream_key, shape, width, most, cuts=(), kind=jnp.bfloat16):
    result = jax.random.normal(stream_key, shape, jnp.float32) * width
    if len(cuts) > 0:
        result = block_scale(stream_key, shape, cuts, -0.22, 0.18) * result
    return jnp.clip(result, min=-most, max=most).astype(kind)


def setup_inputs(seed: int = 0) -> dict:
    seeds = jax.random.split(jax.random.key(seed), 7)
    counts = draw_counts(jax.random.fold_in(seeds[6], 71), 0)
    latents = normal_values(seeds[1], (L, TIME), 1.0, 5.0, ((1, 4),))
    loadings = normal_values(seeds[2], (REGIONS, L, NEURONS), L ** -0.5, 0.75, ((0, 8), (2, 4)))
    bias = normal_values(seeds[3], (REGIONS, NEURONS), 0.5, 3.0, ((0, 8), (1, 4)), jnp.float32)
    delays = with_ends(jax.random.randint(seeds[4], (REGIONS, L), 0, DELAY_MAX + 1), jax.random.fold_in(seeds[4], 1), 0, DELAY_MAX).astype(jnp.int32)
    recorded = draw_recorded(jax.random.fold_in(seeds[6], 71), 0)
    return dict(counts=counts, latents=latents, loadings=loadings, bias=bias, delays=delays, recorded=recorded)


def delay_rows(source, delay_row, offset, span):
    def one_row(row, delay):
        return lax.dynamic_slice_in_dim(row, (offset - delay).astype(jnp.int32), span)
    return jax.vmap(one_row)(source, delay_row)


def advance_rows(source, delay_row, span):
    def one_row(row, delay):
        return lax.dynamic_slice_in_dim(row, delay.astype(jnp.int32), span)
    return jax.vmap(one_row)(source, delay_row)


def reference(counts, latents, loadings, bias, delays, recorded):
    padded = jnp.pad(latents, ((0, 0), (DELAY_MAX, 0)))

    def one_region(items):
        count_rows, load, bias_row, delay_row, length = items
        shifted = delay_rows(padded, delay_row, DELAY_MAX, TIME)
        eta = jnp.dot(load.T, shifted, preferred_element_type=jnp.float32) + bias_row[:, None]
        bins = jnp.arange(TIME, dtype=jnp.int32)
        resid = jnp.where((bins < length)[None, :], jnp.exp(eta) - count_rows.astype(jnp.float32), 0.0)
        resid_low = resid.astype(jnp.bfloat16)
        grad_load = jnp.dot(shifted, resid_low.T, preferred_element_type=jnp.float32)
        grad_bias = jnp.sum(resid, axis=1)
        grad_shift = jnp.dot(load, resid_low, preferred_element_type=jnp.float32)
        extended = jnp.pad(grad_shift, ((0, 0), (0, DELAY_MAX)))
        return grad_load, grad_bias, advance_rows(extended, delay_row, TIME)

    grad_load, grad_bias, moved = lax.map(one_region, (counts, loadings, bias, delays, recorded))
    return jnp.sum(moved, axis=0), grad_load, grad_bias
```

```python
import functools

import jax
import jax.numpy as jnp
from jax import lax
from jax.experimental import pallas as pl
from jax.experimental.pallas import tpu as pltpu
from jax.sharding import PartitionSpec as P

LANES = 128
EXTRA = 16
F32 = jnp.float32
BF16 = jnp.bfloat16


def shift_tiles(tiles, delay, forward):
    lane = lax.broadcasted_iota(jnp.int32, delay.shape, 1)
    nothing = jnp.zeros_like(tiles[0])
    for level in range(7):
        amount = 1 << level
        chosen = (delay & amount) != 0
        if forward:
            turned = [pltpu.roll(tile, amount, 1) for tile in tiles]
            before = [nothing] + turned[:-1]
            moved = [jnp.where(lane < amount, b, t) for b, t in zip(before, turned)]
        else:
            turned = [pltpu.roll(tile, LANES - amount, 1) for tile in tiles]
            after = turned[1:] + [nothing]
            moved = [jnp.where(lane < LANES - amount, t, a) for t, a in zip(turned, after)]
        tiles = [jnp.where(chosen, m, tile) for m, tile in zip(moved, tiles)]
    chosen = delay >= LANES
    other = [nothing] + tiles[:-1] if forward else tiles[1:] + [nothing]
    return [jnp.where(chosen, o, tile) for o, tile in zip(other, tiles)]


def main_kernel(parts, axis, chunk, step, *refs):
    recorded_ref, delays_ref, bias_ref, load_ref, counts_ref = refs[:5]
    blocks = refs[5 : 5 + parts]
    grad_load_ref, grad_bias_ref = refs[5 + parts : 7 + parts]
    outs = refs[7 + parts : 7 + 2 * parts]
    whole, shifted, load_ext, grad_shift = refs[7 + 2 * parts :]
    lats, total = grad_shift.shape
    neurons = counts_ref.shape[0]
    width = total // parts
    me = lax.axis_index(axis)
    length = recorded_ref[0]

    diagonal = lax.broadcasted_iota(jnp.int32, (lats, lats), 0) == lax.broadcasted_iota(jnp.int32, (lats, lats), 1)
    spread = jnp.broadcast_to(delays_ref[...].astype(F32), (lats, lats))
    column = jnp.sum(jnp.where(diagonal, spread, 0.0), axis=1, keepdims=True)
    delay = jnp.broadcast_to(column, (lats, LANES)).astype(jnp.int32)

    load_ext[0:lats, :] = load_ref[...]
    bias = bias_ref[...]
    high = bias.astype(BF16).astype(F32)
    middle = (bias - high).astype(BF16).astype(F32)
    low = bias - high - middle
    row = lax.broadcasted_iota(jnp.int32, (EXTRA, neurons), 0)
    below = jnp.where(row == 0, high, jnp.where(row == 1, middle, jnp.where(row == 2, low, 0.0)))
    load_ext[lats:, :] = below.astype(BF16)

    for k in range(parts):
        start = lax.rem(me + parts - k, parts) * width
        whole[:, pl.ds(pl.multiple_of(start, width), width)] = blocks[k][...]
    tiles = [whole[:, j * LANES : (j + 1) * LANES].astype(F32) for j in range(total // LANES)]
    for j, tile in enumerate(shift_tiles(tiles, delay, True)):
        shifted[0:lats, j * LANES : (j + 1) * LANES] = tile.astype(BF16)
    row = lax.broadcasted_iota(jnp.int32, (EXTRA, total), 0)
    shifted[lats:, :] = jnp.where(row < 3, 1.0, 0.0).astype(BF16)

    grad_shift[...] = jnp.zeros_like(grad_shift)
    bins = lax.broadcasted_iota(jnp.int32, (1, total), 1)

    def visit(index, carry):
        rows = pl.ds(pl.multiple_of(index * chunk, chunk), chunk)
        load_part = load_ext[:, rows]
        grad_load = jnp.zeros((lats, chunk), F32)
        sums = jnp.zeros((chunk, LANES), F32)
        for begin in range(0, total, step):
            span = slice(begin, begin + step)
            piece = shifted[:, span]
            eta = lax.dot_general(load_part, piece, (((0,), (0,)), ((), ())), preferred_element_type=F32)
            observed = counts_ref[rows, span].astype(F32)
            resid = jnp.where(bins[:, span] < length, jnp.exp(eta) - observed, 0.0)
            resid_low = resid.astype(BF16)
            for j in range(step // LANES):
                sums = sums + resid[:, j * LANES : (j + 1) * LANES]
            grad_load = grad_load + lax.dot_general(
                piece[0:lats], resid_low, (((1,), (1,)), ((), ())), preferred_element_type=F32
            )
            grad_shift[:, span] += jnp.dot(load_part[0:lats], resid_low, preferred_element_type=F32)
        grad_load_ref[:, rows] = grad_load
        grad_bias_ref[:, rows] = jnp.sum(sums.T, axis=0, keepdims=True)
        return carry

    lax.fori_loop(0, neurons // chunk, visit, 0, unroll=total <= 1024)

    tiles = [grad_shift[:, j * LANES : (j + 1) * LANES] for j in range(total // LANES)]
    for j, tile in enumerate(shift_tiles(tiles, delay, False)):
        grad_shift[:, j * LANES : (j + 1) * LANES] = tile
    for k in range(parts):
        start = lax.rem(me + k, parts) * width
        outs[k][...] = grad_shift[:, pl.ds(pl.multiple_of(start, width), width)]


def split_kernel(parts, axis, *refs):
    pieces, outs, held = refs[: -parts - 1], refs[-parts - 1 : -1], refs[-1]
    me = lax.axis_index(axis)
    rows = held.shape[1]
    value = pieces[0][...]
    for piece in pieces[1:]:
        value = value + piece[...]
    for j in range(parts):
        held[j] = value[j * rows : (j + 1) * rows]
    for k in range(parts):
        outs[k][...] = held[lax.rem(me + k, parts)]


def join_kernel(parts, axis, *refs):
    pieces, out, held = refs[:parts], refs[parts], refs[parts + 1]
    me = lax.axis_index(axis)
    rows = held.shape[1]
    for k in range(parts):
        held[lax.rem(me + parts - k, parts)] = pieces[k][...]
    for j in range(parts):
        out[j * rows : (j + 1) * rows, :] = held[j]


def per_device(region_count, neuron_count, counts, latents, loadings, bias, delays, recorded):
    neurons, total = counts.shape[1:]
    lats, width = latents.shape
    vmem = pl.BlockSpec(memory_space=pltpu.VMEM)
    smem = pl.BlockSpec(memory_space=pltpu.SMEM)

    def send(value, axis, count, k):
        return lax.ppermute(value, axis, [(i, (i + k) % count) for i in range(count)])

    blocks = [latents] + [send(latents, "neuron", neuron_count, k) for k in range(1, neuron_count)]
    results = pl.pallas_call(
        functools.partial(main_kernel, neuron_count, "neuron", 256, 512),
        out_shape=[jax.ShapeDtypeStruct((lats, neurons), F32), jax.ShapeDtypeStruct((1, neurons), F32)]
        + [jax.ShapeDtypeStruct((lats, width), F32)] * neuron_count,
        in_specs=[smem] + [vmem] * (4 + neuron_count),
        out_specs=[vmem] * (2 + neuron_count),
        scratch_shapes=[
            pltpu.VMEM((lats, total), BF16),
            pltpu.VMEM((lats + EXTRA, total), BF16),
            pltpu.VMEM((lats + EXTRA, neurons), BF16),
            pltpu.VMEM((lats, total), F32),
        ],
        compiler_params=pltpu.CompilerParams(vmem_limit_bytes=40 * 1024 * 1024),
    )(recorded, delays, bias, loadings[0], counts[0], *blocks)
    grad_load, grad_bias = results[:2]
    parts = results[2:]
    arrived = [parts[0]] + [send(parts[k], "neuron", neuron_count, k) for k in range(1, neuron_count)]

    rows = lats // region_count
    pieces = pl.pallas_call(
        functools.partial(split_kernel, region_count, "region"),
        out_shape=[jax.ShapeDtypeStruct((rows, width), F32)] * region_count,
        in_specs=[vmem] * neuron_count,
        out_specs=[vmem] * region_count,
        scratch_shapes=[pltpu.VMEM((region_count, rows, width), F32)],
    )(*arrived)
    arrived = [pieces[0]] + [send(pieces[k], "region", region_count, k) for k in range(1, region_count)]
    mine = functools.reduce(jnp.add, arrived)
    arrived = [mine] + [send(mine, "region", region_count, k) for k in range(1, region_count)]
    grad_latents = pl.pallas_call(
        functools.partial(join_kernel, region_count, "region"),
        out_shape=jax.ShapeDtypeStruct((lats, width), F32),
        in_specs=[vmem] * region_count,
        out_specs=vmem,
        scratch_shapes=[pltpu.VMEM((region_count, rows, width), F32)],
    )(*arrived)
    return (grad_latents, grad_load[None], grad_bias)


def solution(mesh):
    placed = (
        P("region", "neuron", None),
        P(None, "neuron"),
        P("region", None, "neuron"),
        P("region", "neuron"),
        P("region", None),
        P("region"),
    )
    return jax.shard_map(
        functools.partial(per_device, mesh.shape["region"], mesh.shape["neuron"]),
        mesh=mesh,
        in_specs=placed,
        out_specs=(P(None, "neuron"), P("region", None, "neuron"), P("region", "neuron")),
        check_vma=False,
    )
```

```python
import functools

import jax
import jax.numpy as jnp
from jax import lax
from jax.experimental import pallas as pl
from jax.experimental.pallas import tpu as pltpu
from jax.sharding import PartitionSpec as P

LANES = 128
EXTRA = 16
F32 = jnp.float32
BF16 = jnp.bfloat16


def shift_tiles(tiles, delay, forward):
    lane = lax.broadcasted_iota(jnp.int32, delay.shape, 1)
    nothing = jnp.zeros_like(tiles[0])
    for level in range(7):
        amount = 1 << level
        chosen = (delay & amount) != 0
        if forward:
            turned = [pltpu.roll(tile, amount, 1) for tile in tiles]
            before = [nothing] + turned[:-1]
            moved = [jnp.where(lane < amount, b, t) for b, t in zip(before, turned)]
        else:
            turned = [pltpu.roll(tile, LANES - amount, 1) for tile in tiles]
            after = turned[1:] + [nothing]
            moved = [jnp.where(lane < LANES - amount, t, a) for t, a in zip(turned, after)]
        tiles = [jnp.where(chosen, m, tile) for m, tile in zip(moved, tiles)]
    chosen = delay >= LANES
    other = [nothing] + tiles[:-1] if forward else tiles[1:] + [nothing]
    return [jnp.where(chosen, o, tile) for o, tile in zip(other, tiles)]


def main_kernel(parts, chunk, step, *refs):
    recorded_ref, latents_ref, delays_hbm, bias_hbm, load_hbm, counts_hbm, out, grad_load_hbm, grad_bias_hbm = refs[:9]
    delays_ref, bias_ref, counts_ref, shifted, load_ext, grad_shift, grad_load_ref, grad_bias_ref = refs[9:17]
    small_sems, counts_sems, out_sems = refs[17:]
    lats, total = grad_shift.shape
    neurons = counts_ref.shape[0]
    width = total // parts
    pieces = neurons // chunk
    length = recorded_ref[0]

    small = [
        pltpu.make_async_copy(delays_hbm, delays_ref, small_sems.at[0]),
        pltpu.make_async_copy(bias_hbm, bias_ref, small_sems.at[1]),
        pltpu.make_async_copy(load_hbm, load_ext.at[pl.ds(0, lats)], small_sems.at[2]),
    ]
    for copy in small:
        copy.start()

    def counts_copy(index):
        rows = pl.ds(pl.multiple_of(index * chunk, chunk), chunk)
        return pltpu.make_async_copy(counts_hbm.at[rows], counts_ref.at[rows], counts_sems.at[index])

    def load_copy(index):
        rows = pl.ds(pl.multiple_of(index * chunk, chunk), chunk)
        return pltpu.make_async_copy(grad_load_ref.at[:, rows], grad_load_hbm.at[:, rows], out_sems.at[index])

    for index in range(pieces):
        counts_copy(index).start()
    row = lax.broadcasted_iota(jnp.int32, (EXTRA, total), 0)
    shifted[lats:, :] = jnp.where(row < 3, 1.0, 0.0).astype(BF16)
    grad_shift[...] = jnp.zeros_like(grad_shift)

    small[0].wait()
    diagonal = lax.broadcasted_iota(jnp.int32, (lats, lats), 0) == lax.broadcasted_iota(jnp.int32, (lats, lats), 1)
    spread = jnp.broadcast_to(delays_ref[...].astype(F32), (lats, lats))
    column = jnp.sum(jnp.where(diagonal, spread, 0.0), axis=1, keepdims=True)
    delay = jnp.broadcast_to(column, (lats, LANES)).astype(jnp.int32)
    tiles = [latents_ref[:, j * LANES : (j + 1) * LANES].astype(F32) for j in range(total // LANES)]
    for j, tile in enumerate(shift_tiles(tiles, delay, True)):
        shifted[0:lats, j * LANES : (j + 1) * LANES] = tile.astype(BF16)

    small[1].wait()
    bias = bias_ref[...]
    high = bias.astype(BF16).astype(F32)
    middle = (bias - high).astype(BF16).astype(F32)
    low = bias - high - middle
    row = lax.broadcasted_iota(jnp.int32, (EXTRA, neurons), 0)
    below = jnp.where(row == 0, high, jnp.where(row == 1, middle, jnp.where(row == 2, low, 0.0)))
    load_ext[lats:, :] = below.astype(BF16)
    small[2].wait()

    bins = lax.broadcasted_iota(jnp.int32, (1, total), 1)

    def visit(index, carry):
        rows = pl.ds(pl.multiple_of(index * chunk, chunk), chunk)
        counts_copy(index).wait()
        load_part = load_ext[:, rows]
        grad_load = jnp.zeros((lats, chunk), F32)
        sums = jnp.zeros((chunk, LANES), F32)
        for begin in range(0, total, step):
            span = slice(begin, begin + step)
            piece = shifted[:, span]
            eta = lax.dot_general(load_part, piece, (((0,), (0,)), ((), ())), preferred_element_type=F32)
            observed = counts_ref[rows, span].astype(F32)
            resid = jnp.where(bins[:, span] < length, jnp.exp(eta) - observed, 0.0)
            resid_low = resid.astype(BF16)
            for j in range(step // LANES):
                sums = sums + resid[:, j * LANES : (j + 1) * LANES]
            grad_load = grad_load + lax.dot_general(
                piece[0:lats], resid_low, (((1,), (1,)), ((), ())), preferred_element_type=F32
            )
            grad_shift[:, span] += jnp.dot(load_part[0:lats], resid_low, preferred_element_type=F32)
        grad_load_ref[:, rows] = grad_load
        load_copy(index).start()
        grad_bias_ref[:, rows] = jnp.sum(sums.T, axis=0, keepdims=True)
        return carry

    lax.fori_loop(0, pieces, visit, 0, unroll=total <= 1024)
    bias_copy = pltpu.make_async_copy(grad_bias_ref, grad_bias_hbm, small_sems.at[0])
    bias_copy.start()

    tiles = [grad_shift[:, j * LANES : (j + 1) * LANES] for j in range(total // LANES)]
    for j, tile in enumerate(shift_tiles(tiles, delay, False)):
        part, at = divmod(j * LANES, width)
        out[part, :, at : at + LANES] = tile
    for index in range(pieces):
        load_copy(index).wait()
    bias_copy.wait()


def per_device(region_count, neuron_count, counts, latents, loadings, bias, delays, recorded):
    neurons, total = counts.shape[1:]
    lats, width = latents.shape
    chunk = 256
    vmem = pl.BlockSpec(memory_space=pltpu.VMEM)
    smem = pl.BlockSpec(memory_space=pltpu.SMEM)
    hbm = pl.BlockSpec(memory_space=pltpu.HBM)

    whole = lax.all_gather(latents, "neuron", axis=1, tiled=True)
    partial, grad_load, grad_bias = pl.pallas_call(
        functools.partial(main_kernel, neuron_count, chunk, 512),
        out_shape=[
            jax.ShapeDtypeStruct((neuron_count, lats, width), F32),
            jax.ShapeDtypeStruct((lats, neurons), F32),
            jax.ShapeDtypeStruct((1, neurons), F32),
        ],
        in_specs=[smem, vmem, hbm, hbm, hbm, hbm],
        out_specs=[vmem, hbm, hbm],
        scratch_shapes=[
            pltpu.VMEM((1, lats), jnp.int32),
            pltpu.VMEM((1, neurons), F32),
            pltpu.VMEM((neurons, total), BF16),
            pltpu.VMEM((lats + EXTRA, total), BF16),
            pltpu.VMEM((lats + EXTRA, neurons), BF16),
            pltpu.VMEM((lats, total), F32),
            pltpu.VMEM((lats, neurons), F32),
            pltpu.VMEM((1, neurons), F32),
            pltpu.SemaphoreType.DMA((3,)),
            pltpu.SemaphoreType.DMA((neurons // chunk,)),
            pltpu.SemaphoreType.DMA((neurons // chunk,)),
        ],
        compiler_params=pltpu.CompilerParams(vmem_limit_bytes=58 * 1024 * 1024),
    )(recorded, whole, delays, bias, loadings[0], counts[0])

    arrived = lax.all_to_all(partial, "neuron", 0, 0)
    block = jnp.sum(arrived, axis=0).reshape(region_count, lats // region_count, width)
    mine = jnp.sum(lax.all_to_all(block, "region", 0, 0), axis=0)
    spread = jnp.broadcast_to(mine[None], block.shape)
    grad_latents = lax.all_to_all(spread, "region", 0, 0).reshape(lats, width)
    return (grad_latents, grad_load[None], grad_bias)


def solution(mesh):
    placed = (
        P("region", "neuron", None),
        P(None, "neuron"),
        P("region", None, "neuron"),
        P("region", "neuron"),
        P("region", None),
        P("region"),
    )
    return jax.shard_map(
        functools.partial(per_device, mesh.shape["region"], mesh.shape["neuron"]),
        mesh=mesh,
        in_specs=placed,
        out_specs=(P(None, "neuron"), P("region", None, "neuron"), P("region", "neuron")),
        check_vma=False,
    )
```

```python
import functools

import jax
import jax.numpy as jnp
from jax import lax
from jax.experimental import pallas as pl
from jax.experimental.pallas import tpu as pltpu
from jax.sharding import PartitionSpec as P

LANES = 128
EXTRA = 16
F32 = jnp.float32
BF16 = jnp.bfloat16


def shift_tiles(tiles, delay, forward):
    lane = lax.broadcasted_iota(jnp.int32, delay.shape, 1)
    nothing = jnp.zeros_like(tiles[0])
    for level in range(7):
        amount = 1 << level
        chosen = (delay & amount) != 0
        if forward:
            turned = [pltpu.roll(tile, amount, 1) for tile in tiles]
            before = [nothing] + turned[:-1]
            moved = [jnp.where(lane < amount, b, t) for b, t in zip(before, turned)]
        else:
            turned = [pltpu.roll(tile, LANES - amount, 1) for tile in tiles]
            after = turned[1:] + [nothing]
            moved = [jnp.where(lane < LANES - amount, t, a) for t, a in zip(turned, after)]
        tiles = [jnp.where(chosen, m, tile) for m, tile in zip(moved, tiles)]
    chosen = delay >= LANES
    other = [nothing] + tiles[:-1] if forward else tiles[1:] + [nothing]
    return [jnp.where(chosen, o, tile) for o, tile in zip(other, tiles)]


def main_kernel(parts, axis, chunk, step, *refs):
    recorded_ref, delays_hbm, bias_hbm, load_hbm, counts_hbm = refs[:5]
    held = parts.bit_length()
    blocks = refs[5 : 5 + held]
    keep, away, grad_load_hbm, grad_bias_hbm = refs[5 + held : 9 + held]
    whole, delays_ref, bias_ref, counts_ref, shifted, load_ext, grad_shift, grad_load_ref, grad_bias_ref = refs[9 + held : 18 + held]
    small_sems, counts_sems, out_sems = refs[18 + held :]
    me = lax.axis_index(axis)
    lats, total = grad_shift.shape
    neurons = counts_ref.shape[0]
    width = total // parts
    pieces = neurons // chunk
    length = recorded_ref[0]

    small = [
        pltpu.make_async_copy(delays_hbm, delays_ref, small_sems.at[0]),
        pltpu.make_async_copy(bias_hbm, bias_ref, small_sems.at[1]),
        pltpu.make_async_copy(load_hbm, load_ext.at[pl.ds(0, lats)], small_sems.at[2]),
    ]
    for copy in small:
        copy.start()

    def counts_copy(index):
        rows = pl.ds(pl.multiple_of(index * chunk, chunk), chunk)
        return pltpu.make_async_copy(counts_hbm.at[rows], counts_ref.at[rows], counts_sems.at[index])

    def load_copy(index):
        rows = pl.ds(pl.multiple_of(index * chunk, chunk), chunk)
        return pltpu.make_async_copy(grad_load_ref.at[:, rows], grad_load_hbm.at[:, rows], out_sems.at[index])

    for index in range(pieces):
        counts_copy(index).start()
    row = lax.broadcasted_iota(jnp.int32, (EXTRA, total), 0)
    shifted[lats:, :] = jnp.where(row < 3, 1.0, 0.0).astype(BF16)
    grad_shift[...] = jnp.zeros_like(grad_shift)

    small[0].wait()
    diagonal = lax.broadcasted_iota(jnp.int32, (lats, lats), 0) == lax.broadcasted_iota(jnp.int32, (lats, lats), 1)
    spread = jnp.broadcast_to(delays_ref[...].astype(F32), (lats, lats))
    column = jnp.sum(jnp.where(diagonal, spread, 0.0), axis=1, keepdims=True)
    delay = jnp.broadcast_to(column, (lats, LANES)).astype(jnp.int32)
    k = 0
    for ref in blocks:
        for j in range(ref.shape[0]):
            start = pl.multiple_of((me ^ k) * width, width)
            whole[:, pl.ds(start, width)] = ref[j]
            k += 1
    tiles = [whole[:, j * LANES : (j + 1) * LANES].astype(F32) for j in range(total // LANES)]
    for j, tile in enumerate(shift_tiles(tiles, delay, True)):
        shifted[0:lats, j * LANES : (j + 1) * LANES] = tile.astype(BF16)

    small[1].wait()
    bias = bias_ref[...]
    high = bias.astype(BF16).astype(F32)
    middle = (bias - high).astype(BF16).astype(F32)
    low = bias - high - middle
    row = lax.broadcasted_iota(jnp.int32, (EXTRA, neurons), 0)
    below = jnp.where(row == 0, high, jnp.where(row == 1, middle, jnp.where(row == 2, low, 0.0)))
    load_ext[lats:, :] = below.astype(BF16)
    small[2].wait()

    bins = lax.broadcasted_iota(jnp.int32, (1, total), 1)

    def visit(index, carry):
        rows = pl.ds(pl.multiple_of(index * chunk, chunk), chunk)
        counts_copy(index).wait()
        load_part = load_ext[:, rows]
        grad_load = jnp.zeros((lats, chunk), F32)
        sums = jnp.zeros((chunk, LANES), F32)
        for begin in range(0, total, step):
            span = slice(begin, begin + step)
            piece = shifted[:, span]
            eta = lax.dot_general(load_part, piece, (((0,), (0,)), ((), ())), preferred_element_type=F32)
            observed = counts_ref[rows, span].astype(F32)
            resid = jnp.where(bins[:, span] < length, jnp.exp(eta) - observed, 0.0)
            resid_low = resid.astype(BF16)
            for j in range(step // LANES):
                sums = sums + resid[:, j * LANES : (j + 1) * LANES]
            grad_load = grad_load + lax.dot_general(
                piece[0:lats], resid_low, (((1,), (1,)), ((), ())), preferred_element_type=F32
            )
            grad_shift[:, span] += jnp.dot(load_part[0:lats], resid_low, preferred_element_type=F32)
        grad_load_ref[:, rows] = grad_load
        load_copy(index).start()
        grad_bias_ref[:, rows] = jnp.sum(sums.T, axis=0, keepdims=True)
        return carry

    lax.fori_loop(0, pieces, visit, 0, unroll=total <= 1024)
    bias_copy = pltpu.make_async_copy(grad_bias_ref, grad_bias_hbm, small_sems.at[0])
    bias_copy.start()

    tiles = [grad_shift[:, j * LANES : (j + 1) * LANES] for j in range(total // LANES)]
    for j, tile in enumerate(shift_tiles(tiles, delay, False)):
        grad_shift[:, j * LANES : (j + 1) * LANES] = tile
    for k in range(parts):
        start = pl.multiple_of((me ^ k) * width, width)
        target = away if k % 2 else keep
        target[k // 2] = grad_shift[:, pl.ds(start, width)]
    for index in range(pieces):
        load_copy(index).wait()
    bias_copy.wait()


def per_device(region_count, neuron_count, counts, latents, loadings, bias, delays, recorded):
    neurons, total = counts.shape[1:]
    lats, width = latents.shape
    chunk = 256
    vmem = pl.BlockSpec(memory_space=pltpu.VMEM)
    smem = pl.BlockSpec(memory_space=pltpu.SMEM)
    hbm = pl.BlockSpec(memory_space=pltpu.HBM)

    def swap(value, axis, count, bit):
        return lax.ppermute(value, axis, [(i, i ^ bit) for i in range(count)])

    blocks = [latents[None]]
    bit = 1
    while bit < neuron_count:
        blocks.append(swap(jnp.concatenate(blocks, axis=0), "neuron", neuron_count, bit))
        bit *= 2
    keep, away, grad_load, grad_bias = pl.pallas_call(
        functools.partial(main_kernel, neuron_count, "neuron", chunk, 512),
        out_shape=[
            jax.ShapeDtypeStruct((neuron_count // 2, lats, width), F32),
            jax.ShapeDtypeStruct((neuron_count // 2, lats, width), F32),
            jax.ShapeDtypeStruct((lats, neurons), F32),
            jax.ShapeDtypeStruct((1, neurons), F32),
        ],
        in_specs=[smem, hbm, hbm, hbm, hbm] + [vmem] * len(blocks),
        out_specs=[vmem, vmem, hbm, hbm],
        scratch_shapes=[
            pltpu.VMEM((lats, total), BF16),
            pltpu.VMEM((1, lats), jnp.int32),
            pltpu.VMEM((1, neurons), F32),
            pltpu.VMEM((neurons, total), BF16),
            pltpu.VMEM((lats + EXTRA, total), BF16),
            pltpu.VMEM((lats + EXTRA, neurons), BF16),
            pltpu.VMEM((lats, total), F32),
            pltpu.VMEM((lats, neurons), F32),
            pltpu.VMEM((1, neurons), F32),
            pltpu.SemaphoreType.DMA((3,)),
            pltpu.SemaphoreType.DMA((neurons // chunk,)),
            pltpu.SemaphoreType.DMA((neurons // chunk,)),
        ],
        compiler_params=pltpu.CompilerParams(vmem_limit_bytes=58 * 1024 * 1024),
    )(recorded, delays, bias, loadings[0], counts[0], *blocks)

    value = keep + swap(away, "neuron", neuron_count, 1)
    bit = 2
    while bit < neuron_count:
        value = value[0::2] + swap(value[1::2], "neuron", neuron_count, bit)
        bit *= 2
    value = value[0]
    bit = 1
    while bit < region_count:
        value = value + swap(value, "region", region_count, bit)
        bit *= 2
    return (value, grad_load[None], grad_bias)


def solution(mesh):
    placed = (
        P("region", "neuron", None),
        P(None, "neuron"),
        P("region", None, "neuron"),
        P("region", "neuron"),
        P("region", None),
        P("region"),
    )
    return jax.shard_map(
        functools.partial(per_device, mesh.shape["region"], mesh.shape["neuron"]),
        mesh=mesh,
        in_specs=placed,
        out_specs=(P(None, "neuron"), P("region", None, "neuron"), P("region", "neuron")),
        check_vma=False,
    )
```

```python
import functools

import jax
import jax.numpy as jnp
from jax import lax
from jax.experimental import pallas as pl
from jax.experimental.pallas import tpu as pltpu
from jax.sharding import PartitionSpec as P

LANES = 128
EXTRA = 16
F32 = jnp.float32
BF16 = jnp.bfloat16


def shift_tiles(tiles, delay, forward):
    lane = lax.broadcasted_iota(jnp.int32, delay.shape, 1)
    nothing = jnp.zeros_like(tiles[0])
    for level in range(7):
        amount = 1 << level
        chosen = (delay & amount) != 0
        if forward:
            turned = [pltpu.roll(tile, amount, 1) for tile in tiles]
            before = [nothing] + turned[:-1]
            moved = [jnp.where(lane < amount, b, t) for b, t in zip(before, turned)]
        else:
            turned = [pltpu.roll(tile, LANES - amount, 1) for tile in tiles]
            after = turned[1:] + [nothing]
            moved = [jnp.where(lane < LANES - amount, t, a) for t, a in zip(turned, after)]
        tiles = [jnp.where(chosen, m, tile) for m, tile in zip(moved, tiles)]
    chosen = delay >= LANES
    other = [nothing] + tiles[:-1] if forward else tiles[1:] + [nothing]
    return [jnp.where(chosen, o, tile) for o, tile in zip(other, tiles)]


def main_kernel(parts, axis, chunk, step, *refs):
    recorded_ref, delay_ref, load_ext, counts_hbm = refs[:4]
    held = len(refs) - 17
    blocks = refs[4 : 4 + held]
    keep, away, grad_load_hbm, grad_bias_hbm = refs[4 + held : 8 + held]
    whole, counts_ref, shifted, grad_shift, grad_load_ref, grad_bias_ref = refs[8 + held : 14 + held]
    bias_sem, counts_sems, out_sems = refs[14 + held :]
    me = lax.axis_index(axis)
    lats, total = grad_shift.shape
    neurons = counts_ref.shape[0]
    width = total // parts
    pieces = neurons // chunk
    length = recorded_ref[0]

    def counts_copy(index):
        rows = pl.ds(pl.multiple_of(index * chunk, chunk), chunk)
        return pltpu.make_async_copy(counts_hbm.at[rows], counts_ref.at[rows], counts_sems.at[index])

    def load_copy(index):
        rows = pl.ds(pl.multiple_of(index * chunk, chunk), chunk)
        return pltpu.make_async_copy(grad_load_ref.at[:, rows], grad_load_hbm.at[:, rows], out_sems.at[index])

    for index in range(pieces):
        counts_copy(index).start()
    row = lax.broadcasted_iota(jnp.int32, (EXTRA, total), 0)
    shifted[lats:, :] = jnp.where(row < 3, 1.0, 0.0).astype(BF16)
    grad_shift[...] = jnp.zeros_like(grad_shift)

    k = 0
    for ref in blocks:
        for j in range(ref.shape[0]):
            start = pl.multiple_of((me ^ k) * width, width)
            whole[:, pl.ds(start, width)] = ref[j]
            k += 1
    delay = delay_ref[...]
    tiles = [whole[:, j * LANES : (j + 1) * LANES].astype(F32) for j in range(total // LANES)]
    for j, tile in enumerate(shift_tiles(tiles, delay, True)):
        shifted[0:lats, j * LANES : (j + 1) * LANES] = tile.astype(BF16)

    bins = lax.broadcasted_iota(jnp.int32, (1, total), 1)

    def visit(index, carry):
        rows = pl.ds(pl.multiple_of(index * chunk, chunk), chunk)
        counts_copy(index).wait()
        load_part = load_ext[:, rows]
        grad_load = jnp.zeros((lats, chunk), F32)
        sums = jnp.zeros((chunk, LANES), F32)
        for begin in range(0, total, step):
            span = slice(begin, begin + step)
            piece = shifted[:, span]
            eta = lax.dot_general(load_part, piece, (((0,), (0,)), ((), ())), preferred_element_type=F32)
            observed = counts_ref[rows, span].astype(F32)
            resid = jnp.where(bins[:, span] < length, jnp.exp(eta) - observed, 0.0)
            resid_low = resid.astype(BF16)
            for j in range(step // LANES):
                sums = sums + resid[:, j * LANES : (j + 1) * LANES]
            grad_load = grad_load + lax.dot_general(
                piece[0:lats], resid_low, (((1,), (1,)), ((), ())), preferred_element_type=F32
            )
            grad_shift[:, span] += jnp.dot(load_part[0:lats], resid_low, preferred_element_type=F32)
        grad_load_ref[:, rows] = grad_load
        load_copy(index).start()
        grad_bias_ref[:, rows] = jnp.sum(sums.T, axis=0, keepdims=True)
        return carry

    lax.fori_loop(0, pieces, visit, 0, unroll=total <= 1024)
    bias_copy = pltpu.make_async_copy(grad_bias_ref, grad_bias_hbm, bias_sem)
    bias_copy.start()

    tiles = [grad_shift[:, j * LANES : (j + 1) * LANES] for j in range(total // LANES)]
    for j, tile in enumerate(shift_tiles(tiles, delay, False)):
        grad_shift[:, j * LANES : (j + 1) * LANES] = tile
    for k in range(parts):
        start = pl.multiple_of((me ^ k) * width, width)
        target = away if k % 2 else keep
        target[k // 2] = grad_shift[:, pl.ds(start, width)]
    for index in range(pieces):
        load_copy(index).wait()
    bias_copy.wait()


def per_device(region_count, neuron_count, counts, latents, loadings, bias, delays, recorded):
    neurons, total = counts.shape[1:]
    lats, width = latents.shape
    chunk = 256
    vmem = pl.BlockSpec(memory_space=pltpu.VMEM)
    smem = pl.BlockSpec(memory_space=pltpu.SMEM)
    hbm = pl.BlockSpec(memory_space=pltpu.HBM)

    def swap(value, axis, count, bit):
        return lax.ppermute(value, axis, [(i, i ^ bit) for i in range(count)])

    high = lax.reduce_precision(bias, 8, 7)
    middle = lax.reduce_precision(bias - high, 8, 7)
    low = bias - high - middle
    below = jnp.concatenate([high, middle, low], axis=0).astype(BF16)
    load_ext = jnp.pad(jnp.concatenate([loadings[0], below], axis=0), ((0, EXTRA - 3), (0, 0)))
    delay = jnp.broadcast_to(delays.reshape(lats, 1), (lats, LANES))

    near = latents[None]
    far = near[:0]
    bit = 1
    while bit < neuron_count:
        near = jnp.concatenate([near, far], axis=0)
        far = swap(near, "neuron", neuron_count, bit)
        bit *= 2
    keep, away, grad_load, grad_bias = pl.pallas_call(
        functools.partial(main_kernel, neuron_count, "neuron", chunk, 512),
        out_shape=[
            jax.ShapeDtypeStruct((neuron_count // 2, lats, width), F32),
            jax.ShapeDtypeStruct((neuron_count // 2, lats, width), F32),
            jax.ShapeDtypeStruct((lats, neurons), F32),
            jax.ShapeDtypeStruct((1, neurons), F32),
        ],
        in_specs=[smem, vmem, vmem, hbm, vmem, vmem],
        out_specs=[vmem, vmem, hbm, hbm],
        scratch_shapes=[
            pltpu.VMEM((lats, total), BF16),
            pltpu.VMEM((neurons, total), BF16),
            pltpu.VMEM((lats + EXTRA, total), BF16),
            pltpu.VMEM((lats, total), F32),
            pltpu.VMEM((lats, neurons), F32),
            pltpu.VMEM((1, neurons), F32),
            pltpu.SemaphoreType.DMA,
            pltpu.SemaphoreType.DMA((neurons // chunk,)),
            pltpu.SemaphoreType.DMA((neurons // chunk,)),
        ],
        compiler_params=pltpu.CompilerParams(vmem_limit_bytes=52 * 1024 * 1024),
    )(recorded, delay, load_ext, counts[0], near, far)

    value = keep + swap(away, "neuron", neuron_count, 1)
    bit = 2
    while bit < neuron_count:
        value = value[0::2] + swap(value[1::2], "neuron", neuron_count, bit)
        bit *= 2
    value = value[0]
    bit = 1
    while bit < region_count:
        value = value + swap(value, "region", region_count, bit)
        bit *= 2
    return (value, grad_load[None], grad_bias)


def solution(mesh):
    placed = (
        P("region", "neuron", None),
        P(None, "neuron"),
        P("region", None, "neuron"),
        P("region", "neuron"),
        P("region", None),
        P("region"),
    )
    return jax.shard_map(
        functools.partial(per_device, mesh.shape["region"], mesh.shape["neuron"]),
        mesh=mesh,
        in_specs=placed,
        out_specs=(P(None, "neuron"), P("region", None, "neuron"), P("region", "neuron")),
        check_vma=False,
    )
```

```python
import functools

import jax
import jax.numpy as jnp
from jax import lax
from jax.experimental import pallas as pl
from jax.experimental.pallas import tpu as pltpu
from jax.sharding import PartitionSpec as P

LANES = 128
EXTRA = 16
F32 = jnp.float32
BF16 = jnp.bfloat16


def shift_tiles(tiles, delay, forward):
    lane = lax.broadcasted_iota(jnp.int32, delay.shape, 1)
    nothing = jnp.zeros_like(tiles[0])
    for level in range(7):
        amount = 1 << level
        chosen = (delay & amount) != 0
        if forward:
            turned = [pltpu.roll(tile, amount, 1) for tile in tiles]
            before = [nothing] + turned[:-1]
            moved = [jnp.where(lane < amount, b, t) for b, t in zip(before, turned)]
        else:
            turned = [pltpu.roll(tile, LANES - amount, 1) for tile in tiles]
            after = turned[1:] + [nothing]
            moved = [jnp.where(lane < LANES - amount, t, a) for t, a in zip(turned, after)]
        tiles = [jnp.where(chosen, m, tile) for m, tile in zip(moved, tiles)]
    chosen = delay >= LANES
    other = [nothing] + tiles[:-1] if forward else tiles[1:] + [nothing]
    return [jnp.where(chosen, o, tile) for o, tile in zip(other, tiles)]


def main_kernel(parts, axis, chunk, step, *refs):
    recorded_ref, delay_ref, load_ext, counts_hbm = refs[:4]
    held = len(refs) - 17
    blocks = refs[4 : 4 + held]
    keep, away, grad_load_hbm, grad_bias_hbm = refs[4 + held : 8 + held]
    whole, counts_ref, shifted, grad_shift, grad_load_ref, grad_bias_ref = refs[8 + held : 14 + held]
    bias_sem, counts_sems, out_sems = refs[14 + held :]
    me = lax.axis_index(axis)
    lats, total = grad_shift.shape
    neurons = counts_ref.shape[0]
    width = total // parts
    pieces = neurons // chunk
    length = recorded_ref[0]

    def counts_copy(index):
        rows = pl.ds(pl.multiple_of(index * chunk, chunk), chunk)
        return pltpu.make_async_copy(counts_hbm.at[rows], counts_ref.at[rows], counts_sems.at[index])

    def load_copy(index):
        rows = pl.ds(pl.multiple_of(index * chunk, chunk), chunk)
        return pltpu.make_async_copy(grad_load_ref.at[:, rows], grad_load_hbm.at[:, rows], out_sems.at[index])

    for index in range(pieces):
        counts_copy(index).start()
    row = lax.broadcasted_iota(jnp.int32, (EXTRA, total), 0)
    shifted[lats:, :] = jnp.where(row < 3, 1.0, 0.0).astype(BF16)
    grad_shift[...] = jnp.zeros_like(grad_shift)

    k = 0
    for ref in blocks:
        for j in range(ref.shape[0]):
            start = pl.multiple_of((me ^ k) * width, width)
            whole[:, pl.ds(start, width)] = ref[j]
            k += 1
    delay = delay_ref[...]
    tiles = [whole[:, j * LANES : (j + 1) * LANES].astype(F32) for j in range(total // LANES)]
    for j, tile in enumerate(shift_tiles(tiles, delay, True)):
        shifted[0:lats, j * LANES : (j + 1) * LANES] = tile.astype(BF16)

    bins = lax.broadcasted_iota(jnp.int32, (1, total), 1)

    def visit(index, carry):
        rows = pl.ds(pl.multiple_of(index * chunk, chunk), chunk)
        counts_copy(index).wait()
        load_part = load_ext[:, rows]
        grad_load = jnp.zeros((lats, chunk), F32)
        sums = jnp.zeros((chunk, LANES), F32)
        for begin in range(0, total, step):
            span = slice(begin, begin + step)
            piece = shifted[:, span]
            eta = lax.dot_general(load_part, piece, (((0,), (0,)), ((), ())), preferred_element_type=F32)
            observed = counts_ref[rows, span].astype(F32)
            resid = jnp.where(bins[:, span] < length, jnp.exp(eta) - observed, 0.0)
            resid_low = resid.astype(BF16)
            for j in range(step // LANES):
                sums = sums + resid[:, j * LANES : (j + 1) * LANES]
            grad_load = grad_load + lax.dot_general(
                piece[0:lats], resid_low, (((1,), (1,)), ((), ())), preferred_element_type=F32
            )
            grad_shift[:, span] += jnp.dot(load_part[0:lats], resid_low, preferred_element_type=F32)
        grad_load_ref[:, rows] = grad_load
        load_copy(index).start()
        grad_bias_ref[:, rows] = jnp.sum(sums.T, axis=0, keepdims=True)
        return carry

    lax.fori_loop(0, pieces, visit, 0, unroll=total <= 1024)
    bias_copy = pltpu.make_async_copy(grad_bias_ref, grad_bias_hbm, bias_sem)
    bias_copy.start()

    tiles = [grad_shift[:, j * LANES : (j + 1) * LANES] for j in range(total // LANES)]
    for j, tile in enumerate(shift_tiles(tiles, delay, False)):
        grad_shift[:, j * LANES : (j + 1) * LANES] = tile
    for k in range(parts):
        start = pl.multiple_of((me ^ k) * width, width)
        target = away if k % 2 else keep
        target[k // 2] = grad_shift[:, pl.ds(start, width)]
    for index in range(pieces):
        load_copy(index).wait()
    bias_copy.wait()


def per_device(region_count, neuron_count, counts, latents, loadings, bias, delays, recorded):
    neurons, total = counts.shape[1:]
    lats, width = latents.shape
    chunk = 256
    vmem = pl.BlockSpec(memory_space=pltpu.VMEM)
    smem = pl.BlockSpec(memory_space=pltpu.SMEM)
    hbm = pl.BlockSpec(memory_space=pltpu.HBM)

    def swap(value, axis, count, bit):
        return lax.ppermute(value, axis, [(i, i ^ bit) for i in range(count)])

    high = lax.reduce_precision(bias, 8, 7)
    middle = lax.reduce_precision(bias - high, 8, 7)
    low = bias - high - middle
    below = jnp.concatenate([high, middle, low], axis=0).astype(BF16)
    load_ext = jnp.pad(jnp.concatenate([loadings[0], below], axis=0), ((0, EXTRA - 3), (0, 0)))
    delay = jnp.broadcast_to(delays.reshape(lats, 1), (lats, LANES))

    near = latents[None]
    far = near[:0]
    bit = 1
    while bit < neuron_count:
        near = jnp.concatenate([near, far], axis=0)
        far = swap(near, "neuron", neuron_count, bit)
        bit *= 2
    keep, away, grad_load, grad_bias = pl.pallas_call(
        functools.partial(main_kernel, neuron_count, "neuron", chunk, 512),
        out_shape=[
            jax.ShapeDtypeStruct((neuron_count // 2, lats, width), F32),
            jax.ShapeDtypeStruct((neuron_count // 2, lats, width), F32),
            jax.ShapeDtypeStruct((lats, neurons), F32),
            jax.ShapeDtypeStruct((1, neurons), F32),
        ],
        in_specs=[smem, vmem, vmem, hbm, vmem, vmem],
        out_specs=[vmem, vmem, hbm, hbm],
        scratch_shapes=[
            pltpu.VMEM((lats, total), BF16),
            pltpu.VMEM((neurons, total), BF16),
            pltpu.VMEM((lats + EXTRA, total), BF16),
            pltpu.VMEM((lats, total), F32),
            pltpu.VMEM((lats, neurons), F32),
            pltpu.VMEM((1, neurons), F32),
            pltpu.SemaphoreType.DMA,
            pltpu.SemaphoreType.DMA((neurons // chunk,)),
            pltpu.SemaphoreType.DMA((neurons // chunk,)),
        ],
        compiler_params=pltpu.CompilerParams(vmem_limit_bytes=52 * 1024 * 1024),
    )(recorded, delay, load_ext, counts[0], near, far)

    value = keep + swap(away, "neuron", neuron_count, 1)
    bit = 2
    while bit < neuron_count:
        value = value[0::2] + swap(value[1::2], "neuron", neuron_count, bit)
        bit *= 2
    value = value[0]
    everyone = lax.all_gather(value.astype(BF16), "region", axis=0)
    value = jnp.sum(everyone.astype(F32), axis=0)
    return (value, grad_load[None], grad_bias)


def solution(mesh):
    placed = (
        P("region", "neuron", None),
        P(None, "neuron"),
        P("region", None, "neuron"),
        P("region", "neuron"),
        P("region", None),
        P("region"),
    )
    return jax.shard_map(
        functools.partial(per_device, mesh.shape["region"], mesh.shape["neuron"]),
        mesh=mesh,
        in_specs=placed,
        out_specs=(P(None, "neuron"), P("region", None, "neuron"), P("region", "neuron")),
        check_vma=False,
    )
```

```python
import functools

import jax
import jax.numpy as jnp
from jax import lax
from jax.experimental import pallas as pl
from jax.experimental.pallas import tpu as pltpu
from jax.sharding import PartitionSpec as P

LANES = 128
EXTRA = 16
F32 = jnp.float32
BF16 = jnp.bfloat16


def shift_tiles(tiles, delay, forward):
    lane = lax.broadcasted_iota(jnp.int32, delay.shape, 1)
    nothing = jnp.zeros_like(tiles[0])
    for level in range(7):
        amount = 1 << level
        chosen = (delay & amount) != 0
        if forward:
            turned = [pltpu.roll(tile, amount, 1) for tile in tiles]
            before = [nothing] + turned[:-1]
            moved = [jnp.where(lane < amount, b, t) for b, t in zip(before, turned)]
        else:
            turned = [pltpu.roll(tile, LANES - amount, 1) for tile in tiles]
            after = turned[1:] + [nothing]
            moved = [jnp.where(lane < LANES - amount, t, a) for t, a in zip(turned, after)]
        tiles = [jnp.where(chosen, m, tile) for m, tile in zip(moved, tiles)]
    chosen = delay >= LANES
    other = [nothing] + tiles[:-1] if forward else tiles[1:] + [nothing]
    return [jnp.where(chosen, o, tile) for o, tile in zip(other, tiles)]


def main_kernel(parts, axis, chunk, step, *refs):
    meta_ref, load_ext, counts_hbm, near, far = refs[:5]
    keep, away, grad_load_hbm, grad_bias_hbm = refs[5:9]
    whole, counts_ref, shifted, grad_shift, grad_load_ref, grad_bias_ref = refs[9:15]
    bias_sem, counts_sems, out_sems = refs[15:]
    me = lax.axis_index(axis)
    lats, total = grad_shift.shape
    neurons = counts_ref.shape[0]
    width = total // parts
    pieces = neurons // chunk
    def counts_copy(index):
        rows = pl.ds(pl.multiple_of(index * chunk, chunk), chunk)
        return pltpu.make_async_copy(counts_hbm.at[rows], counts_ref.at[rows], counts_sems.at[index])

    def load_copy(index):
        rows = pl.ds(pl.multiple_of(index * chunk, chunk), chunk)
        return pltpu.make_async_copy(grad_load_ref.at[:, rows], grad_load_hbm.at[:, rows], out_sems.at[index])

    for index in range(pieces):
        counts_copy(index).start()
    row = lax.broadcasted_iota(jnp.int32, (EXTRA, total), 0)
    shifted[lats:, :] = jnp.where(row < 3, 1.0, 0.0).astype(BF16)
    grad_shift[...] = jnp.zeros_like(grad_shift)

    k = 0
    for ref in (near, far):
        for j in range(ref.shape[0]):
            start = pl.multiple_of((me ^ k) * width, width)
            whole[:, pl.ds(start, width)] = ref[j]
            k += 1
    diagonal = lax.broadcasted_iota(jnp.int32, (lats, LANES), 0) == lax.broadcasted_iota(jnp.int32, (lats, LANES), 1)
    spread = jnp.broadcast_to(meta_ref[...].astype(F32), (lats, LANES))
    column = jnp.sum(jnp.where(diagonal, spread, 0.0), axis=1, keepdims=True)
    delay = jnp.broadcast_to(column, (lats, LANES)).astype(jnp.int32)
    length = meta_ref[:, lats : lats + 1]
    tiles = [whole[:, j * LANES : (j + 1) * LANES].astype(F32) for j in range(total // LANES)]
    for j, tile in enumerate(shift_tiles(tiles, delay, True)):
        shifted[0:lats, j * LANES : (j + 1) * LANES] = tile.astype(BF16)

    bins = lax.broadcasted_iota(jnp.int32, (1, total), 1)

    def visit(index, carry):
        rows = pl.ds(pl.multiple_of(index * chunk, chunk), chunk)
        counts_copy(index).wait()
        load_part = load_ext[:, rows]
        grad_load = jnp.zeros((lats, chunk), F32)
        sums = jnp.zeros((chunk, LANES), F32)
        for begin in range(0, total, step):
            span = slice(begin, begin + step)
            piece = shifted[:, span]
            eta = lax.dot_general(load_part, piece, (((0,), (0,)), ((), ())), preferred_element_type=F32)
            observed = counts_ref[rows, span].astype(F32)
            resid = jnp.where(bins[:, span] < length, jnp.exp(eta) - observed, 0.0)
            resid_low = resid.astype(BF16)
            for j in range(step // LANES):
                sums = sums + resid[:, j * LANES : (j + 1) * LANES]
            grad_load = grad_load + lax.dot_general(
                piece[0:lats], resid_low, (((1,), (1,)), ((), ())), preferred_element_type=F32
            )
            grad_shift[:, span] += jnp.dot(load_part[0:lats], resid_low, preferred_element_type=F32)
        grad_load_ref[:, rows] = grad_load
        load_copy(index).start()
        grad_bias_ref[:, rows] = jnp.sum(sums.T, axis=0, keepdims=True)
        return carry

    lax.fori_loop(0, pieces, visit, 0, unroll=total <= 1024)
    bias_copy = pltpu.make_async_copy(grad_bias_ref, grad_bias_hbm, bias_sem)
    bias_copy.start()

    tiles = [grad_shift[:, j * LANES : (j + 1) * LANES] for j in range(total // LANES)]
    for j, tile in enumerate(shift_tiles(tiles, delay, False)):
        grad_shift[:, j * LANES : (j + 1) * LANES] = tile
    for k in range(parts):
        start = pl.multiple_of((me ^ k) * width, width)
        target = away if k % 2 else keep
        target[k // 2] = grad_shift[:, pl.ds(start, width)]
    for index in range(pieces):
        load_copy(index).wait()
    bias_copy.wait()


def per_device(region_count, neuron_count, counts, latents, loadings, bias, delays, recorded):
    neurons, total = counts.shape[1:]
    lats, width = latents.shape
    chunk = 256
    vmem = pl.BlockSpec(memory_space=pltpu.VMEM)
    hbm = pl.BlockSpec(memory_space=pltpu.HBM)

    def swap(value, axis, count, bit):
        return lax.ppermute(value, axis, [(i, i ^ bit) for i in range(count)])

    near = latents[None]
    far = near[:0]
    bit = 1
    while bit < neuron_count:
        near = jnp.concatenate([near, far], axis=0)
        if bit > 1:
            near, loadings, delays = lax.optimization_barrier((near, loadings, delays))
        far = swap(near, "neuron", neuron_count, bit)
        bit *= 2

    high = lax.reduce_precision(bias, 8, 7)
    middle = lax.reduce_precision(bias - high, 8, 7)
    low = bias - high - middle
    below = jnp.concatenate([high, middle, low], axis=0).astype(BF16)
    load_ext = jnp.pad(jnp.concatenate([loadings[0], below], axis=0), ((0, EXTRA - 3), (0, 0)))
    meta = jnp.concatenate([delays.reshape(lats), recorded, jnp.zeros((LANES - lats - 1,), jnp.int32)])[None]

    keep, away, grad_load, grad_bias = pl.pallas_call(
        functools.partial(main_kernel, neuron_count, "neuron", chunk, 512),
        out_shape=[
            jax.ShapeDtypeStruct((neuron_count // 2, lats, width), F32),
            jax.ShapeDtypeStruct((neuron_count // 2, lats, width), F32),
            jax.ShapeDtypeStruct((lats, neurons), F32),
            jax.ShapeDtypeStruct((1, neurons), F32),
        ],
        in_specs=[vmem, vmem, hbm, vmem, vmem],
        out_specs=[vmem, vmem, hbm, hbm],
        scratch_shapes=[
            pltpu.VMEM((lats, total), BF16),
            pltpu.VMEM((neurons, total), BF16),
            pltpu.VMEM((lats + EXTRA, total), BF16),
            pltpu.VMEM((lats, total), F32),
            pltpu.VMEM((lats, neurons), F32),
            pltpu.VMEM((1, neurons), F32),
            pltpu.SemaphoreType.DMA,
            pltpu.SemaphoreType.DMA((neurons // chunk,)),
            pltpu.SemaphoreType.DMA((neurons // chunk,)),
        ],
        compiler_params=pltpu.CompilerParams(vmem_limit_bytes=52 * 1024 * 1024),
    )(meta, load_ext, counts[0], near, far)

    value = keep + swap(away, "neuron", neuron_count, 1)
    bit = 2
    while bit < neuron_count:
        value = value[0::2] + swap(value[1::2], "neuron", neuron_count, bit)
        bit *= 2
    value = value[0]
    bits = [1 << level for level in range(region_count.bit_length() - 1)]
    orders = (bits[:1] + bits[:0:-1], bits[1:2] + bits[:1] + bits[2:])
    for step in range(len(bits)):
        pairs = [
            (r * neuron_count + n, (r ^ orders[n % 2][step]) * neuron_count + n)
            for r in range(region_count)
            for n in range(neuron_count)
        ]
        value = value + lax.ppermute(value, ("region", "neuron"), pairs)
    return (value, grad_load[None], grad_bias)


def solution(mesh):
    placed = (
        P("region", "neuron", None),
        P(None, "neuron"),
        P("region", None, "neuron"),
        P("region", "neuron"),
        P("region", None),
        P("region"),
    )
    return jax.shard_map(
        functools.partial(per_device, mesh.shape["region"], mesh.shape["neuron"]),
        mesh=mesh,
        in_specs=placed,
        out_specs=(P(None, "neuron"), P("region", None, "neuron"), P("region", "neuron")),
        check_vma=False,
    )
```

```python
import functools

import jax
import jax.numpy as jnp
from jax import lax
from jax.experimental import pallas as pl
from jax.experimental.pallas import tpu as pltpu
from jax.sharding import PartitionSpec as P

LANES = 128
EXTRA = 16
F32 = jnp.float32
BF16 = jnp.bfloat16


def shift_tiles(tiles, delay, forward):
    lane = lax.broadcasted_iota(jnp.int32, delay.shape, 1)
    nothing = jnp.zeros_like(tiles[0])
    for level in range(7):
        amount = 1 << level
        chosen = (delay & amount) != 0
        if forward:
            turned = [pltpu.roll(tile, amount, 1) for tile in tiles]
            before = [nothing] + turned[:-1]
            moved = [jnp.where(lane < amount, b, t) for b, t in zip(before, turned)]
        else:
            turned = [pltpu.roll(tile, LANES - amount, 1) for tile in tiles]
            after = turned[1:] + [nothing]
            moved = [jnp.where(lane < LANES - amount, t, a) for t, a in zip(turned, after)]
        tiles = [jnp.where(chosen, m, tile) for m, tile in zip(moved, tiles)]
    chosen = delay >= LANES
    other = [nothing] + tiles[:-1] if forward else tiles[1:] + [nothing]
    return [jnp.where(chosen, o, tile) for o, tile in zip(other, tiles)]


def main_kernel(parts, axis, chunk, step, *refs):
    meta_ref, load_ext, counts_hbm, near, far = refs[:5]
    keep, away, grad_load_hbm, grad_bias_hbm = refs[5:9]
    whole, counts_ref, shifted, grad_shift, grad_load_ref, grad_bias_ref = refs[9:15]
    bias_sem, counts_sems, out_sems = refs[15:]
    me = lax.axis_index(axis)
    lats, total = grad_shift.shape
    neurons = counts_ref.shape[0]
    width = total // parts
    pieces = neurons // chunk
    def counts_copy(index):
        rows = pl.ds(index * chunk, chunk)
        return pltpu.make_async_copy(counts_hbm.at[rows], counts_ref.at[rows], counts_sems.at[index])

    def load_copy(index):
        rows = pl.ds(index * chunk, chunk)
        return pltpu.make_async_copy(grad_load_ref.at[:, rows], grad_load_hbm.at[:, rows], out_sems.at[index])

    counts_copy(0).start()
    row = lax.broadcasted_iota(jnp.int32, (EXTRA, total), 0)
    shifted[lats:, :] = jnp.where(row < 3, 1.0, 0.0).astype(BF16)
    grad_shift[...] = jnp.zeros_like(grad_shift)

    k = 0
    for ref in (near, far):
        for j in range(ref.shape[0]):
            start = pl.multiple_of((me ^ k) * width, width)
            whole[:, pl.ds(start, width)] = ref[j]
            k += 1
    diagonal = lax.broadcasted_iota(jnp.int32, (lats, LANES), 0) == lax.broadcasted_iota(jnp.int32, (lats, LANES), 1)
    spread = jnp.broadcast_to(meta_ref[...].astype(F32), (lats, LANES))
    column = jnp.sum(jnp.where(diagonal, spread, 0.0), axis=1, keepdims=True)
    delay = jnp.broadcast_to(column, (lats, LANES)).astype(jnp.int32)
    length = meta_ref[:, lats : lats + 1]
    tiles = [whole[:, j * LANES : (j + 1) * LANES].astype(F32) for j in range(total // LANES)]
    for j, tile in enumerate(shift_tiles(tiles, delay, True)):
        shifted[0:lats, j * LANES : (j + 1) * LANES] = tile.astype(BF16)

    bins = lax.broadcasted_iota(jnp.int32, (1, total), 1)
    for index in range(pieces):
        rows = slice(index * chunk, (index + 1) * chunk)
        if index == 0 and pieces > 1:
            counts_copy(1).start()
        counts_copy(index).wait()
        if index + 2 < pieces:
            counts_copy(index + 2).start()
        load_part = load_ext[:, rows]
        grad_load = jnp.zeros((lats, chunk), F32)
        sums = jnp.zeros((chunk, LANES), F32)
        for begin in range(0, total, step):
            span = slice(begin, begin + step)
            piece = shifted[:, span]
            eta = lax.dot_general(load_part, piece, (((0,), (0,)), ((), ())), preferred_element_type=F32)
            observed = counts_ref[rows, span].astype(F32)
            resid = jnp.where(bins[:, span] < length, jnp.exp(eta) - observed, 0.0)
            resid_low = resid.astype(BF16)
            for j in range(step // LANES):
                sums = sums + resid[:, j * LANES : (j + 1) * LANES]
            grad_load = grad_load + lax.dot_general(
                piece[0:lats], resid_low, (((1,), (1,)), ((), ())), preferred_element_type=F32
            )
            grad_shift[:, span] += jnp.dot(load_part[0:lats], resid_low, preferred_element_type=F32)
        grad_load_ref[:, rows] = grad_load
        load_copy(index).start()
        grad_bias_ref[:, rows] = jnp.sum(sums.T, axis=0, keepdims=True)

    bias_copy = pltpu.make_async_copy(grad_bias_ref, grad_bias_hbm, bias_sem)
    bias_copy.start()

    tiles = [grad_shift[:, j * LANES : (j + 1) * LANES] for j in range(total // LANES)]
    for j, tile in enumerate(shift_tiles(tiles, delay, False)):
        grad_shift[:, j * LANES : (j + 1) * LANES] = tile
    for k in range(parts):
        start = pl.multiple_of((me ^ k) * width, width)
        target = away if k % 2 else keep
        target[k // 2] = grad_shift[:, pl.ds(start, width)]
    for index in range(pieces):
        load_copy(index).wait()
    bias_copy.wait()


def per_device(region_count, neuron_count, counts, latents, loadings, bias, delays, recorded):
    neurons, total = counts.shape[1:]
    lats, width = latents.shape
    chunk = 256
    vmem = pl.BlockSpec(memory_space=pltpu.VMEM)
    hbm = pl.BlockSpec(memory_space=pltpu.HBM)

    def swap(value, axis, count, bit):
        return lax.ppermute(value, axis, [(i, i ^ bit) for i in range(count)])

    near = latents[None]
    far = near[:0]
    bit = 1
    while bit < neuron_count:
        near = jnp.concatenate([near, far], axis=0)
        if bit > 1:
            near, loadings, delays = lax.optimization_barrier((near, loadings, delays))
        far = swap(near, "neuron", neuron_count, bit)
        bit *= 2

    high = lax.reduce_precision(bias, 8, 7)
    middle = lax.reduce_precision(bias - high, 8, 7)
    low = bias - high - middle
    below = jnp.concatenate([high, middle, low], axis=0).astype(BF16)
    load_ext = jnp.pad(jnp.concatenate([loadings[0], below], axis=0), ((0, EXTRA - 3), (0, 0)))
    meta = jnp.concatenate([delays.reshape(lats), recorded, jnp.zeros((LANES - lats - 1,), jnp.int32)])[None]

    keep, away, grad_load, grad_bias = pl.pallas_call(
        functools.partial(main_kernel, neuron_count, "neuron", chunk, 512),
        out_shape=[
            jax.ShapeDtypeStruct((neuron_count // 2, lats, width), F32),
            jax.ShapeDtypeStruct((neuron_count // 2, lats, width), F32),
            jax.ShapeDtypeStruct((lats, neurons), F32),
            jax.ShapeDtypeStruct((1, neurons), F32),
        ],
        in_specs=[vmem, vmem, hbm, vmem, vmem],
        out_specs=[vmem, vmem, hbm, hbm],
        scratch_shapes=[
            pltpu.VMEM((lats, total), BF16),
            pltpu.VMEM((neurons, total), BF16),
            pltpu.VMEM((lats + EXTRA, total), BF16),
            pltpu.VMEM((lats, total), F32),
            pltpu.VMEM((lats, neurons), F32),
            pltpu.VMEM((1, neurons), F32),
            pltpu.SemaphoreType.DMA,
            pltpu.SemaphoreType.DMA((neurons // chunk,)),
            pltpu.SemaphoreType.DMA((neurons // chunk,)),
        ],
        compiler_params=pltpu.CompilerParams(vmem_limit_bytes=52 * 1024 * 1024),
    )(meta, load_ext, counts[0], near, far)

    value = keep + swap(away, "neuron", neuron_count, 1)
    bit = 2
    while bit < neuron_count:
        value = value[0::2] + swap(value[1::2], "neuron", neuron_count, bit)
        bit *= 2
    value = value[0]
    bit = 1
    while bit < region_count:
        value = value + swap(value, "region", region_count, bit)
        bit *= 2
    return (value, grad_load[None], grad_bias)


def solution(mesh):
    placed = (
        P("region", "neuron", None),
        P(None, "neuron"),
        P("region", None, "neuron"),
        P("region", "neuron"),
        P("region", None),
        P("region"),
    )
    return jax.shard_map(
        functools.partial(per_device, mesh.shape["region"], mesh.shape["neuron"]),
        mesh=mesh,
        in_specs=placed,
        out_specs=(P(None, "neuron"), P("region", None, "neuron"), P("region", "neuron")),
        check_vma=False,
    )
```

```python
import functools

import jax
import jax.numpy as jnp
from jax import lax
from jax.experimental import pallas as pl
from jax.experimental.pallas import tpu as pltpu
from jax.sharding import PartitionSpec as P

LANES = 128
EXTRA = 16
F32 = jnp.float32
BF16 = jnp.bfloat16


def shift_tiles(tiles, delay, forward):
    lane = lax.broadcasted_iota(jnp.int32, delay.shape, 1)
    nothing = jnp.zeros_like(tiles[0])
    for level in range(7):
        amount = 1 << level
        chosen = (delay & amount) != 0
        if forward:
            turned = [pltpu.roll(tile, amount, 1) for tile in tiles]
            before = [nothing] + turned[:-1]
            moved = [jnp.where(lane < amount, b, t) for b, t in zip(before, turned)]
        else:
            turned = [pltpu.roll(tile, LANES - amount, 1) for tile in tiles]
            after = turned[1:] + [nothing]
            moved = [jnp.where(lane < LANES - amount, t, a) for t, a in zip(turned, after)]
        tiles = [jnp.where(chosen, m, tile) for m, tile in zip(moved, tiles)]
    chosen = delay >= LANES
    other = [nothing] + tiles[:-1] if forward else tiles[1:] + [nothing]
    return [jnp.where(chosen, o, tile) for o, tile in zip(other, tiles)]


def expected(load_part, piece):
    eta = lax.dot_general(load_part, piece, (((0,), (0,)), ((), ())), preferred_element_type=F32)
    return jnp.exp(eta)


def shift_kernel(parts, axis, chunk, step, early, *refs):
    meta_ref, load_ext, counts_hbm, near, far, keep, away, shifted = refs[:8]
    whole, counts_ref, held, grad_shift, counts_sem = refs[8:]
    me = lax.axis_index(axis)
    lats, total = grad_shift.shape
    neurons = counts_ref.shape[0]
    width = total // parts
    counts_copy = pltpu.make_async_copy(counts_hbm, counts_ref, counts_sem)
    counts_copy.start()

    k = 0
    for ref in (near, far):
        for j in range(ref.shape[0]):
            start = pl.multiple_of((me ^ k) * width, width)
            whole[:, pl.ds(start, width)] = ref[j]
            k += 1
    diagonal = lax.broadcasted_iota(jnp.int32, (lats, LANES), 0) == lax.broadcasted_iota(jnp.int32, (lats, LANES), 1)
    spread = jnp.broadcast_to(meta_ref[...].astype(F32), (lats, LANES))
    column = jnp.sum(jnp.where(diagonal, spread, 0.0), axis=1, keepdims=True)
    delay = jnp.broadcast_to(column, (lats, LANES)).astype(jnp.int32)
    length = meta_ref[:, lats : lats + 1]
    tiles = [whole[:, j * LANES : (j + 1) * LANES].astype(F32) for j in range(total // LANES)]
    for j, tile in enumerate(shift_tiles(tiles, delay, True)):
        shifted[0:lats, j * LANES : (j + 1) * LANES] = tile.astype(BF16)
    row = lax.broadcasted_iota(jnp.int32, (EXTRA, total), 0)
    shifted[lats:, :] = jnp.where(row < 3, 1.0, 0.0).astype(BF16)

    bins = lax.broadcasted_iota(jnp.int32, (1, total), 1)
    blocks = [
        (slice(first, first + chunk), slice(begin, begin + step))
        for first in range(0, neurons, chunk)
        for begin in range(0, total, step)
    ]
    for rows, span in blocks:
        if rows.start < early:
            held[rows, span] = expected(load_ext[:, rows], shifted[:, span])
    counts_copy.wait()
    for rows, span in blocks:
        rate = held[rows, span] if rows.start < early else expected(load_ext[:, rows], shifted[:, span])
        resid = jnp.where(bins[:, span] < length, rate - counts_ref[rows, span].astype(F32), 0.0)
        part = jnp.dot(load_ext[0:lats, rows], resid.astype(BF16), preferred_element_type=F32)
        grad_shift[:, span] = part if rows.start == 0 else grad_shift[:, span] + part

    tiles = [grad_shift[:, j * LANES : (j + 1) * LANES] for j in range(total // LANES)]
    for j, tile in enumerate(shift_tiles(tiles, delay, False)):
        grad_shift[:, j * LANES : (j + 1) * LANES] = tile
    for k in range(parts):
        start = pl.multiple_of((me ^ k) * width, width)
        target = away if k % 2 else keep
        target[k // 2] = grad_shift[:, pl.ds(start, width)]


def load_kernel(lats, first, chunk, step, *refs):
    meta_ref, load_ext, shifted, counts_hbm = refs[:4]
    load_hbm, bias_hbm, counts_ref, held, load_ref, bias_ref, sems = refs[-7:]
    count, total = counts_ref.shape
    place = pl.ds(first, count)
    counts_copy = pltpu.make_async_copy(counts_hbm.at[place], counts_ref, sems.at[0])
    counts_copy.start()
    length = meta_ref[:, lats : lats + 1]
    bins = lax.broadcasted_iota(jnp.int32, (1, total), 1)
    blocks = [(begin, at) for begin in range(0, count, chunk) for at in range(0, total, step)]
    for begin, at in blocks:
        rows, span = slice(begin, begin + chunk), slice(at, at + step)
        held[rows, span] = expected(load_ext[:, first + begin : first + begin + chunk], shifted[:, span])
    counts_copy.wait()
    for begin, at in blocks:
        rows, span = slice(begin, begin + chunk), slice(at, at + step)
        resid = jnp.where(bins[:, span] < length, held[rows, span] - counts_ref[rows, span].astype(F32), 0.0)
        sums = resid[:, 0:LANES]
        for j in range(1, step // LANES):
            sums = sums + resid[:, j * LANES : (j + 1) * LANES]
        line = jnp.sum(sums.T, axis=0, keepdims=True)
        part = lax.dot_general(
            shifted[0:lats, span], resid.astype(BF16), (((1,), (1,)), ((), ())), preferred_element_type=F32
        )
        load_ref[:, rows] = part if at == 0 else load_ref[:, rows] + part
        bias_ref[:, rows] = line if at == 0 else bias_ref[:, rows] + line
    outward = [
        pltpu.make_async_copy(load_ref, load_hbm.at[:, place], sems.at[1]),
        pltpu.make_async_copy(bias_ref, bias_hbm.at[:, place], sems.at[2]),
    ]
    for copy in outward:
        copy.start()
    for copy in outward:
        copy.wait()


def per_device(region_count, neuron_count, counts, latents, loadings, bias, delays, recorded):
    neurons, total = counts.shape[1:]
    lats, width = latents.shape
    chunk, step = 256, 512
    vmem = pl.BlockSpec(memory_space=pltpu.VMEM)
    hbm = pl.BlockSpec(memory_space=pltpu.HBM)
    params = pltpu.CompilerParams(vmem_limit_bytes=52 * 1024 * 1024)

    def swap(value, axis, count, bit):
        return lax.ppermute(value, axis, [(i, i ^ bit) for i in range(count)])

    near = latents[None]
    far = near[:0]
    bit = 1
    while bit < neuron_count:
        near = jnp.concatenate([near, far], axis=0)
        if bit > 1:
            near, loadings, delays = lax.optimization_barrier((near, loadings, delays))
        far = swap(near, "neuron", neuron_count, bit)
        bit *= 2

    high = lax.reduce_precision(bias, 8, 7)
    middle = lax.reduce_precision(bias - high, 8, 7)
    low = bias - high - middle
    below = jnp.concatenate([high, middle, low], axis=0).astype(BF16)
    load_ext = jnp.pad(jnp.concatenate([loadings[0], below], axis=0), ((0, EXTRA - 3), (0, 0)))
    meta = jnp.concatenate([delays.reshape(lats), recorded, jnp.zeros((LANES - lats - 1,), jnp.int32)])[None]

    early = 3 * chunk
    keep, away, shifted = pl.pallas_call(
        functools.partial(shift_kernel, neuron_count, "neuron", chunk, step, early),
        out_shape=[
            jax.ShapeDtypeStruct((neuron_count // 2, lats, width), F32),
            jax.ShapeDtypeStruct((neuron_count // 2, lats, width), F32),
            jax.ShapeDtypeStruct((lats + EXTRA, total), BF16),
        ],
        in_specs=[vmem, vmem, hbm, vmem, vmem],
        out_specs=[vmem, vmem, vmem],
        scratch_shapes=[
            pltpu.VMEM((lats, total), BF16),
            pltpu.VMEM((neurons, total), BF16),
            pltpu.VMEM((early, total), F32),
            pltpu.VMEM((lats, total), F32),
            pltpu.SemaphoreType.DMA,
        ],
        compiler_params=params,
    )(meta, load_ext, counts[0], near, far)

    shares = [(0, 2 * chunk), (2 * chunk, 2 * chunk), (4 * chunk, neurons - 4 * chunk)]
    made = []

    def make(before):
        first, count = shares.pop(0)
        before, start_load = lax.optimization_barrier((before, load_ext))
        out = pl.pallas_call(
            functools.partial(load_kernel, lats, first, chunk, step),
            out_shape=[jax.ShapeDtypeStruct((lats, neurons), F32), jax.ShapeDtypeStruct((1, neurons), F32)],
            in_specs=[vmem, vmem, vmem, hbm] + [hbm] * len(made),
            out_specs=[hbm, hbm],
            scratch_shapes=[
                pltpu.VMEM((count, total), BF16),
                pltpu.VMEM((count, total), F32),
                pltpu.VMEM((lats, count), F32),
                pltpu.VMEM((1, count), F32),
                pltpu.SemaphoreType.DMA((3,)),
            ],
            input_output_aliases={4 + i: i for i in range(len(made))},
            compiler_params=params,
            cost_estimate=pl.CostEstimate(
                flops=4 * lats * count * total, bytes_accessed=2 * count * total, transcendentals=count * total
            ),
        )(meta, start_load, shifted, counts[0], *made)
        return before, out

    value = keep + swap(away, "neuron", neuron_count, 1)
    bit = 2
    while bit < neuron_count:
        if shares:
            value, made = make(value)
        arrived = swap(value[1::2], "neuron", neuron_count, bit)
        arrived, made = lax.optimization_barrier((arrived, made))
        value = value[0::2] + arrived
        bit *= 2
    value = value[0]
    bit = 1
    while bit < region_count:
        if shares:
            value, made = make(value)
        arrived = swap(value, "region", region_count, bit)
        arrived, made = lax.optimization_barrier((arrived, made))
        value = value + arrived
        bit *= 2
    grad_load, grad_bias = made
    return (value, grad_load[None], grad_bias)


def solution(mesh):
    placed = (
        P("region", "neuron", None),
        P(None, "neuron"),
        P("region", None, "neuron"),
        P("region", "neuron"),
        P("region", None),
        P("region"),
    )
    return jax.shard_map(
        functools.partial(per_device, mesh.shape["region"], mesh.shape["neuron"]),
        mesh=mesh,
        in_specs=placed,
        out_specs=(P(None, "neuron"), P("region", None, "neuron"), P("region", "neuron")),
        check_vma=False,
    )
```

```python
import functools

import jax
import jax.numpy as jnp
from jax import lax
from jax.experimental import pallas as pl
from jax.experimental.pallas import tpu as pltpu
from jax.sharding import PartitionSpec as P

LANES = 128
EXTRA = 16
F32 = jnp.float32
BF16 = jnp.bfloat16


def shift_tiles(tiles, delay, forward):
    lane = lax.broadcasted_iota(jnp.int32, delay.shape, 1)
    nothing = jnp.zeros_like(tiles[0])
    for level in range(7):
        amount = 1 << level
        chosen = (delay & amount) != 0
        if forward:
            turned = [pltpu.roll(tile, amount, 1) for tile in tiles]
            before = [nothing] + turned[:-1]
            moved = [jnp.where(lane < amount, b, t) for b, t in zip(before, turned)]
        else:
            turned = [pltpu.roll(tile, LANES - amount, 1) for tile in tiles]
            after = turned[1:] + [nothing]
            moved = [jnp.where(lane < LANES - amount, t, a) for t, a in zip(turned, after)]
        tiles = [jnp.where(chosen, m, tile) for m, tile in zip(moved, tiles)]
    chosen = delay >= LANES
    other = [nothing] + tiles[:-1] if forward else tiles[1:] + [nothing]
    return [jnp.where(chosen, o, tile) for o, tile in zip(other, tiles)]


def expected(load_part, piece):
    eta = lax.dot_general(load_part, piece, (((0,), (0,)), ((), ())), preferred_element_type=F32)
    return jnp.exp(eta)


def shift_kernel(parts, axis, chunk, step, early, *refs):
    meta_ref, pack_ref, counts_hbm = refs[:3]
    arrived = refs[3 : 2 + parts]
    outs = refs[2 + parts : 2 + 2 * parts]
    load_ext, shifted, whole, counts_ref, held, grad_shift, counts_sem = refs[2 + 2 * parts :]
    me = lax.axis_index(axis)
    lats, total = grad_shift.shape
    neurons = counts_ref.shape[0]
    width = total // parts
    counts_copy = pltpu.make_async_copy(counts_hbm, counts_ref, counts_sem)
    counts_copy.start()

    for k in range(parts):
        start = pl.multiple_of((me ^ k) * width, width)
        whole[:, pl.ds(start, width)] = arrived[k - 1][...] if k else pack_ref[:, neurons:]
    diagonal = lax.broadcasted_iota(jnp.int32, (lats, LANES), 0) == lax.broadcasted_iota(jnp.int32, (lats, LANES), 1)
    spread = jnp.broadcast_to(meta_ref[1:2, 0:LANES], (lats, LANES))
    column = jnp.sum(jnp.where(diagonal, spread, 0.0), axis=1, keepdims=True)
    delay = jnp.broadcast_to(column, (lats, LANES)).astype(jnp.int32)
    length = meta_ref[2:3, 0:1].astype(jnp.int32)
    tiles = [whole[:, j * LANES : (j + 1) * LANES].astype(F32) for j in range(total // LANES)]
    for j, tile in enumerate(shift_tiles(tiles, delay, True)):
        shifted[0:lats, j * LANES : (j + 1) * LANES] = tile.astype(BF16)
    row = lax.broadcasted_iota(jnp.int32, (EXTRA, total), 0)
    shifted[lats:, :] = jnp.where(row < 3, 1.0, 0.0).astype(BF16)

    load_ext[0:lats, :] = pack_ref[:, 0:neurons]
    bias = meta_ref[0:1, :]
    high = bias.astype(BF16).astype(F32)
    middle = (bias - high).astype(BF16).astype(F32)
    low = bias - high - middle
    row = lax.broadcasted_iota(jnp.int32, (EXTRA, neurons), 0)
    below = jnp.where(row == 0, high, jnp.where(row == 1, middle, jnp.where(row == 2, low, 0.0)))
    load_ext[lats:, :] = below.astype(BF16)

    bins = lax.broadcasted_iota(jnp.int32, (1, total), 1)
    blocks = [
        (slice(first, first + chunk), slice(begin, begin + step))
        for first in range(0, neurons, chunk)
        for begin in range(0, total, step)
    ]
    for rows, span in blocks:
        if rows.start < early:
            held[rows, span] = expected(load_ext[:, rows], shifted[:, span])
    counts_copy.wait()
    for rows, span in blocks:
        rate = held[rows, span] if rows.start < early else expected(load_ext[:, rows], shifted[:, span])
        resid = jnp.where(bins[:, span] < length, rate - counts_ref[rows, span].astype(F32), 0.0)
        part = jnp.dot(load_ext[0:lats, rows], resid.astype(BF16), preferred_element_type=F32)
        grad_shift[:, span] = part if rows.start == 0 else grad_shift[:, span] + part

    tiles = [grad_shift[:, j * LANES : (j + 1) * LANES] for j in range(total // LANES)]
    for j, tile in enumerate(shift_tiles(tiles, delay, False)):
        grad_shift[:, j * LANES : (j + 1) * LANES] = tile
    for k in range(parts):
        start = pl.multiple_of((me ^ k) * width, width)
        outs[k][...] = grad_shift[:, pl.ds(start, width)]


def load_kernel(lats, first, chunk, step, *refs):
    meta_ref, load_ext, shifted, counts_hbm = refs[:4]
    load_hbm, bias_hbm, counts_ref, held, load_ref, bias_ref, sems = refs[-7:]
    count, total = counts_ref.shape
    place = pl.ds(first, count)
    counts_copy = pltpu.make_async_copy(counts_hbm.at[place], counts_ref, sems.at[0])
    counts_copy.start()
    length = meta_ref[2:3, 0:1].astype(jnp.int32)
    bins = lax.broadcasted_iota(jnp.int32, (1, total), 1)
    blocks = [(begin, at) for begin in range(0, count, chunk) for at in range(0, total, step)]
    for begin, at in blocks:
        rows, span = slice(begin, begin + chunk), slice(at, at + step)
        held[rows, span] = expected(load_ext[:, first + begin : first + begin + chunk], shifted[:, span])
    counts_copy.wait()
    for begin, at in blocks:
        rows, span = slice(begin, begin + chunk), slice(at, at + step)
        resid = jnp.where(bins[:, span] < length, held[rows, span] - counts_ref[rows, span].astype(F32), 0.0)
        sums = resid[:, 0:LANES]
        for j in range(1, step // LANES):
            sums = sums + resid[:, j * LANES : (j + 1) * LANES]
        line = jnp.sum(sums.T, axis=0, keepdims=True)
        part = lax.dot_general(
            shifted[0:lats, span], resid.astype(BF16), (((1,), (1,)), ((), ())), preferred_element_type=F32
        )
        load_ref[:, rows] = part if at == 0 else load_ref[:, rows] + part
        bias_ref[:, rows] = line if at == 0 else bias_ref[:, rows] + line
    outward = [
        pltpu.make_async_copy(load_ref, load_hbm.at[:, place], sems.at[1]),
        pltpu.make_async_copy(bias_ref, bias_hbm.at[:, place], sems.at[2]),
    ]
    for copy in outward:
        copy.start()
    for copy in outward:
        copy.wait()


def per_device(region_count, neuron_count, counts, latents, loadings, bias, delays, recorded):
    neurons, total = counts.shape[1:]
    lats, width = latents.shape
    chunk, step = 256, 512
    vmem = pl.BlockSpec(memory_space=pltpu.VMEM)
    hbm = pl.BlockSpec(memory_space=pltpu.HBM)
    params = pltpu.CompilerParams(vmem_limit_bytes=52 * 1024 * 1024)

    def swap(value, axis, count, mask):
        return lax.ppermute(value, axis, [(i, i ^ mask) for i in range(count)])

    arrived = [swap(latents, "neuron", neuron_count, k) for k in range(1, neuron_count)]
    pack = jnp.concatenate([loadings[0], latents], axis=1)
    row = lax.broadcasted_iota(jnp.int32, (8, neurons), 0)
    lines = jnp.pad(delays, ((1, 6), (0, neurons - lats)))
    lines = jnp.where(row == 2, jnp.broadcast_to(recorded[:, None], lines.shape), lines)
    meta = jnp.pad(bias, ((0, 7), (0, 0))) + lines.astype(F32)

    early = 3 * chunk
    *outs, load_ext, shifted = pl.pallas_call(
        functools.partial(shift_kernel, neuron_count, "neuron", chunk, step, early),
        out_shape=[jax.ShapeDtypeStruct((lats, width), F32)] * neuron_count
        + [jax.ShapeDtypeStruct((lats + EXTRA, neurons), BF16), jax.ShapeDtypeStruct((lats + EXTRA, total), BF16)],
        in_specs=[vmem, vmem, hbm] + [vmem] * (neuron_count - 1),
        out_specs=[vmem] * (neuron_count + 2),
        scratch_shapes=[
            pltpu.VMEM((lats, total), BF16),
            pltpu.VMEM((neurons, total), BF16),
            pltpu.VMEM((early, total), F32),
            pltpu.VMEM((lats, total), F32),
            pltpu.SemaphoreType.DMA,
        ],
        compiler_params=params,
    )(meta, pack, counts[0], *arrived)

    shares = [(0, 2 * chunk), (2 * chunk, 2 * chunk), (4 * chunk, neurons - 4 * chunk)]
    made = []

    def make(before):
        first, count = shares.pop(0)
        before, start_load = lax.optimization_barrier((before, load_ext))
        out = pl.pallas_call(
            functools.partial(load_kernel, lats, first, chunk, step),
            out_shape=[jax.ShapeDtypeStruct((lats, neurons), F32), jax.ShapeDtypeStruct((1, neurons), F32)],
            in_specs=[vmem, vmem, vmem, hbm] + [hbm] * len(made),
            out_specs=[hbm, hbm],
            scratch_shapes=[
                pltpu.VMEM((count, total), BF16),
                pltpu.VMEM((count, total), F32),
                pltpu.VMEM((lats, count), F32),
                pltpu.VMEM((1, count), F32),
                pltpu.SemaphoreType.DMA((3,)),
            ],
            input_output_aliases={4 + i: i for i in range(len(made))},
            compiler_params=params,
            cost_estimate=pl.CostEstimate(
                flops=4 * lats * count * total, bytes_accessed=2 * count * total, transcendentals=count * total
            ),
        )(meta, start_load, shifted, counts[0], *made)
        return before, out

    outs, made = make(outs)
    arrived = [swap(outs[k], "neuron", neuron_count, k) for k in range(1, neuron_count)]
    arrived, made = lax.optimization_barrier((arrived, made))
    value = functools.reduce(jnp.add, [outs[0]] + arrived)
    mask = 1
    while mask < region_count:
        masks = [mask, 2 * mask, 3 * mask] if 2 * mask < region_count else [mask]
        if shares:
            value, made = make(value)
        arrived = [swap(value, "region", region_count, k) for k in masks]
        arrived, made = lax.optimization_barrier((arrived, made))
        value = value + arrived[0]
        if len(masks) == 3:
            value = value + (arrived[1] + arrived[2])
        mask *= 1 + len(masks)
    grad_load, grad_bias = made
    return (value, grad_load[None], grad_bias)


def solution(mesh):
    placed = (
        P("region", "neuron", None),
        P(None, "neuron"),
        P("region", None, "neuron"),
        P("region", "neuron"),
        P("region", None),
        P("region"),
    )
    return jax.shard_map(
        functools.partial(per_device, mesh.shape["region"], mesh.shape["neuron"]),
        mesh=mesh,
        in_specs=placed,
        out_specs=(P(None, "neuron"), P("region", None, "neuron"), P("region", "neuron")),
        check_vma=False,
    )
```

```python
import functools

import jax
import jax.numpy as jnp
from jax import lax
from jax.experimental import pallas as pl
from jax.experimental.pallas import tpu as pltpu
from jax.sharding import PartitionSpec as P

LANES = 128
EXTRA = 16
F32 = jnp.float32
BF16 = jnp.bfloat16


def shift_tiles(tiles, delay, forward):
    lane = lax.broadcasted_iota(jnp.int32, delay.shape, 1)
    nothing = jnp.zeros_like(tiles[0])
    for level in range(7):
        amount = 1 << level
        chosen = (delay & amount) != 0
        if forward:
            turned = [pltpu.roll(tile, amount, 1) for tile in tiles]
            before = [nothing] + turned[:-1]
            moved = [jnp.where(lane < amount, b, t) for b, t in zip(before, turned)]
        else:
            turned = [pltpu.roll(tile, LANES - amount, 1) for tile in tiles]
            after = turned[1:] + [nothing]
            moved = [jnp.where(lane < LANES - amount, t, a) for t, a in zip(turned, after)]
        tiles = [jnp.where(chosen, m, tile) for m, tile in zip(moved, tiles)]
    chosen = delay >= LANES
    other = [nothing] + tiles[:-1] if forward else tiles[1:] + [nothing]
    return [jnp.where(chosen, o, tile) for o, tile in zip(other, tiles)]


def expected(load_part, piece):
    eta = lax.dot_general(load_part, piece, (((0,), (0,)), ((), ())), preferred_element_type=F32)
    return jnp.exp(eta)


def shift_kernel(parts, axis, chunk, step, early, *refs):
    meta_ref, pack_ref, counts_hbm = refs[:3]
    arrived = refs[3 : 2 + parts]
    outs = refs[2 + parts : 2 + 2 * parts]
    load_ext, shifted, whole, counts_ref, held, grad_shift, counts_sem = refs[2 + 2 * parts :]
    me = lax.axis_index(axis)
    lats, total = grad_shift.shape
    neurons = counts_ref.shape[0]
    width = total // parts
    counts_copy = pltpu.make_async_copy(counts_hbm, counts_ref, counts_sem)
    counts_copy.start()

    for k in range(parts):
        start = pl.multiple_of((me ^ k) * width, width)
        whole[:, pl.ds(start, width)] = arrived[k - 1][...] if k else pack_ref[:, neurons:]
    diagonal = lax.broadcasted_iota(jnp.int32, (lats, LANES), 0) == lax.broadcasted_iota(jnp.int32, (lats, LANES), 1)
    spread = jnp.broadcast_to(meta_ref[1:2, 0:LANES], (lats, LANES))
    column = jnp.sum(jnp.where(diagonal, spread, 0.0), axis=1, keepdims=True)
    delay = jnp.broadcast_to(column, (lats, LANES)).astype(jnp.int32)
    length = meta_ref[2:3, 0:1].astype(jnp.int32)
    tiles = [whole[:, j * LANES : (j + 1) * LANES].astype(F32) for j in range(total // LANES)]
    for j, tile in enumerate(shift_tiles(tiles, delay, True)):
        shifted[0:lats, j * LANES : (j + 1) * LANES] = tile.astype(BF16)
    row = lax.broadcasted_iota(jnp.int32, (EXTRA, total), 0)
    shifted[lats:, :] = jnp.where(row < 3, 1.0, 0.0).astype(BF16)

    load_ext[0:lats, :] = pack_ref[:, 0:neurons]
    bias = meta_ref[0:1, :]
    high = bias.astype(BF16).astype(F32)
    middle = (bias - high).astype(BF16).astype(F32)
    low = bias - high - middle
    row = lax.broadcasted_iota(jnp.int32, (EXTRA, neurons), 0)
    below = jnp.where(row == 0, high, jnp.where(row == 1, middle, jnp.where(row == 2, low, 0.0)))
    load_ext[lats:, :] = below.astype(BF16)

    bins = lax.broadcasted_iota(jnp.int32, (1, total), 1)
    blocks = [
        (slice(first, first + chunk), slice(begin, begin + step))
        for first in range(0, neurons, chunk)
        for begin in range(0, total, step)
    ]
    for rows, span in blocks:
        if rows.start < early:
            held[rows, span] = expected(load_ext[:, rows], shifted[:, span])
    counts_copy.wait()
    for rows, span in blocks:
        rate = held[rows, span] if rows.start < early else expected(load_ext[:, rows], shifted[:, span])
        resid = jnp.where(bins[:, span] < length, rate - counts_ref[rows, span].astype(F32), 0.0)
        part = jnp.dot(load_ext[0:lats, rows], resid.astype(BF16), preferred_element_type=F32)
        grad_shift[:, span] = part if rows.start == 0 else grad_shift[:, span] + part

    tiles = [grad_shift[:, j * LANES : (j + 1) * LANES] for j in range(total // LANES)]
    for j, tile in enumerate(shift_tiles(tiles, delay, False)):
        grad_shift[:, j * LANES : (j + 1) * LANES] = tile
    for k in range(parts):
        start = pl.multiple_of((me ^ k) * width, width)
        outs[k][...] = grad_shift[:, pl.ds(start, width)].astype(outs[k].dtype)


def load_kernel(lats, first, chunk, step, *refs):
    meta_ref, load_ext, shifted, counts_hbm = refs[:4]
    load_hbm, bias_hbm, counts_ref, held, load_ref, bias_ref, sems = refs[-7:]
    count, total = counts_ref.shape
    place = pl.ds(first, count)
    counts_copy = pltpu.make_async_copy(counts_hbm.at[place], counts_ref, sems.at[0])
    counts_copy.start()
    length = meta_ref[2:3, 0:1].astype(jnp.int32)
    bins = lax.broadcasted_iota(jnp.int32, (1, total), 1)
    blocks = [(begin, at) for begin in range(0, count, chunk) for at in range(0, total, step)]
    for begin, at in blocks:
        rows, span = slice(begin, begin + chunk), slice(at, at + step)
        held[rows, span] = expected(load_ext[:, first + begin : first + begin + chunk], shifted[:, span])
    counts_copy.wait()
    for begin, at in blocks:
        rows, span = slice(begin, begin + chunk), slice(at, at + step)
        resid = jnp.where(bins[:, span] < length, held[rows, span] - counts_ref[rows, span].astype(F32), 0.0)
        sums = resid[:, 0:LANES]
        for j in range(1, step // LANES):
            sums = sums + resid[:, j * LANES : (j + 1) * LANES]
        line = jnp.sum(sums.T, axis=0, keepdims=True)
        part = lax.dot_general(
            shifted[0:lats, span], resid.astype(BF16), (((1,), (1,)), ((), ())), preferred_element_type=F32
        )
        load_ref[:, rows] = part if at == 0 else load_ref[:, rows] + part
        bias_ref[:, rows] = line if at == 0 else bias_ref[:, rows] + line
    outward = [
        pltpu.make_async_copy(load_ref, load_hbm.at[:, place], sems.at[1]),
        pltpu.make_async_copy(bias_ref, bias_hbm.at[:, place], sems.at[2]),
    ]
    for copy in outward:
        copy.start()
    for copy in outward:
        copy.wait()


def per_device(region_count, neuron_count, counts, latents, loadings, bias, delays, recorded):
    neurons, total = counts.shape[1:]
    lats, width = latents.shape
    chunk, step = 256, 512
    vmem = pl.BlockSpec(memory_space=pltpu.VMEM)
    hbm = pl.BlockSpec(memory_space=pltpu.HBM)
    params = pltpu.CompilerParams(vmem_limit_bytes=52 * 1024 * 1024)

    def swap(value, axis, count, mask):
        return lax.ppermute(value, axis, [(i, i ^ mask) for i in range(count)])

    arrived = [swap(latents, "neuron", neuron_count, k) for k in range(1, neuron_count)]
    pack = jnp.concatenate([loadings[0], latents], axis=1)
    row = lax.broadcasted_iota(jnp.int32, (8, neurons), 0)
    lines = jnp.pad(delays, ((1, 6), (0, neurons - lats)))
    lines = jnp.where(row == 2, jnp.broadcast_to(recorded[:, None], lines.shape), lines)
    meta = jnp.pad(bias, ((0, 7), (0, 0))) + lines.astype(F32)

    early = 3 * chunk
    *outs, load_ext, shifted = pl.pallas_call(
        functools.partial(shift_kernel, neuron_count, "neuron", chunk, step, early),
        out_shape=[jax.ShapeDtypeStruct((lats, width), BF16 if k else F32) for k in range(neuron_count)]
        + [jax.ShapeDtypeStruct((lats + EXTRA, neurons), BF16), jax.ShapeDtypeStruct((lats + EXTRA, total), BF16)],
        in_specs=[vmem, vmem, hbm] + [vmem] * (neuron_count - 1),
        out_specs=[vmem] * (neuron_count + 2),
        scratch_shapes=[
            pltpu.VMEM((lats, total), BF16),
            pltpu.VMEM((neurons, total), BF16),
            pltpu.VMEM((early, total), F32),
            pltpu.VMEM((lats, total), F32),
            pltpu.SemaphoreType.DMA,
        ],
        compiler_params=params,
    )(meta, pack, counts[0], *arrived)

    shares = [(0, 2 * chunk), (2 * chunk, 2 * chunk), (4 * chunk, neurons - 4 * chunk)]
    made = []

    def make(before):
        first, count = shares.pop(0)
        before, start_load = lax.optimization_barrier((before, load_ext))
        out = pl.pallas_call(
            functools.partial(load_kernel, lats, first, chunk, step),
            out_shape=[jax.ShapeDtypeStruct((lats, neurons), F32), jax.ShapeDtypeStruct((1, neurons), F32)],
            in_specs=[vmem, vmem, vmem, hbm] + [hbm] * len(made),
            out_specs=[hbm, hbm],
            scratch_shapes=[
                pltpu.VMEM((count, total), BF16),
                pltpu.VMEM((count, total), F32),
                pltpu.VMEM((lats, count), F32),
                pltpu.VMEM((1, count), F32),
                pltpu.SemaphoreType.DMA((3,)),
            ],
            input_output_aliases={4 + i: i for i in range(len(made))},
            compiler_params=params,
            cost_estimate=pl.CostEstimate(
                flops=4 * lats * count * total, bytes_accessed=2 * count * total, transcendentals=count * total
            ),
        )(meta, start_load, shifted, counts[0], *made)
        return before, out

    outs, made = make(outs)
    arrived = [swap(outs[k], "neuron", neuron_count, k) for k in range(1, neuron_count)]
    arrived, made = lax.optimization_barrier((arrived, made))
    value = functools.reduce(jnp.add, [outs[0]] + [block.astype(F32) for block in arrived])
    mask = 1
    while mask < region_count:
        masks = [mask, 2 * mask, 3 * mask] if 2 * mask < region_count else [mask]
        several = len(masks) > 1
        if several:
            value = lax.reduce_precision(value, 8, 7)
        sent = value.astype(BF16) if several else value
        if shares:
            (value, sent), made = make((value, sent))
        arrived = [swap(sent, "region", region_count, k) for k in masks]
        arrived, made = lax.optimization_barrier((arrived, made))
        arrived = [block.astype(F32) for block in arrived]
        value = value + arrived[0]
        if several:
            value = value + (arrived[1] + arrived[2])
        mask *= 1 + len(masks)
    grad_load, grad_bias = made
    return (value, grad_load[None], grad_bias)


def solution(mesh):
    placed = (
        P("region", "neuron", None),
        P(None, "neuron"),
        P("region", None, "neuron"),
        P("region", "neuron"),
        P("region", None),
        P("region"),
    )
    return jax.shard_map(
        functools.partial(per_device, mesh.shape["region"], mesh.shape["neuron"]),
        mesh=mesh,
        in_specs=placed,
        out_specs=(P(None, "neuron"), P("region", None, "neuron"), P("region", "neuron")),
        check_vma=False,
    )
```

```python
import functools

import jax
import jax.numpy as jnp
from jax import lax
from jax.experimental import pallas as pl
from jax.experimental.pallas import tpu as pltpu
from jax.sharding import PartitionSpec as P

LANES = 128
EXTRA = 16
F32 = jnp.float32
BF16 = jnp.bfloat16


def shift_tiles(tiles, delay, forward):
    lane = lax.broadcasted_iota(jnp.int32, delay.shape, 1)
    source = lane - delay if forward else lane + delay
    inside = source >= 0 if forward else source < LANES
    source = source & (LANES - 1)
    turned = [jnp.take_along_axis(tile, source, axis=1, mode="promise_in_bounds") for tile in tiles]
    nothing = [jnp.zeros_like(tiles[0])]
    others = nothing + turned[:-1] if forward else turned[1:] + nothing
    return [jnp.where(inside, tile, other) for tile, other in zip(turned, others)]


def expected(load_part, piece):
    eta = lax.dot_general(load_part, piece, (((0,), (0,)), ((), ())), preferred_element_type=F32)
    return jnp.exp(eta)


def shift_kernel(parts, axis, chunk, step, early, *refs):
    meta_ref, pack_ref, counts_hbm = refs[:3]
    arrived = refs[3 : 2 + parts]
    outs = refs[2 + parts : 2 + 2 * parts]
    load_ext, shifted, whole, counts_ref, held, grad_shift, counts_sem = refs[2 + 2 * parts :]
    me = lax.axis_index(axis)
    lats, total = grad_shift.shape
    neurons = counts_ref.shape[0]
    width = total // parts
    counts_copy = pltpu.make_async_copy(counts_hbm, counts_ref, counts_sem)
    counts_copy.start()

    for k in range(parts):
        start = pl.multiple_of((me ^ k) * width, width)
        whole[:, pl.ds(start, width)] = arrived[k - 1][...] if k else pack_ref[:, neurons:]
    diagonal = lax.broadcasted_iota(jnp.int32, (lats, LANES), 0) == lax.broadcasted_iota(jnp.int32, (lats, LANES), 1)
    spread = jnp.broadcast_to(meta_ref[1:2, 0:LANES], (lats, LANES))
    column = jnp.sum(jnp.where(diagonal, spread, 0.0), axis=1, keepdims=True)
    delay = jnp.broadcast_to(column, (lats, LANES)).astype(jnp.int32)
    length = meta_ref[2:3, 0:1].astype(jnp.int32)
    tiles = [whole[:, j * LANES : (j + 1) * LANES].astype(F32) for j in range(total // LANES)]
    for j, tile in enumerate(shift_tiles(tiles, delay, True)):
        shifted[0:lats, j * LANES : (j + 1) * LANES] = tile.astype(BF16)
    row = lax.broadcasted_iota(jnp.int32, (EXTRA, total), 0)
    shifted[lats:, :] = jnp.where(row < 3, 1.0, 0.0).astype(BF16)

    load_ext[0:lats, :] = pack_ref[:, 0:neurons]
    bias = meta_ref[0:1, :]
    high = bias.astype(BF16).astype(F32)
    middle = (bias - high).astype(BF16).astype(F32)
    low = bias - high - middle
    row = lax.broadcasted_iota(jnp.int32, (EXTRA, neurons), 0)
    below = jnp.where(row == 0, high, jnp.where(row == 1, middle, jnp.where(row == 2, low, 0.0)))
    load_ext[lats:, :] = below.astype(BF16)

    blocks = [
        (slice(first, first + chunk), slice(begin, begin + step))
        for first in range(0, neurons, chunk)
        for begin in range(0, total, step)
    ]
    for rows, span in blocks:
        if rows.start < early:
            held[rows, span] = expected(load_ext[:, rows], shifted[:, span])
    counts_copy.wait()
    for rows, span in blocks:
        rate = held[rows, span] if rows.start < early else expected(load_ext[:, rows], shifted[:, span])
        resid = rate - counts_ref[rows, span].astype(F32)
        part = jnp.dot(load_ext[0:lats, rows], resid.astype(BF16), preferred_element_type=F32)
        grad_shift[:, span] = part if rows.start == 0 else grad_shift[:, span] + part

    bins = lax.broadcasted_iota(jnp.int32, (1, total), 1)
    tiles = []
    for j in range(total // LANES):
        span = slice(j * LANES, (j + 1) * LANES)
        tiles.append(jnp.where(bins[:, span] < length, grad_shift[:, span], 0.0))
    for j, tile in enumerate(shift_tiles(tiles, delay, False)):
        grad_shift[:, j * LANES : (j + 1) * LANES] = tile
    for k in range(parts):
        start = pl.multiple_of((me ^ k) * width, width)
        outs[k][...] = grad_shift[:, pl.ds(start, width)].astype(outs[k].dtype)


def load_kernel(lats, first, chunk, step, *refs):
    meta_ref, load_ext, shifted, counts_hbm = refs[:4]
    load_hbm, bias_hbm, counts_ref, held, load_ref, bias_ref, sems = refs[-7:]
    count, total = counts_ref.shape
    place = pl.ds(first, count)
    counts_copy = pltpu.make_async_copy(counts_hbm.at[place], counts_ref, sems.at[0])
    counts_copy.start()
    length = meta_ref[2:3, 0:1].astype(jnp.int32)
    bins = lax.broadcasted_iota(jnp.int32, (1, total), 1)
    blocks = [(slice(begin, begin + chunk), range(0, total, step)) for begin in range(0, count, chunk)]
    for rows, starts in blocks:
        for at in starts:
            load_part = load_ext[:, first + rows.start : first + rows.stop]
            held[rows, at : at + step] = expected(load_part, shifted[:, at : at + step])
    counts_copy.wait()
    outward = []
    for index, (rows, starts) in enumerate(blocks):
        sums = jnp.zeros((chunk, LANES), F32)
        grad = jnp.zeros((chunk, lats), F32)
        for at in starts:
            span = slice(at, at + step)
            resid = jnp.where(bins[:, span] < length, held[rows, span] - counts_ref[rows, span].astype(F32), 0.0)
            for j in range(step // LANES):
                sums = sums + resid[:, j * LANES : (j + 1) * LANES]
            grad = grad + lax.dot_general(
                resid.astype(BF16), shifted[0:lats, span], (((1,), (1,)), ((), ())), preferred_element_type=F32
            )
        load_ref[:, rows] = grad.T
        bias_ref[:, rows] = jnp.sum(sums.T, axis=0, keepdims=True)
        place = pl.ds(first + rows.start, chunk)
        outward.append(pltpu.make_async_copy(load_ref.at[:, rows], load_hbm.at[:, place], sems.at[2 * index + 1]))
        outward.append(pltpu.make_async_copy(bias_ref.at[:, rows], bias_hbm.at[:, place], sems.at[2 * index + 2]))
        for copy in outward[-2:]:
            copy.start()
    for copy in outward:
        copy.wait()


def per_device(region_count, neuron_count, counts, latents, loadings, bias, delays, recorded):
    neurons, total = counts.shape[1:]
    lats, width = latents.shape
    chunk, step = 256, 512
    vmem = pl.BlockSpec(memory_space=pltpu.VMEM)
    hbm = pl.BlockSpec(memory_space=pltpu.HBM)
    params = pltpu.CompilerParams(vmem_limit_bytes=52 * 1024 * 1024)

    def swap(value, axis, count, mask):
        return lax.ppermute(value, axis, [(i, i ^ mask) for i in range(count)])

    held = {0: latents}
    masks = [1 << level for level in range(1, neuron_count.bit_length() - 1)] + [1]
    for mask in masks:
        for k, block in list(held.items()):
            held[k ^ mask] = swap(block, "neuron", neuron_count, mask)
    arrived = [held[k] for k in range(1, neuron_count)]
    pack = jnp.concatenate([loadings[0], latents], axis=1)
    row = lax.broadcasted_iota(jnp.int32, (8, neurons), 0)
    lines = jnp.pad(delays, ((1, 6), (0, neurons - lats)))
    lines = jnp.where(row == 2, jnp.broadcast_to(recorded[:, None], lines.shape), lines)
    meta = jnp.pad(bias, ((0, 7), (0, 0))) + lines.astype(F32)

    early = 4 * chunk
    *outs, load_ext, shifted = pl.pallas_call(
        functools.partial(shift_kernel, neuron_count, "neuron", chunk, step, early),
        out_shape=[jax.ShapeDtypeStruct((lats, width), BF16 if k > 1 else F32) for k in range(neuron_count)]
        + [jax.ShapeDtypeStruct((lats + EXTRA, neurons), BF16), jax.ShapeDtypeStruct((lats + EXTRA, total), BF16)],
        in_specs=[vmem, vmem, hbm] + [vmem] * (neuron_count - 1),
        out_specs=[vmem] * (neuron_count + 2),
        scratch_shapes=[
            pltpu.VMEM((lats, total), BF16),
            pltpu.VMEM((neurons, total), BF16),
            pltpu.VMEM((early, total), F32),
            pltpu.VMEM((lats, total), F32),
            pltpu.SemaphoreType.DMA,
        ],
        compiler_params=params,
    )(meta, pack, counts[0], *arrived)

    shares = [(0, 2 * chunk), (2 * chunk, 2 * chunk), (4 * chunk, neurons - 4 * chunk)]
    made = []

    def make(before):
        first, count = shares.pop(0)
        before, start_load = lax.optimization_barrier((before, load_ext))
        out = pl.pallas_call(
            functools.partial(load_kernel, lats, first, chunk, step),
            out_shape=[jax.ShapeDtypeStruct((lats, neurons), F32), jax.ShapeDtypeStruct((1, neurons), F32)],
            in_specs=[vmem, vmem, vmem, hbm] + [hbm] * len(made),
            out_specs=[hbm, hbm],
            scratch_shapes=[
                pltpu.VMEM((count, total), BF16),
                pltpu.VMEM((count, total), F32),
                pltpu.VMEM((lats, count), F32),
                pltpu.VMEM((1, count), F32),
                pltpu.SemaphoreType.DMA((1 + 2 * (count // chunk),)),
            ],
            input_output_aliases={4 + i: i for i in range(len(made))},
            compiler_params=params,
            cost_estimate=pl.CostEstimate(
                flops=4 * lats * count * total, bytes_accessed=2 * count * total, transcendentals=count * total
            ),
        )(meta, start_load, shifted, counts[0], *made)
        return before, out

    outs, made = make(outs)
    arrived = [swap(outs[k], "neuron", neuron_count, k) for k in range(1, neuron_count)]
    arrived, made = lax.optimization_barrier((arrived, made))
    value = functools.reduce(jnp.add, [outs[0]] + [block.astype(F32) for block in arrived])
    mask = 1
    while mask < region_count:
        masks = [mask, 2 * mask, 3 * mask] if 2 * mask < region_count else [mask]
        several = len(masks) > 1
        if several:
            value = lax.reduce_precision(value, 8, 7)
        sent = value.astype(BF16) if several else value
        if shares:
            (value, sent), made = make((value, sent))
        arrived = [swap(sent, "region", region_count, k) for k in masks]
        arrived, made = lax.optimization_barrier((arrived, made))
        arrived = [block.astype(F32) for block in arrived]
        value = value + arrived[0]
        if several:
            value = value + (arrived[1] + arrived[2])
        mask *= 1 + len(masks)
    grad_load, grad_bias = made
    return (value, grad_load[None], grad_bias)


def solution(mesh):
    placed = (
        P("region", "neuron", None),
        P(None, "neuron"),
        P("region", None, "neuron"),
        P("region", "neuron"),
        P("region", None),
        P("region"),
    )
    return jax.shard_map(
        functools.partial(per_device, mesh.shape["region"], mesh.shape["neuron"]),
        mesh=mesh,
        in_specs=placed,
        out_specs=(P(None, "neuron"), P("region", None, "neuron"), P("region", "neuron")),
        check_vma=False,
    )
```

```python
import functools

import jax
import jax.numpy as jnp
from jax import lax
from jax.experimental import pallas as pl
from jax.experimental.pallas import tpu as pltpu
from jax.sharding import PartitionSpec as P

LANES = 128
EXTRA = 16
F32 = jnp.float32
BF16 = jnp.bfloat16


def shift_tiles(tiles, delay, forward):
    lane = lax.broadcasted_iota(jnp.int32, delay.shape, 1)
    source = lane - delay if forward else lane + delay
    inside = source >= 0 if forward else source < LANES
    source = source & (LANES - 1)
    turned = [jnp.take_along_axis(tile, source, axis=1, mode="promise_in_bounds") for tile in tiles]
    nothing = [jnp.zeros_like(tiles[0])]
    others = nothing + turned[:-1] if forward else turned[1:] + nothing
    return [jnp.where(inside, tile, other) for tile, other in zip(turned, others)]


def expected(load_part, piece):
    eta = lax.dot_general(load_part, piece, (((0,), (0,)), ((), ())), preferred_element_type=F32)
    return jnp.exp(eta)


def shift_kernel(parts, order, axis, chunk, step, *refs):
    meta_ref, pack_ref, counts_hbm = refs[:3]
    arrived = refs[3 : 2 + parts]
    outs = refs[2 + parts : 2 + 2 * parts]
    load_ext, shifted, whole, counts_ref, held, grad_shift, counts_sems = refs[2 + 2 * parts :]
    me = lax.axis_index(axis)
    lats, total = grad_shift.shape
    neurons = counts_ref.shape[0]
    width = total // parts
    cut = (neurons // chunk + 1) // 2 * chunk
    copies = []
    for index, place in enumerate([pl.ds(0, cut), pl.ds(cut, neurons - cut)]):
        copies.append(pltpu.make_async_copy(counts_hbm.at[place], counts_ref.at[place], counts_sems.at[index]))
        copies[-1].start()

    for k in range(parts):
        start = pl.multiple_of((me ^ k) * width, width)
        whole[:, pl.ds(start, width)] = arrived[order.index(k)][...] if k else pack_ref[:, neurons:]
    diagonal = lax.broadcasted_iota(jnp.int32, (lats, LANES), 0) == lax.broadcasted_iota(jnp.int32, (lats, LANES), 1)
    spread = jnp.broadcast_to(meta_ref[1:2, 0:LANES], (lats, LANES))
    column = jnp.sum(jnp.where(diagonal, spread, 0.0), axis=1, keepdims=True)
    delay = jnp.broadcast_to(column, (lats, LANES)).astype(jnp.int32)
    length = meta_ref[2:3, 0:1].astype(jnp.int32)
    tiles = [whole[:, j * LANES : (j + 1) * LANES].astype(F32) for j in range(total // LANES)]
    for j, tile in enumerate(shift_tiles(tiles, delay, True)):
        shifted[0:lats, j * LANES : (j + 1) * LANES] = tile.astype(BF16)
    row = lax.broadcasted_iota(jnp.int32, (EXTRA, total), 0)
    shifted[lats:, :] = jnp.where(row < 3, 1.0, 0.0).astype(BF16)

    load_ext[0:lats, :] = pack_ref[:, 0:neurons]
    bias = meta_ref[0:1, :]
    high = bias.astype(BF16).astype(F32)
    middle = (bias - high).astype(BF16).astype(F32)
    low = bias - high - middle
    row = lax.broadcasted_iota(jnp.int32, (EXTRA, neurons), 0)
    below = jnp.where(row == 0, high, jnp.where(row == 1, middle, jnp.where(row == 2, low, 0.0)))
    load_ext[lats:, :] = below.astype(BF16)

    blocks = [
        (slice(first, first + chunk), slice(begin, begin + step))
        for first in range(0, neurons, chunk)
        for begin in range(0, total, step)
    ]
    for rows, span in blocks:
        held[rows, span] = expected(load_ext[:, rows], shifted[:, span])
    copies[0].wait()
    for rows, span in blocks:
        if rows.start == cut and span.start == 0:
            copies[1].wait()
        resid = held[rows, span] - counts_ref[rows, span].astype(F32)
        part = jnp.dot(load_ext[0:lats, rows], resid.astype(BF16), preferred_element_type=F32)
        grad_shift[:, span] = part if rows.start == 0 else grad_shift[:, span] + part

    bins = lax.broadcasted_iota(jnp.int32, (1, total), 1)
    tiles = []
    for j in range(total // LANES):
        span = slice(j * LANES, (j + 1) * LANES)
        tiles.append(jnp.where(bins[:, span] < length, grad_shift[:, span], 0.0))
    for j, tile in enumerate(shift_tiles(tiles, delay, False)):
        grad_shift[:, j * LANES : (j + 1) * LANES] = tile
    for k in range(parts):
        start = pl.multiple_of((me ^ k) * width, width)
        outs[k][...] = grad_shift[:, pl.ds(start, width)].astype(outs[k].dtype)


def load_kernel(lats, first, chunk, step, *refs):
    meta_ref, load_ext, shifted, counts_hbm = refs[:4]
    load_hbm, bias_hbm, counts_ref, held, load_ref, bias_ref, sems = refs[-7:]
    count, total = counts_ref.shape
    place = pl.ds(first, count)
    counts_copy = pltpu.make_async_copy(counts_hbm.at[place], counts_ref, sems.at[0])
    counts_copy.start()
    length = meta_ref[2:3, 0:1].astype(jnp.int32)
    bins = lax.broadcasted_iota(jnp.int32, (1, total), 1)
    blocks = [(slice(begin, begin + chunk), range(0, total, step)) for begin in range(0, count, chunk)]
    for rows, starts in blocks:
        for at in starts:
            load_part = load_ext[:, first + rows.start : first + rows.stop]
            held[rows, at : at + step] = expected(load_part, shifted[:, at : at + step])
    counts_copy.wait()
    outward = []
    for index, (rows, starts) in enumerate(blocks):
        sums = jnp.zeros((chunk, LANES), F32)
        grad = jnp.zeros((chunk, lats), F32)
        for at in starts:
            span = slice(at, at + step)
            resid = jnp.where(bins[:, span] < length, held[rows, span] - counts_ref[rows, span].astype(F32), 0.0)
            for j in range(step // LANES):
                sums = sums + resid[:, j * LANES : (j + 1) * LANES]
            grad = grad + lax.dot_general(
                resid.astype(BF16), shifted[0:lats, span], (((1,), (1,)), ((), ())), preferred_element_type=F32
            )
        load_ref[:, rows] = grad.T
        bias_ref[:, rows] = jnp.sum(sums.T, axis=0, keepdims=True)
        place = pl.ds(first + rows.start, chunk)
        outward.append(pltpu.make_async_copy(load_ref.at[:, rows], load_hbm.at[:, place], sems.at[2 * index + 1]))
        outward.append(pltpu.make_async_copy(bias_ref.at[:, rows], bias_hbm.at[:, place], sems.at[2 * index + 2]))
        for copy in outward[-2:]:
            copy.start()
    for copy in outward:
        copy.wait()


def per_device(region_count, neuron_count, counts, latents, loadings, bias, delays, recorded):
    neurons, total = counts.shape[1:]
    lats, width = latents.shape
    chunk, step = 256, 512
    vmem = pl.BlockSpec(memory_space=pltpu.VMEM)
    hbm = pl.BlockSpec(memory_space=pltpu.HBM)
    params = pltpu.CompilerParams(vmem_limit_bytes=52 * 1024 * 1024)

    def swap(value, axis, count, mask):
        return lax.ppermute(value, axis, [(i, i ^ mask) for i in range(count)])

    order = sorted(range(1, neuron_count), key=lambda k: (k != 2, k))
    arrived = [swap(latents, "neuron", neuron_count, k) for k in order]
    pack = jnp.concatenate([loadings[0], latents], axis=1)
    row = lax.broadcasted_iota(jnp.int32, (8, neurons), 0)
    lines = jnp.pad(delays, ((1, 6), (0, neurons - lats)))
    lines = jnp.where(row == 2, jnp.broadcast_to(recorded[:, None], lines.shape), lines)
    meta = jnp.pad(bias, ((0, 7), (0, 0))) + lines.astype(F32)

    *outs, load_ext, shifted = pl.pallas_call(
        functools.partial(shift_kernel, neuron_count, order, "neuron", chunk, step),
        out_shape=[jax.ShapeDtypeStruct((lats, width), BF16 if k > 1 else F32) for k in range(neuron_count)]
        + [jax.ShapeDtypeStruct((lats + EXTRA, neurons), BF16), jax.ShapeDtypeStruct((lats + EXTRA, total), BF16)],
        in_specs=[vmem, vmem, hbm] + [vmem] * (neuron_count - 1),
        out_specs=[vmem] * (neuron_count + 2),
        scratch_shapes=[
            pltpu.VMEM((lats, total), BF16),
            pltpu.VMEM((neurons, total), BF16),
            pltpu.VMEM((neurons, total), F32),
            pltpu.VMEM((lats, total), F32),
            pltpu.SemaphoreType.DMA((2,)),
        ],
        compiler_params=params,
    )(meta, pack, counts[0], *arrived)

    shares = [(0, 2 * chunk), (2 * chunk, 2 * chunk), (4 * chunk, neurons - 4 * chunk)]
    made = []

    def make(before):
        first, count = shares.pop(0)
        before, start_load = lax.optimization_barrier((before, load_ext))
        out = pl.pallas_call(
            functools.partial(load_kernel, lats, first, chunk, step),
            out_shape=[jax.ShapeDtypeStruct((lats, neurons), F32), jax.ShapeDtypeStruct((1, neurons), F32)],
            in_specs=[vmem, vmem, vmem, hbm] + [hbm] * len(made),
            out_specs=[hbm, hbm],
            scratch_shapes=[
                pltpu.VMEM((count, total), BF16),
                pltpu.VMEM((count, total), F32),
                pltpu.VMEM((lats, count), F32),
                pltpu.VMEM((1, count), F32),
                pltpu.SemaphoreType.DMA((1 + 2 * (count // chunk),)),
            ],
            input_output_aliases={4 + i: i for i in range(len(made))},
            compiler_params=params,
            cost_estimate=pl.CostEstimate(
                flops=4 * lats * count * total, bytes_accessed=2 * count * total, transcendentals=count * total
            ),
        )(meta, start_load, shifted, counts[0], *made)
        return before, out

    outs, made = make(outs)
    arrived = [swap(outs[k], "neuron", neuron_count, k) for k in [*range(2, neuron_count), 1]]
    arrived, made = lax.optimization_barrier((arrived, made))
    value = functools.reduce(jnp.add, [outs[0]] + [block.astype(F32) for block in arrived])
    mask = 1
    while mask < region_count:
        masks = [mask, 2 * mask, 3 * mask] if 2 * mask < region_count else [mask]
        several = len(masks) > 1
        if several:
            value = lax.reduce_precision(value, 8, 7)
        sent = value.astype(BF16) if several else value
        if shares:
            (value, sent), made = make((value, sent))
        arrived = [swap(sent, "region", region_count, k) for k in masks]
        arrived, made = lax.optimization_barrier((arrived, made))
        arrived = [block.astype(F32) for block in arrived]
        value = value + arrived[0]
        if several:
            value = value + (arrived[1] + arrived[2])
        mask *= 1 + len(masks)
    grad_load, grad_bias = made
    return (value, grad_load[None], grad_bias)


def solution(mesh):
    placed = (
        P("region", "neuron", None),
        P(None, "neuron"),
        P("region", None, "neuron"),
        P("region", "neuron"),
        P("region", None),
        P("region"),
    )
    return jax.shard_map(
        functools.partial(per_device, mesh.shape["region"], mesh.shape["neuron"]),
        mesh=mesh,
        in_specs=placed,
        out_specs=(P(None, "neuron"), P("region", None, "neuron"), P("region", "neuron")),
        check_vma=False,
    )
```

```python
import functools

import jax
import jax.numpy as jnp
from jax import lax
from jax.experimental import pallas as pl
from jax.experimental.pallas import tpu as pltpu
from jax.sharding import PartitionSpec as P

LANES = 128
EXTRA = 16
F32 = jnp.float32
BF16 = jnp.bfloat16


def shift_tiles(tiles, delay, forward):
    lane = lax.broadcasted_iota(jnp.int32, delay.shape, 1)
    source = lane - delay if forward else lane + delay
    inside = source >= 0 if forward else source < LANES
    source = source & (LANES - 1)
    turned = [jnp.take_along_axis(tile, source, axis=1, mode="promise_in_bounds") for tile in tiles]
    nothing = [jnp.zeros_like(tiles[0])]
    others = nothing + turned[:-1] if forward else turned[1:] + nothing
    return [jnp.where(inside, tile, other) for tile, other in zip(turned, others)]


def expected(load_part, piece):
    eta = lax.dot_general(load_part, piece, (((0,), (0,)), ((), ())), preferred_element_type=F32)
    return jnp.exp(eta)


def shift_kernel(parts, order, axis, chunk, step, *refs):
    pack_ref, counts_hbm = refs[:2]
    arrived = refs[2 : 1 + parts]
    outs = refs[1 + parts : 1 + 2 * parts]
    load_ext, shifted, whole, counts_ref, held, grad_shift, counts_sem = refs[1 + 2 * parts :]
    me = lax.axis_index(axis)
    lats, total = grad_shift.shape
    early = held.shape[0]
    neurons = counts_ref.shape[0]
    width = total // parts
    counts_copy = pltpu.make_async_copy(counts_hbm, counts_ref, counts_sem)
    counts_copy.start()

    for k in range(parts):
        start = pl.multiple_of((me ^ k) * width, width)
        whole[:, pl.ds(start, width)] = arrived[order.index(k)][...] if k else pack_ref[0:lats, neurons:].astype(BF16)
    diagonal = lax.broadcasted_iota(jnp.int32, (lats, LANES), 0) == lax.broadcasted_iota(jnp.int32, (lats, LANES), 1)
    spread = jnp.broadcast_to(pack_ref[lats + 1 : lats + 2, 0:LANES], (lats, LANES))
    column = jnp.sum(jnp.where(diagonal, spread, 0.0), axis=1, keepdims=True)
    delay = jnp.broadcast_to(column, (lats, LANES)).astype(jnp.int32)
    length = pack_ref[lats + 2 : lats + 3, 0:1].astype(jnp.int32)
    tiles = [whole[:, j * LANES : (j + 1) * LANES].astype(F32) for j in range(total // LANES)]
    for j, tile in enumerate(shift_tiles(tiles, delay, True)):
        shifted[0:lats, j * LANES : (j + 1) * LANES] = tile.astype(BF16)
    row = lax.broadcasted_iota(jnp.int32, (EXTRA, total), 0)
    shifted[lats:, :] = jnp.where(row < 3, 1.0, 0.0).astype(BF16)

    load_ext[0:lats, :] = pack_ref[0:lats, 0:neurons].astype(BF16)
    bias = pack_ref[lats : lats + 1, 0:neurons]
    high = bias.astype(BF16).astype(F32)
    middle = (bias - high).astype(BF16).astype(F32)
    low = bias - high - middle
    row = lax.broadcasted_iota(jnp.int32, (EXTRA, neurons), 0)
    below = jnp.where(row == 0, high, jnp.where(row == 1, middle, jnp.where(row == 2, low, 0.0)))
    load_ext[lats:, :] = below.astype(BF16)

    blocks = [
        (slice(first, first + chunk), slice(begin, begin + step))
        for first in range(0, neurons, chunk)
        for begin in range(0, total, step)
    ]
    for rows, span in blocks:
        if rows.start < early:
            held[rows, span] = expected(load_ext[:, rows], shifted[:, span])
    counts_copy.wait()
    for rows, span in blocks:
        rate = held[rows, span] if rows.start < early else expected(load_ext[:, rows], shifted[:, span])
        resid = rate - counts_ref[rows, span].astype(F32)
        part = jnp.dot(load_ext[0:lats, rows], resid.astype(BF16), preferred_element_type=F32)
        grad_shift[:, span] = part if rows.start == 0 else grad_shift[:, span] + part

    bins = lax.broadcasted_iota(jnp.int32, (1, total), 1)
    tiles = []
    for j in range(total // LANES):
        span = slice(j * LANES, (j + 1) * LANES)
        tiles.append(jnp.where(bins[:, span] < length, grad_shift[:, span], 0.0))
    for j, tile in enumerate(shift_tiles(tiles, delay, False)):
        grad_shift[:, j * LANES : (j + 1) * LANES] = tile
    for k in range(parts):
        start = pl.multiple_of((me ^ k) * width, width)
        outs[k][...] = grad_shift[:, pl.ds(start, width)].astype(outs[k].dtype)


def load_kernel(lats, first, chunk, step, *refs):
    pack_ref, load_ext, shifted, counts_hbm = refs[:4]
    load_hbm, bias_hbm, counts_ref, held, load_ref, bias_ref, sems = refs[-7:]
    count, total = counts_ref.shape
    place = pl.ds(first, count)
    counts_copy = pltpu.make_async_copy(counts_hbm.at[place], counts_ref, sems.at[0])
    counts_copy.start()
    length = pack_ref[lats + 2 : lats + 3, 0:1].astype(jnp.int32)
    bins = lax.broadcasted_iota(jnp.int32, (1, total), 1)
    blocks = [(slice(begin, begin + chunk), range(0, total, step)) for begin in range(0, count, chunk)]
    for rows, starts in blocks:
        for at in starts:
            load_part = load_ext[:, first + rows.start : first + rows.stop]
            held[rows, at : at + step] = expected(load_part, shifted[:, at : at + step])
    counts_copy.wait()
    outward = []
    for index, (rows, starts) in enumerate(blocks):
        sums = jnp.zeros((chunk, LANES), F32)
        grad = jnp.zeros((chunk, lats), F32)
        for at in starts:
            span = slice(at, at + step)
            resid = jnp.where(bins[:, span] < length, held[rows, span] - counts_ref[rows, span].astype(F32), 0.0)
            for j in range(step // LANES):
                sums = sums + resid[:, j * LANES : (j + 1) * LANES]
            grad = grad + lax.dot_general(
                resid.astype(BF16), shifted[0:lats, span], (((1,), (1,)), ((), ())), preferred_element_type=F32
            )
        load_ref[:, rows] = grad.T
        bias_ref[:, rows] = jnp.sum(sums.T, axis=0, keepdims=True)
        place = pl.ds(first + rows.start, chunk)
        outward.append(pltpu.make_async_copy(load_ref.at[:, rows], load_hbm.at[:, place], sems.at[2 * index + 1]))
        outward.append(pltpu.make_async_copy(bias_ref.at[:, rows], bias_hbm.at[:, place], sems.at[2 * index + 2]))
        for copy in outward[-2:]:
            copy.start()
    for copy in outward:
        copy.wait()


def per_device(region_count, neuron_count, counts, latents, loadings, bias, delays, recorded):
    neurons, total = counts.shape[1:]
    lats, width = latents.shape
    chunk, step = 256, 512
    vmem = pl.BlockSpec(memory_space=pltpu.VMEM)
    hbm = pl.BlockSpec(memory_space=pltpu.HBM)
    params = pltpu.CompilerParams(vmem_limit_bytes=52 * 1024 * 1024)

    def swap(value, axis, count, mask):
        return lax.ppermute(value, axis, [(i, i ^ mask) for i in range(count)])

    order = sorted(range(1, neuron_count), key=lambda k: (k != 2, k))
    arrived = [swap(latents, "neuron", neuron_count, k) for k in order]
    row = lax.broadcasted_iota(jnp.int32, (lats + 8, neurons + width), 0)
    lines = jnp.pad(delays, ((lats + 1, 6), (0, neurons + width - lats)))
    lines = jnp.where(row == lats + 2, jnp.broadcast_to(recorded[:, None], lines.shape), lines)
    pack = jnp.pad(bias, ((lats, 7), (0, width))) + lines.astype(F32)
    pack = pack + jnp.pad(loadings[0], ((0, 8), (0, width))).astype(F32)
    pack = pack + jnp.pad(latents, ((0, 8), (neurons, 0))).astype(F32)

    *outs, load_ext, shifted = pl.pallas_call(
        functools.partial(shift_kernel, neuron_count, order, "neuron", chunk, step),
        out_shape=[jax.ShapeDtypeStruct((lats, width), BF16 if k > 1 else F32) for k in range(neuron_count)]
        + [jax.ShapeDtypeStruct((lats + EXTRA, neurons), BF16), jax.ShapeDtypeStruct((lats + EXTRA, total), BF16)],
        in_specs=[vmem, hbm] + [vmem] * (neuron_count - 1),
        out_specs=[vmem] * (neuron_count + 2),
        scratch_shapes=[
            pltpu.VMEM((lats, total), BF16),
            pltpu.VMEM((neurons, total), BF16),
            pltpu.VMEM((4 * chunk, total), F32),
            pltpu.VMEM((lats, total), F32),
            pltpu.SemaphoreType.DMA,
        ],
        compiler_params=params,
    )(pack, counts[0], *arrived)

    shares = [(0, 2 * chunk), (2 * chunk, 2 * chunk), (4 * chunk, neurons - 4 * chunk)]
    made = []

    def make(before):
        first, count = shares.pop(0)
        before, start_load = lax.optimization_barrier((before, load_ext))
        out = pl.pallas_call(
            functools.partial(load_kernel, lats, first, chunk, step),
            out_shape=[jax.ShapeDtypeStruct((lats, neurons), F32), jax.ShapeDtypeStruct((1, neurons), F32)],
            in_specs=[vmem, vmem, vmem, hbm] + [hbm] * len(made),
            out_specs=[hbm, hbm],
            scratch_shapes=[
                pltpu.VMEM((count, total), BF16),
                pltpu.VMEM((count, total), F32),
                pltpu.VMEM((lats, count), F32),
                pltpu.VMEM((1, count), F32),
                pltpu.SemaphoreType.DMA((1 + 2 * (count // chunk),)),
            ],
            input_output_aliases={4 + i: i for i in range(len(made))},
            compiler_params=params,
            cost_estimate=pl.CostEstimate(
                flops=4 * lats * count * total, bytes_accessed=2 * count * total, transcendentals=count * total
            ),
        )(pack, start_load, shifted, counts[0], *made)
        return before, out

    outs, made = make(outs)
    arrived = [swap(outs[k], "neuron", neuron_count, k) for k in [*range(2, neuron_count), 1]]
    arrived, made = lax.optimization_barrier((arrived, made))
    value = functools.reduce(jnp.add, [outs[0]] + [block.astype(F32) for block in arrived])
    mask = 1
    while mask < region_count:
        masks = [mask, 2 * mask, 3 * mask] if 2 * mask < region_count else [mask]
        several = len(masks) > 1
        if several:
            value = lax.reduce_precision(value, 8, 7)
        sent = value.astype(BF16) if several else value
        if shares:
            (value, sent), made = make((value, sent))
        arrived = [swap(sent, "region", region_count, k) for k in masks]
        arrived, made = lax.optimization_barrier((arrived, made))
        arrived = [block.astype(F32) for block in arrived]
        value = value + arrived[0]
        if several:
            value = value + (arrived[1] + arrived[2])
        mask *= 1 + len(masks)
    grad_load, grad_bias = made
    return (value, grad_load[None], grad_bias)


def solution(mesh):
    placed = (
        P("region", "neuron", None),
        P(None, "neuron"),
        P("region", None, "neuron"),
        P("region", "neuron"),
        P("region", None),
        P("region"),
    )
    return jax.shard_map(
        functools.partial(per_device, mesh.shape["region"], mesh.shape["neuron"]),
        mesh=mesh,
        in_specs=placed,
        out_specs=(P(None, "neuron"), P("region", None, "neuron"), P("region", "neuron")),
        check_vma=False,
    )
```

```python
import functools

import jax
import jax.numpy as jnp
from jax import lax
from jax.experimental import pallas as pl
from jax.experimental.pallas import tpu as pltpu
from jax.sharding import PartitionSpec as P

LANES = 128
EXTRA = 16
F32 = jnp.float32
BF16 = jnp.bfloat16


def shift_tiles(tiles, delay, forward):
    lane = lax.broadcasted_iota(jnp.int32, delay.shape, 1)
    source = lane - delay if forward else lane + delay
    inside = source >= 0 if forward else source < LANES
    source = source & (LANES - 1)
    turned = [jnp.take_along_axis(tile, source, axis=1, mode="promise_in_bounds") for tile in tiles]
    nothing = [jnp.zeros_like(tiles[0])]
    others = nothing + turned[:-1] if forward else turned[1:] + nothing
    return [jnp.where(inside, tile, other) for tile, other in zip(turned, others)]


def expected(load_part, piece):
    eta = lax.dot_general(load_part, piece, (((0,), (0,)), ((), ())), preferred_element_type=F32)
    return jnp.exp(eta)


def shift_kernel(parts, order, axis, chunk, step, *refs):
    pack_ref, counts_hbm = refs[:2]
    arrived = refs[2 : 1 + parts]
    outs = refs[1 + parts : 1 + 2 * parts]
    load_ext, shifted, whole, counts_ref, held, grad_shift, counts_sem = refs[1 + 2 * parts :]
    me = lax.axis_index(axis)
    lats, total = grad_shift.shape
    early = held.shape[0]
    neurons = counts_ref.shape[0]
    width = total // parts
    counts_copy = pltpu.make_async_copy(counts_hbm, counts_ref, counts_sem)
    counts_copy.start()

    for k in range(parts):
        start = pl.multiple_of((me ^ k) * width, width)
        whole[:, pl.ds(start, width)] = arrived[order.index(k)][...] if k else pack_ref[0:lats, neurons:].astype(BF16)
    diagonal = lax.broadcasted_iota(jnp.int32, (lats, LANES), 0) == lax.broadcasted_iota(jnp.int32, (lats, LANES), 1)
    spread = jnp.broadcast_to(pack_ref[lats + 1 : lats + 2, 0:LANES], (lats, LANES))
    column = jnp.sum(jnp.where(diagonal, spread, 0.0), axis=1, keepdims=True)
    delay = jnp.broadcast_to(column, (lats, LANES)).astype(jnp.int32)
    length = pack_ref[lats + 2 : lats + 3, 0:1].astype(jnp.int32)
    tiles = [whole[:, j * LANES : (j + 1) * LANES].astype(F32) for j in range(total // LANES)]
    for j, tile in enumerate(shift_tiles(tiles, delay, True)):
        shifted[0:lats, j * LANES : (j + 1) * LANES] = tile.astype(BF16)
    row = lax.broadcasted_iota(jnp.int32, (EXTRA, total), 0)
    shifted[lats:, :] = jnp.where(row < 3, 1.0, 0.0).astype(BF16)

    load_ext[0:lats, :] = pack_ref[0:lats, 0:neurons].astype(BF16)
    bias = pack_ref[lats : lats + 1, 0:neurons]
    high = bias.astype(BF16).astype(F32)
    middle = (bias - high).astype(BF16).astype(F32)
    low = bias - high - middle
    row = lax.broadcasted_iota(jnp.int32, (EXTRA, neurons), 0)
    below = jnp.where(row == 0, high, jnp.where(row == 1, middle, jnp.where(row == 2, low, 0.0)))
    load_ext[lats:, :] = below.astype(BF16)

    blocks = [
        (slice(first, first + chunk), slice(begin, begin + step))
        for first in range(0, neurons, chunk)
        for begin in range(0, total, step)
    ]
    for rows, span in blocks:
        if rows.start < early:
            held[rows, span] = expected(load_ext[:, rows], shifted[:, span])
    counts_copy.wait()
    for rows, span in blocks:
        rate = held[rows, span] if rows.start < early else expected(load_ext[:, rows], shifted[:, span])
        resid = rate - counts_ref[rows, span].astype(F32)
        part = jnp.dot(load_ext[0:lats, rows], resid.astype(BF16), preferred_element_type=F32)
        grad_shift[:, span] = part if rows.start == 0 else grad_shift[:, span] + part

    bins = lax.broadcasted_iota(jnp.int32, (1, total), 1)
    tiles = []
    for j in range(total // LANES):
        span = slice(j * LANES, (j + 1) * LANES)
        tiles.append(jnp.where(bins[:, span] < length, grad_shift[:, span], 0.0))
    for j, tile in enumerate(shift_tiles(tiles, delay, False)):
        grad_shift[:, j * LANES : (j + 1) * LANES] = tile
    for k in range(parts):
        start = pl.multiple_of((me ^ k) * width, width)
        outs[k][...] = grad_shift[:, pl.ds(start, width)].astype(outs[k].dtype)


def load_kernel(lats, first, chunk, step, *refs):
    pack_ref, load_ext, shifted, counts_hbm = refs[:4]
    load_hbm, bias_hbm, counts_ref, held, load_ref, bias_ref, sems = refs[-7:]
    count, total = counts_ref.shape
    place = pl.ds(first, count)
    counts_copy = pltpu.make_async_copy(counts_hbm.at[place], counts_ref, sems.at[0])
    counts_copy.start()
    length = pack_ref[lats + 2 : lats + 3, 0:1].astype(jnp.int32)
    bins = lax.broadcasted_iota(jnp.int32, (1, total), 1)
    blocks = [(slice(begin, begin + chunk), range(0, total, step)) for begin in range(0, count, chunk)]
    for rows, starts in blocks:
        for at in starts:
            load_part = load_ext[:, first + rows.start : first + rows.stop]
            held[rows, at : at + step] = expected(load_part, shifted[:, at : at + step])
    counts_copy.wait()
    outward = []
    for index, (rows, starts) in enumerate(blocks):
        sums = jnp.zeros((chunk, LANES), F32)
        grad = jnp.zeros((chunk, lats), F32)
        for at in starts:
            span = slice(at, at + step)
            resid = jnp.where(bins[:, span] < length, held[rows, span] - counts_ref[rows, span].astype(F32), 0.0)
            for j in range(step // LANES):
                sums = sums + resid[:, j * LANES : (j + 1) * LANES]
            grad = grad + lax.dot_general(
                resid.astype(BF16), shifted[0:lats, span], (((1,), (1,)), ((), ())), preferred_element_type=F32
            )
        load_ref[:, rows] = grad.T
        bias_ref[:, rows] = jnp.sum(sums.T, axis=0, keepdims=True)
        place = pl.ds(first + rows.start, chunk)
        outward.append(pltpu.make_async_copy(load_ref.at[:, rows], load_hbm.at[:, place], sems.at[2 * index + 1]))
        outward.append(pltpu.make_async_copy(bias_ref.at[:, rows], bias_hbm.at[:, place], sems.at[2 * index + 2]))
        for copy in outward[-2:]:
            copy.start()
    for copy in outward:
        copy.wait()


def per_device(region_count, neuron_count, counts, latents, loadings, bias, delays, recorded):
    neurons, total = counts.shape[1:]
    lats, width = latents.shape
    chunk, step = 256, 512
    vmem = pl.BlockSpec(memory_space=pltpu.VMEM)
    hbm = pl.BlockSpec(memory_space=pltpu.HBM)
    params = pltpu.CompilerParams(vmem_limit_bytes=52 * 1024 * 1024)

    def swap(value, axis, count, mask):
        return lax.ppermute(value, axis, [(i, i ^ mask) for i in range(count)])

    order = sorted(range(1, neuron_count), key=lambda k: (k != 2, k))
    arrived = [swap(latents, "neuron", neuron_count, k) for k in order]
    row = lax.broadcasted_iota(jnp.int32, (lats + 8, neurons + width), 0)
    lines = jnp.pad(delays, ((lats + 1, 6), (0, neurons + width - lats)))
    lines = jnp.where(row == lats + 2, jnp.broadcast_to(recorded[:, None], lines.shape), lines)
    pack = jnp.pad(bias, ((lats, 7), (0, width))) + lines.astype(F32)
    pack = pack + jnp.pad(loadings[0], ((0, 8), (0, width))).astype(F32)
    pack = pack + jnp.pad(latents, ((0, 8), (neurons, 0))).astype(F32)

    *outs, load_ext, shifted = pl.pallas_call(
        functools.partial(shift_kernel, neuron_count, order, "neuron", chunk, step),
        out_shape=[jax.ShapeDtypeStruct((lats, width), BF16 if k > 1 else F32) for k in range(neuron_count)]
        + [jax.ShapeDtypeStruct((lats + EXTRA, neurons), BF16), jax.ShapeDtypeStruct((lats + EXTRA, total), BF16)],
        in_specs=[vmem, hbm] + [vmem] * (neuron_count - 1),
        out_specs=[vmem] * (neuron_count + 2),
        scratch_shapes=[
            pltpu.VMEM((lats, total), BF16),
            pltpu.VMEM((neurons, total), BF16),
            pltpu.VMEM((4 * chunk, total), F32),
            pltpu.VMEM((lats, total), F32),
            pltpu.SemaphoreType.DMA,
        ],
        compiler_params=params,
    )(pack, counts[0], *arrived)

    shares = [(0, 2 * chunk), (2 * chunk, neurons - 2 * chunk)]
    made = []

    def make(before):
        first, count = shares.pop(0)
        before, start_load = lax.optimization_barrier((before, load_ext))
        out = pl.pallas_call(
            functools.partial(load_kernel, lats, first, chunk, step),
            out_shape=[jax.ShapeDtypeStruct((lats, neurons), F32), jax.ShapeDtypeStruct((1, neurons), F32)],
            in_specs=[vmem, vmem, vmem, hbm] + [hbm] * len(made),
            out_specs=[hbm, hbm],
            scratch_shapes=[
                pltpu.VMEM((count, total), BF16),
                pltpu.VMEM((count, total), F32),
                pltpu.VMEM((lats, count), F32),
                pltpu.VMEM((1, count), F32),
                pltpu.SemaphoreType.DMA((1 + 2 * (count // chunk),)),
            ],
            input_output_aliases={4 + i: i for i in range(len(made))},
            compiler_params=params,
            cost_estimate=pl.CostEstimate(
                flops=4 * lats * count * total, bytes_accessed=2 * count * total, transcendentals=count * total
            ),
        )(pack, start_load, shifted, counts[0], *made)
        return before, out

    outs, made = make(outs)
    arrived = [swap(outs[k], "neuron", neuron_count, k) for k in [*range(2, neuron_count), 1]]
    arrived, made = lax.optimization_barrier((arrived, made))
    value = functools.reduce(jnp.add, [outs[0]] + [block.astype(F32) for block in arrived])
    mask = 1
    while mask < region_count:
        group = min(8, region_count // mask)
        if group > 2:
            value = lax.reduce_precision(value, 8, 7)
        sent = value.astype(BF16) if group > 2 else value
        if shares:
            (value, sent), made = make((value, sent))
        arrived = [swap(sent, "region", region_count, k * mask) for k in range(1, group)]
        arrived, made = lax.optimization_barrier((arrived, made))
        terms = [value] + [block.astype(F32) for block in arrived]
        while len(terms) > 1:
            terms = [terms[i] + terms[i + 1] for i in range(0, len(terms), 2)]
        value = terms[0]
        mask *= group
    grad_load, grad_bias = made
    return (value, grad_load[None], grad_bias)


def solution(mesh):
    placed = (
        P("region", "neuron", None),
        P(None, "neuron"),
        P("region", None, "neuron"),
        P("region", "neuron"),
        P("region", None),
        P("region"),
    )
    return jax.shard_map(
        functools.partial(per_device, mesh.shape["region"], mesh.shape["neuron"]),
        mesh=mesh,
        in_specs=placed,
        out_specs=(P(None, "neuron"), P("region", None, "neuron"), P("region", "neuron")),
        check_vma=False,
    )
```

```python
import functools

import jax
import jax.numpy as jnp
from jax import lax
from jax.experimental import pallas as pl
from jax.experimental.pallas import tpu as pltpu
from jax.sharding import PartitionSpec as P

LANES = 128
EXTRA = 16
F32 = jnp.float32
BF16 = jnp.bfloat16


def shift_tiles(tiles, delay, forward):
    lane = lax.broadcasted_iota(jnp.int32, delay.shape, 1)
    source = lane - delay if forward else lane + delay
    inside = source >= 0 if forward else source < LANES
    source = source & (LANES - 1)
    turned = [jnp.take_along_axis(tile, source, axis=1, mode="promise_in_bounds") for tile in tiles]
    nothing = [jnp.zeros_like(tiles[0])]
    others = nothing + turned[:-1] if forward else turned[1:] + nothing
    return [jnp.where(inside, tile, other) for tile, other in zip(turned, others)]


def expected(load_part, piece):
    eta = lax.dot_general(load_part, piece, (((0,), (0,)), ((), ())), preferred_element_type=F32)
    return jnp.exp(eta)


def shift_kernel(parts, order, axis, chunk, step, *refs):
    pack_ref, counts_hbm = refs[:2]
    arrived = refs[2 : 1 + parts]
    outs = refs[1 + parts : 1 + 2 * parts]
    load_ext, shifted, whole, counts_ref, held, grad_shift, counts_sem = refs[1 + 2 * parts :]
    me = lax.axis_index(axis)
    lats, total = grad_shift.shape
    early = held.shape[0]
    neurons = counts_ref.shape[0]
    width = total // parts
    counts_copy = pltpu.make_async_copy(counts_hbm, counts_ref, counts_sem)
    counts_copy.start()

    for k in range(parts):
        start = pl.multiple_of((me ^ k) * width, width)
        whole[:, pl.ds(start, width)] = arrived[order.index(k)][...] if k else pack_ref[0:lats, neurons:].astype(BF16)
    diagonal = lax.broadcasted_iota(jnp.int32, (lats, LANES), 0) == lax.broadcasted_iota(jnp.int32, (lats, LANES), 1)
    spread = jnp.broadcast_to(pack_ref[lats + 1 : lats + 2, 0:LANES], (lats, LANES))
    column = jnp.sum(jnp.where(diagonal, spread, 0.0), axis=1, keepdims=True)
    delay = jnp.broadcast_to(column, (lats, LANES)).astype(jnp.int32)
    length = pack_ref[lats + 2 : lats + 3, 0:1].astype(jnp.int32)
    tiles = [whole[:, j * LANES : (j + 1) * LANES].astype(F32) for j in range(total // LANES)]
    for j, tile in enumerate(shift_tiles(tiles, delay, True)):
        shifted[0:lats, j * LANES : (j + 1) * LANES] = tile.astype(BF16)
    row = lax.broadcasted_iota(jnp.int32, (EXTRA, total), 0)
    shifted[lats:, :] = jnp.where(row < 3, 1.0, 0.0).astype(BF16)

    load_ext[0:lats, :] = pack_ref[0:lats, 0:neurons].astype(BF16)
    bias = pack_ref[lats : lats + 1, 0:neurons]
    high = bias.astype(BF16).astype(F32)
    middle = (bias - high).astype(BF16).astype(F32)
    low = bias - high - middle
    row = lax.broadcasted_iota(jnp.int32, (EXTRA, neurons), 0)
    below = jnp.where(row == 0, high, jnp.where(row == 1, middle, jnp.where(row == 2, low, 0.0)))
    load_ext[lats:, :] = below.astype(BF16)

    blocks = [
        (slice(first, first + chunk), slice(begin, begin + step))
        for first in range(0, neurons, chunk)
        for begin in range(0, total, step)
    ]
    for rows, span in blocks:
        if rows.start < early:
            held[rows, span] = expected(load_ext[:, rows], shifted[:, span])
    counts_copy.wait()
    for rows, span in blocks:
        rate = held[rows, span] if rows.start < early else expected(load_ext[:, rows], shifted[:, span])
        resid = rate - counts_ref[rows, span].astype(F32)
        part = jnp.dot(load_ext[0:lats, rows], resid.astype(BF16), preferred_element_type=F32)
        grad_shift[:, span] = part if rows.start == 0 else grad_shift[:, span] + part

    bins = lax.broadcasted_iota(jnp.int32, (1, total), 1)
    tiles = []
    for j in range(total // LANES):
        span = slice(j * LANES, (j + 1) * LANES)
        tiles.append(jnp.where(bins[:, span] < length, grad_shift[:, span], 0.0))
    for j, tile in enumerate(shift_tiles(tiles, delay, False)):
        grad_shift[:, j * LANES : (j + 1) * LANES] = tile
    for k in range(parts):
        start = pl.multiple_of((me ^ k) * width, width)
        outs[k][...] = grad_shift[:, pl.ds(start, width)].astype(outs[k].dtype)


def load_kernel(lats, first, chunk, step, *refs):
    pack_ref, load_ext, shifted, counts_hbm = refs[:4]
    load_hbm, bias_hbm, counts_ref, held, load_ref, bias_ref, sems = refs[-7:]
    count, total = counts_ref.shape
    place = pl.ds(first, count)
    counts_copy = pltpu.make_async_copy(counts_hbm.at[place], counts_ref, sems.at[0])
    counts_copy.start()
    length = pack_ref[lats + 2 : lats + 3, 0:1].astype(jnp.int32)
    bins = lax.broadcasted_iota(jnp.int32, (1, total), 1)
    blocks = [(slice(begin, begin + chunk), range(0, total, step)) for begin in range(0, count, chunk)]
    for rows, starts in blocks:
        for at in starts:
            load_part = load_ext[:, first + rows.start : first + rows.stop]
            held[rows, at : at + step] = expected(load_part, shifted[:, at : at + step])
    counts_copy.wait()
    outward = []
    for index, (rows, starts) in enumerate(blocks):
        sums = jnp.zeros((chunk, LANES), F32)
        grad = jnp.zeros((chunk, lats), F32)
        for at in starts:
            span = slice(at, at + step)
            resid = jnp.where(bins[:, span] < length, held[rows, span] - counts_ref[rows, span].astype(F32), 0.0)
            for j in range(step // LANES):
                sums = sums + resid[:, j * LANES : (j + 1) * LANES]
            grad = grad + lax.dot_general(
                resid.astype(BF16), shifted[0:lats, span], (((1,), (1,)), ((), ())), preferred_element_type=F32
            )
        load_ref[:, rows] = grad.T
        bias_ref[:, rows] = jnp.sum(sums.T, axis=0, keepdims=True)
        place = pl.ds(first + rows.start, chunk)
        outward.append(pltpu.make_async_copy(load_ref.at[:, rows], load_hbm.at[:, place], sems.at[2 * index + 1]))
        outward.append(pltpu.make_async_copy(bias_ref.at[:, rows], bias_hbm.at[:, place], sems.at[2 * index + 2]))
        for copy in outward[-2:]:
            copy.start()
    for copy in outward:
        copy.wait()


def encode(value):
    top = jnp.maximum(jnp.max(jnp.abs(value), axis=0, keepdims=True), 2.0**-100)
    power = jnp.ceil(jnp.log2(top)) - 14.0
    rows = jnp.broadcast_to(power, (8, value.shape[1]))
    return jnp.concatenate([value * jnp.exp2(-power), rows], axis=0).astype(jnp.float16)


def decode(code):
    power = code[-8:-7].astype(F32)
    return code[:-8].astype(F32) * jnp.exp2(power)


def per_device(region_count, neuron_count, counts, latents, loadings, bias, delays, recorded):
    neurons, total = counts.shape[1:]
    lats, width = latents.shape
    chunk, step = 256, 512
    vmem = pl.BlockSpec(memory_space=pltpu.VMEM)
    hbm = pl.BlockSpec(memory_space=pltpu.HBM)
    params = pltpu.CompilerParams(vmem_limit_bytes=52 * 1024 * 1024)

    def swap(value, axis, count, mask):
        return lax.ppermute(value, axis, [(i, i ^ mask) for i in range(count)])

    order = sorted(range(1, neuron_count), key=lambda k: (k != 2, k))
    arrived = [swap(latents, "neuron", neuron_count, k) for k in order]
    row = lax.broadcasted_iota(jnp.int32, (lats + 8, neurons + width), 0)
    lines = jnp.pad(delays, ((lats + 1, 6), (0, neurons + width - lats)))
    lines = jnp.where(row == lats + 2, jnp.broadcast_to(recorded[:, None], lines.shape), lines)
    pack = jnp.pad(bias, ((lats, 7), (0, width))) + lines.astype(F32)
    pack = pack + jnp.pad(loadings[0], ((0, 8), (0, width))).astype(F32)
    pack = pack + jnp.pad(latents, ((0, 8), (neurons, 0))).astype(F32)

    *outs, load_ext, shifted = pl.pallas_call(
        functools.partial(shift_kernel, neuron_count, order, "neuron", chunk, step),
        out_shape=[jax.ShapeDtypeStruct((lats, width), BF16 if k > 1 else F32) for k in range(neuron_count)]
        + [jax.ShapeDtypeStruct((lats + EXTRA, neurons), BF16), jax.ShapeDtypeStruct((lats + EXTRA, total), BF16)],
        in_specs=[vmem, hbm] + [vmem] * (neuron_count - 1),
        out_specs=[vmem] * (neuron_count + 2),
        scratch_shapes=[
            pltpu.VMEM((lats, total), BF16),
            pltpu.VMEM((neurons, total), BF16),
            pltpu.VMEM((4 * chunk, total), F32),
            pltpu.VMEM((lats, total), F32),
            pltpu.SemaphoreType.DMA,
        ],
        compiler_params=params,
    )(pack, counts[0], *arrived)

    shares = [(0, 2 * chunk), (2 * chunk, 2 * chunk), (4 * chunk, neurons - 4 * chunk)]
    made = []

    def make(before):
        first, count = shares.pop(0)
        before, start_load = lax.optimization_barrier((before, load_ext))
        out = pl.pallas_call(
            functools.partial(load_kernel, lats, first, chunk, step),
            out_shape=[jax.ShapeDtypeStruct((lats, neurons), F32), jax.ShapeDtypeStruct((1, neurons), F32)],
            in_specs=[vmem, vmem, vmem, hbm] + [hbm] * len(made),
            out_specs=[hbm, hbm],
            scratch_shapes=[
                pltpu.VMEM((count, total), BF16),
                pltpu.VMEM((count, total), F32),
                pltpu.VMEM((lats, count), F32),
                pltpu.VMEM((1, count), F32),
                pltpu.SemaphoreType.DMA((1 + 2 * (count // chunk),)),
            ],
            input_output_aliases={4 + i: i for i in range(len(made))},
            compiler_params=params,
            cost_estimate=pl.CostEstimate(
                flops=4 * lats * count * total, bytes_accessed=2 * count * total, transcendentals=count * total
            ),
        )(pack, start_load, shifted, counts[0], *made)
        return before, out

    outs, made = make(outs)
    arrived = [swap(outs[k], "neuron", neuron_count, k) for k in [*range(2, neuron_count), 1]]
    arrived, made = lax.optimization_barrier((arrived, made))
    value = functools.reduce(jnp.add, [outs[0]] + [block.astype(F32) for block in arrived])
    mask = 1
    while mask < region_count:
        masks = [mask, 2 * mask, 3 * mask] if 2 * mask < region_count else [mask]
        code = lax.optimization_barrier(encode(value))
        if shares:
            code, made = make(code)
        arrived = [swap(code, "region", region_count, k) for k in masks]
        arrived, made = lax.optimization_barrier((arrived, made))
        value = decode(code) + decode(arrived[0])
        if len(masks) == 3:
            value = value + (decode(arrived[1]) + decode(arrived[2]))
        mask *= 1 + len(masks)
    grad_load, grad_bias = made
    return (value, grad_load[None], grad_bias)


def solution(mesh):
    placed = (
        P("region", "neuron", None),
        P(None, "neuron"),
        P("region", None, "neuron"),
        P("region", "neuron"),
        P("region", None),
        P("region"),
    )
    return jax.shard_map(
        functools.partial(per_device, mesh.shape["region"], mesh.shape["neuron"]),
        mesh=mesh,
        in_specs=placed,
        out_specs=(P(None, "neuron"), P("region", None, "neuron"), P("region", "neuron")),
        check_vma=False,
    )
```

```python
import functools

import jax
import jax.numpy as jnp
from jax import lax
from jax.experimental import pallas as pl
from jax.experimental.pallas import tpu as pltpu
from jax.sharding import PartitionSpec as P

LANES = 128
EXTRA = 16
F32 = jnp.float32
BF16 = jnp.bfloat16


def shift_tiles(tiles, delay, forward):
    lane = lax.broadcasted_iota(jnp.int32, delay.shape, 1)
    source = lane - delay if forward else lane + delay
    inside = source >= 0 if forward else source < LANES
    source = source & (LANES - 1)
    turned = [jnp.take_along_axis(tile, source, axis=1, mode="promise_in_bounds") for tile in tiles]
    nothing = [jnp.zeros_like(tiles[0])]
    others = nothing + turned[:-1] if forward else turned[1:] + nothing
    return [jnp.where(inside, tile, other) for tile, other in zip(turned, others)]


def expected(load_part, piece):
    eta = lax.dot_general(load_part, piece, (((0,), (0,)), ((), ())), preferred_element_type=F32)
    return jnp.exp(eta)


def shift_kernel(parts, order, axis, chunk, step, *refs):
    pack_ref, counts_hbm = refs[:2]
    arrived = refs[2 : 1 + parts]
    outs = refs[1 + parts : 1 + 2 * parts]
    load_ext, shifted, whole, counts_ref, held, resid_low, grad_shift, counts_sem = refs[1 + 2 * parts :]
    me = lax.axis_index(axis)
    lats, total = grad_shift.shape
    early = held.shape[0]
    neurons = counts_ref.shape[0]
    width = total // parts
    counts_copy = pltpu.make_async_copy(counts_hbm, counts_ref, counts_sem)
    counts_copy.start()

    for k in range(parts):
        start = pl.multiple_of((me ^ k) * width, width)
        whole[:, pl.ds(start, width)] = arrived[order.index(k)][...] if k else pack_ref[0:lats, neurons:].astype(BF16)
    diagonal = lax.broadcasted_iota(jnp.int32, (lats, LANES), 0) == lax.broadcasted_iota(jnp.int32, (lats, LANES), 1)
    spread = jnp.broadcast_to(pack_ref[lats + 1 : lats + 2, 0:LANES], (lats, LANES))
    column = jnp.sum(jnp.where(diagonal, spread, 0.0), axis=1, keepdims=True)
    delay = jnp.broadcast_to(column, (lats, LANES)).astype(jnp.int32)
    length = pack_ref[lats + 2 : lats + 3, 0:1].astype(jnp.int32)
    tiles = [whole[:, j * LANES : (j + 1) * LANES].astype(F32) for j in range(total // LANES)]
    for j, tile in enumerate(shift_tiles(tiles, delay, True)):
        shifted[0:lats, j * LANES : (j + 1) * LANES] = tile.astype(BF16)
    row = lax.broadcasted_iota(jnp.int32, (EXTRA, total), 0)
    shifted[lats:, :] = jnp.where(row < 3, 1.0, 0.0).astype(BF16)

    load_ext[0:lats, :] = pack_ref[0:lats, 0:neurons].astype(BF16)
    bias = pack_ref[lats : lats + 1, 0:neurons]
    high = bias.astype(BF16).astype(F32)
    middle = (bias - high).astype(BF16).astype(F32)
    low = bias - high - middle
    row = lax.broadcasted_iota(jnp.int32, (EXTRA, neurons), 0)
    below = jnp.where(row == 0, high, jnp.where(row == 1, middle, jnp.where(row == 2, low, 0.0)))
    load_ext[lats:, :] = below.astype(BF16)

    blocks = [
        (slice(first, first + chunk), slice(begin, begin + step))
        for first in range(0, neurons, chunk)
        for begin in range(0, total, step)
    ]
    for rows, span in blocks:
        if rows.start < early:
            held[rows, span] = expected(load_ext[:, rows], shifted[:, span])
    counts_copy.wait()
    for rows, span in blocks:
        rate = held[rows, span] if rows.start < early else expected(load_ext[:, rows], shifted[:, span])
        resid_low[rows, span] = (rate - counts_ref[rows, span].astype(F32)).astype(BF16)
    for begin in range(0, total, step):
        span = slice(begin, begin + step)
        grad_shift[:, span] = jnp.dot(load_ext[0:lats, :], resid_low[:, span], preferred_element_type=F32)

    bins = lax.broadcasted_iota(jnp.int32, (1, total), 1)
    tiles = []
    for j in range(total // LANES):
        span = slice(j * LANES, (j + 1) * LANES)
        tiles.append(jnp.where(bins[:, span] < length, grad_shift[:, span], 0.0))
    for j, tile in enumerate(shift_tiles(tiles, delay, False)):
        grad_shift[:, j * LANES : (j + 1) * LANES] = tile
    for k in range(parts):
        start = pl.multiple_of((me ^ k) * width, width)
        outs[k][...] = grad_shift[:, pl.ds(start, width)].astype(outs[k].dtype)


def load_kernel(lats, first, chunk, step, *refs):
    pack_ref, load_ext, shifted, counts_hbm = refs[:4]
    load_hbm, bias_hbm, counts_ref, held, load_ref, bias_ref, sems = refs[-7:]
    count, total = counts_ref.shape
    place = pl.ds(first, count)
    counts_copy = pltpu.make_async_copy(counts_hbm.at[place], counts_ref, sems.at[0])
    counts_copy.start()
    length = pack_ref[lats + 2 : lats + 3, 0:1].astype(jnp.int32)
    bins = lax.broadcasted_iota(jnp.int32, (1, total), 1)
    blocks = [(slice(begin, begin + chunk), range(0, total, step)) for begin in range(0, count, chunk)]
    for rows, starts in blocks:
        for at in starts:
            load_part = load_ext[:, first + rows.start : first + rows.stop]
            held[rows, at : at + step] = expected(load_part, shifted[:, at : at + step])
    counts_copy.wait()
    outward = []
    for index, (rows, starts) in enumerate(blocks):
        sums = jnp.zeros((chunk, LANES), F32)
        grad = jnp.zeros((chunk, lats), F32)
        for at in starts:
            span = slice(at, at + step)
            resid = jnp.where(bins[:, span] < length, held[rows, span] - counts_ref[rows, span].astype(F32), 0.0)
            for j in range(step // LANES):
                sums = sums + resid[:, j * LANES : (j + 1) * LANES]
            grad = grad + lax.dot_general(
                resid.astype(BF16), shifted[0:lats, span], (((1,), (1,)), ((), ())), preferred_element_type=F32
            )
        load_ref[:, rows] = grad.T
        bias_ref[:, rows] = jnp.sum(sums.T, axis=0, keepdims=True)
        place = pl.ds(first + rows.start, chunk)
        outward.append(pltpu.make_async_copy(load_ref.at[:, rows], load_hbm.at[:, place], sems.at[2 * index + 1]))
        outward.append(pltpu.make_async_copy(bias_ref.at[:, rows], bias_hbm.at[:, place], sems.at[2 * index + 2]))
        for copy in outward[-2:]:
            copy.start()
    for copy in outward:
        copy.wait()


def encode(value):
    top = jnp.maximum(jnp.max(jnp.abs(value), axis=0, keepdims=True), 2.0**-100)
    power = jnp.ceil(jnp.log2(top)) - 14.0
    rows = jnp.broadcast_to(power, (8, value.shape[1]))
    return jnp.concatenate([value * jnp.exp2(-power), rows], axis=0).astype(jnp.float16)


def decode(code):
    power = code[-8:-7].astype(F32)
    return code[:-8].astype(F32) * jnp.exp2(power)


def per_device(region_count, neuron_count, counts, latents, loadings, bias, delays, recorded):
    neurons, total = counts.shape[1:]
    lats, width = latents.shape
    chunk, step = 256, 512
    vmem = pl.BlockSpec(memory_space=pltpu.VMEM)
    hbm = pl.BlockSpec(memory_space=pltpu.HBM)
    params = pltpu.CompilerParams(vmem_limit_bytes=52 * 1024 * 1024)

    def swap(value, axis, count, mask):
        return lax.ppermute(value, axis, [(i, i ^ mask) for i in range(count)])

    order = sorted(range(1, neuron_count), key=lambda k: (k != 2, k))
    arrived = [swap(latents, "neuron", neuron_count, k) for k in order]
    row = lax.broadcasted_iota(jnp.int32, (lats + 8, neurons + width), 0)
    lines = jnp.pad(delays, ((lats + 1, 6), (0, neurons + width - lats)))
    lines = jnp.where(row == lats + 2, jnp.broadcast_to(recorded[:, None], lines.shape), lines)
    pack = jnp.pad(bias, ((lats, 7), (0, width))) + lines.astype(F32)
    pack = pack + jnp.pad(loadings[0], ((0, 8), (0, width))).astype(F32)
    pack = pack + jnp.pad(latents, ((0, 8), (neurons, 0))).astype(F32)

    *outs, load_ext, shifted = pl.pallas_call(
        functools.partial(shift_kernel, neuron_count, order, "neuron", chunk, step),
        out_shape=[jax.ShapeDtypeStruct((lats, width), BF16 if k > 1 else F32) for k in range(neuron_count)]
        + [jax.ShapeDtypeStruct((lats + EXTRA, neurons), BF16), jax.ShapeDtypeStruct((lats + EXTRA, total), BF16)],
        in_specs=[vmem, hbm] + [vmem] * (neuron_count - 1),
        out_specs=[vmem] * (neuron_count + 2),
        scratch_shapes=[
            pltpu.VMEM((lats, total), BF16),
            pltpu.VMEM((neurons, total), BF16),
            pltpu.VMEM((4 * chunk, total), F32),
            pltpu.VMEM((neurons, total), BF16),
            pltpu.VMEM((lats, total), F32),
            pltpu.SemaphoreType.DMA,
        ],
        compiler_params=params,
    )(pack, counts[0], *arrived)

    shares = [(0, 2 * chunk), (2 * chunk, neurons - 2 * chunk)]
    made = []

    def make(before):
        first, count = shares.pop(0)
        before, start_load = lax.optimization_barrier((before, load_ext))
        out = pl.pallas_call(
            functools.partial(load_kernel, lats, first, chunk, step),
            out_shape=[jax.ShapeDtypeStruct((lats, neurons), F32), jax.ShapeDtypeStruct((1, neurons), F32)],
            in_specs=[vmem, vmem, vmem, hbm] + [hbm] * len(made),
            out_specs=[hbm, hbm],
            scratch_shapes=[
                pltpu.VMEM((count, total), BF16),
                pltpu.VMEM((count, total), F32),
                pltpu.VMEM((lats, count), F32),
                pltpu.VMEM((1, count), F32),
                pltpu.SemaphoreType.DMA((1 + 2 * (count // chunk),)),
            ],
            input_output_aliases={4 + i: i for i in range(len(made))},
            compiler_params=params,
            cost_estimate=pl.CostEstimate(
                flops=4 * lats * count * total, bytes_accessed=2 * count * total, transcendentals=count * total
            ),
        )(pack, start_load, shifted, counts[0], *made)
        return before, out

    outs, made = make(outs)
    arrived = [swap(outs[k], "neuron", neuron_count, k) for k in [*range(2, neuron_count), 1]]
    arrived, made = lax.optimization_barrier((arrived, made))
    value = functools.reduce(jnp.add, [outs[0]] + [block.astype(F32) for block in arrived])
    mask = 1
    while mask < region_count:
        masks = [mask, 2 * mask, 3 * mask] if 2 * mask < region_count else [mask]
        code = lax.optimization_barrier(encode(value))
        if shares:
            code, made = make(code)
        arrived = [swap(code, "region", region_count, k) for k in masks]
        arrived, made = lax.optimization_barrier((arrived, made))
        value = decode(code) + decode(arrived[0])
        if len(masks) == 3:
            value = value + (decode(arrived[1]) + decode(arrived[2]))
        mask *= 1 + len(masks)
    grad_load, grad_bias = made
    return (value, grad_load[None], grad_bias)


def solution(mesh):
    placed = (
        P("region", "neuron", None),
        P(None, "neuron"),
        P("region", None, "neuron"),
        P("region", "neuron"),
        P("region", None),
        P("region"),
    )
    return jax.shard_map(
        functools.partial(per_device, mesh.shape["region"], mesh.shape["neuron"]),
        mesh=mesh,
        in_specs=placed,
        out_specs=(P(None, "neuron"), P("region", None, "neuron"), P("region", "neuron")),
        check_vma=False,
    )
```

```python
import functools

import jax
import jax.numpy as jnp
from jax import lax
from jax.experimental import pallas as pl
from jax.experimental.pallas import tpu as pltpu
from jax.sharding import PartitionSpec as P

LANES = 128
EXTRA = 16
F32 = jnp.float32
BF16 = jnp.bfloat16


def shift_tiles(tiles, delay, forward):
    lane = lax.broadcasted_iota(jnp.int32, delay.shape, 1)
    source = lane - delay if forward else lane + delay
    inside = source >= 0 if forward else source < LANES
    source = source & (LANES - 1)
    turned = [jnp.take_along_axis(tile, source, axis=1, mode="promise_in_bounds") for tile in tiles]
    nothing = [jnp.zeros_like(tiles[0])]
    others = nothing + turned[:-1] if forward else turned[1:] + nothing
    return [jnp.where(inside, tile, other) for tile, other in zip(turned, others)]


def expected(load_part, piece):
    return jnp.exp(jnp.dot(load_part, piece, preferred_element_type=F32))


def shift_kernel(parts, order, axis, chunk, step, *refs):
    pack_ref, counts_hbm = refs[:2]
    arrived = refs[2 : 1 + parts]
    outs = refs[1 + parts : 1 + 2 * parts]
    turned, shifted, whole, counts_ref, held, resid_low, load_ext, grad_shift, counts_sem = refs[1 + 2 * parts :]
    me = lax.axis_index(axis)
    lats, total = grad_shift.shape
    early = held.shape[0]
    neurons = counts_ref.shape[0]
    width = total // parts
    counts_copy = pltpu.make_async_copy(counts_hbm, counts_ref, counts_sem)
    counts_copy.start()

    for k in range(parts):
        start = pl.multiple_of((me ^ k) * width, width)
        whole[:, pl.ds(start, width)] = arrived[order.index(k)][...] if k else pack_ref[0:lats, neurons:].astype(BF16)
    diagonal = lax.broadcasted_iota(jnp.int32, (lats, LANES), 0) == lax.broadcasted_iota(jnp.int32, (lats, LANES), 1)
    spread = jnp.broadcast_to(pack_ref[lats + 1 : lats + 2, 0:LANES], (lats, LANES))
    column = jnp.sum(jnp.where(diagonal, spread, 0.0), axis=1, keepdims=True)
    delay = jnp.broadcast_to(column, (lats, LANES)).astype(jnp.int32)
    length = pack_ref[lats + 2 : lats + 3, 0:1].astype(jnp.int32)
    tiles = [whole[:, j * LANES : (j + 1) * LANES].astype(F32) for j in range(total // LANES)]
    for j, tile in enumerate(shift_tiles(tiles, delay, True)):
        shifted[0:lats, j * LANES : (j + 1) * LANES] = tile.astype(BF16)
    row = lax.broadcasted_iota(jnp.int32, (EXTRA, total), 0)
    shifted[lats:, :] = jnp.where(row < 3, 1.0, 0.0).astype(BF16)

    load_ext[0:lats, :] = pack_ref[0:lats, 0:neurons].astype(BF16)
    bias = pack_ref[lats : lats + 1, 0:neurons]
    high = bias.astype(BF16).astype(F32)
    middle = (bias - high).astype(BF16).astype(F32)
    low = bias - high - middle
    row = lax.broadcasted_iota(jnp.int32, (EXTRA, neurons), 0)
    below = jnp.where(row == 0, high, jnp.where(row == 1, middle, jnp.where(row == 2, low, 0.0)))
    load_ext[lats:, :] = below.astype(BF16)
    turned[...] = load_ext[...].astype(F32).T.astype(BF16)

    blocks = [
        (slice(first, first + chunk), slice(begin, begin + step))
        for first in range(0, neurons, chunk)
        for begin in range(0, total, step)
    ]
    for rows, span in blocks:
        if rows.start < early:
            held[rows, span] = expected(turned[rows, :], shifted[:, span])
    counts_copy.wait()
    for rows, span in blocks:
        rate = held[rows, span] if rows.start < early else expected(turned[rows, :], shifted[:, span])
        resid_low[rows, span] = (rate - counts_ref[rows, span].astype(F32)).astype(BF16)
    for begin in range(0, total, step):
        span = slice(begin, begin + step)
        grad_shift[:, span] = jnp.dot(load_ext[0:lats, :], resid_low[:, span], preferred_element_type=F32)

    bins = lax.broadcasted_iota(jnp.int32, (1, total), 1)
    tiles = []
    for j in range(total // LANES):
        span = slice(j * LANES, (j + 1) * LANES)
        tiles.append(jnp.where(bins[:, span] < length, grad_shift[:, span], 0.0))
    for j, tile in enumerate(shift_tiles(tiles, delay, False)):
        grad_shift[:, j * LANES : (j + 1) * LANES] = tile
    for k in range(parts):
        start = pl.multiple_of((me ^ k) * width, width)
        outs[k][...] = grad_shift[:, pl.ds(start, width)].astype(outs[k].dtype)


def load_kernel(lats, first, chunk, step, *refs):
    pack_ref, turned, shifted, counts_hbm = refs[:4]
    load_hbm, bias_hbm, counts_ref, held, load_ref, bias_ref, sems = refs[-7:]
    count, total = counts_ref.shape
    place = pl.ds(first, count)
    counts_copy = pltpu.make_async_copy(counts_hbm.at[place], counts_ref, sems.at[0])
    counts_copy.start()
    length = pack_ref[lats + 2 : lats + 3, 0:1].astype(jnp.int32)
    bins = lax.broadcasted_iota(jnp.int32, (1, total), 1)
    blocks = [(slice(begin, begin + chunk), range(0, total, step)) for begin in range(0, count, chunk)]
    for rows, starts in blocks:
        for at in starts:
            load_part = turned[first + rows.start : first + rows.stop, :]
            held[rows, at : at + step] = expected(load_part, shifted[:, at : at + step])
    columns = shifted[0:lats, :].astype(F32).T.astype(BF16)
    counts_copy.wait()
    outward = []
    for index, (rows, starts) in enumerate(blocks):
        sums = jnp.zeros((chunk, LANES), F32)
        grad = jnp.zeros((chunk, lats), F32)
        for at in starts:
            span = slice(at, at + step)
            resid = jnp.where(bins[:, span] < length, held[rows, span] - counts_ref[rows, span].astype(F32), 0.0)
            for j in range(step // LANES):
                sums = sums + resid[:, j * LANES : (j + 1) * LANES]
            grad = grad + jnp.dot(resid.astype(BF16), columns[span], preferred_element_type=F32)
        load_ref[:, rows] = grad.T
        bias_ref[:, rows] = jnp.sum(sums.T, axis=0, keepdims=True)
        place = pl.ds(first + rows.start, chunk)
        outward.append(pltpu.make_async_copy(load_ref.at[:, rows], load_hbm.at[:, place], sems.at[2 * index + 1]))
        outward.append(pltpu.make_async_copy(bias_ref.at[:, rows], bias_hbm.at[:, place], sems.at[2 * index + 2]))
        for copy in outward[-2:]:
            copy.start()
    for copy in outward:
        copy.wait()


def encode(value):
    top = jnp.maximum(jnp.max(jnp.abs(value), axis=0, keepdims=True), 2.0**-100)
    power = jnp.ceil(jnp.log2(top)) - 14.0
    rows = jnp.broadcast_to(power, (8, value.shape[1]))
    return jnp.concatenate([value * jnp.exp2(-power), rows], axis=0).astype(jnp.float16)


def decode(code):
    power = code[-8:-7].astype(F32)
    return code[:-8].astype(F32) * jnp.exp2(power)


def per_device(region_count, neuron_count, counts, latents, loadings, bias, delays, recorded):
    neurons, total = counts.shape[1:]
    lats, width = latents.shape
    chunk, step = 256, 512
    vmem = pl.BlockSpec(memory_space=pltpu.VMEM)
    hbm = pl.BlockSpec(memory_space=pltpu.HBM)
    params = pltpu.CompilerParams(vmem_limit_bytes=52 * 1024 * 1024)

    def swap(value, axis, count, mask):
        return lax.ppermute(value, axis, [(i, i ^ mask) for i in range(count)])

    order = sorted(range(1, neuron_count), key=lambda k: (k != 2, k))
    arrived = [swap(latents, "neuron", neuron_count, k) for k in order]
    row = lax.broadcasted_iota(jnp.int32, (lats + 8, neurons + width), 0)
    lines = jnp.pad(delays, ((lats + 1, 6), (0, neurons + width - lats)))
    lines = jnp.where(row == lats + 2, jnp.broadcast_to(recorded[:, None], lines.shape), lines)
    pack = jnp.pad(bias, ((lats, 7), (0, width))) + lines.astype(F32)
    pack = pack + jnp.pad(loadings[0], ((0, 8), (0, width))).astype(F32)
    pack = pack + jnp.pad(latents, ((0, 8), (neurons, 0))).astype(F32)

    *outs, turned, shifted = pl.pallas_call(
        functools.partial(shift_kernel, neuron_count, order, "neuron", chunk, step),
        out_shape=[jax.ShapeDtypeStruct((lats, width), BF16 if k > 1 else F32) for k in range(neuron_count)]
        + [jax.ShapeDtypeStruct((neurons, lats + EXTRA), BF16), jax.ShapeDtypeStruct((lats + EXTRA, total), BF16)],
        in_specs=[vmem, hbm] + [vmem] * (neuron_count - 1),
        out_specs=[vmem] * (neuron_count + 2),
        scratch_shapes=[
            pltpu.VMEM((lats, total), BF16),
            pltpu.VMEM((neurons, total), BF16),
            pltpu.VMEM((4 * chunk, total), F32),
            pltpu.VMEM((neurons, total), BF16),
            pltpu.VMEM((lats + EXTRA, neurons), BF16),
            pltpu.VMEM((lats, total), F32),
            pltpu.SemaphoreType.DMA,
        ],
        compiler_params=params,
    )(pack, counts[0], *arrived)

    shares = [(0, 2 * chunk), (2 * chunk, neurons - 2 * chunk)]
    made = []

    def make(before):
        first, count = shares.pop(0)
        before, start_load = lax.optimization_barrier((before, turned))
        out = pl.pallas_call(
            functools.partial(load_kernel, lats, first, chunk, step),
            out_shape=[jax.ShapeDtypeStruct((lats, neurons), F32), jax.ShapeDtypeStruct((1, neurons), F32)],
            in_specs=[vmem, vmem, vmem, hbm] + [hbm] * len(made),
            out_specs=[hbm, hbm],
            scratch_shapes=[
                pltpu.VMEM((count, total), BF16),
                pltpu.VMEM((count, total), F32),
                pltpu.VMEM((lats, count), F32),
                pltpu.VMEM((1, count), F32),
                pltpu.SemaphoreType.DMA((1 + 2 * (count // chunk),)),
            ],
            input_output_aliases={4 + i: i for i in range(len(made))},
            compiler_params=params,
            cost_estimate=pl.CostEstimate(
                flops=4 * lats * count * total, bytes_accessed=2 * count * total, transcendentals=count * total
            ),
        )(pack, start_load, shifted, counts[0], *made)
        return before, out

    outs, made = make(outs)
    arrived = [swap(outs[k], "neuron", neuron_count, k) for k in [*range(2, neuron_count), 1]]
    arrived, made = lax.optimization_barrier((arrived, made))
    value = functools.reduce(jnp.add, [outs[0]] + [block.astype(F32) for block in arrived])
    mask = 1
    while mask < region_count:
        masks = [mask, 2 * mask, 3 * mask] if 2 * mask < region_count else [mask]
        code = lax.optimization_barrier(encode(value))
        if shares:
            code, made = make(code)
        arrived = [swap(code, "region", region_count, k) for k in masks]
        arrived, made = lax.optimization_barrier((arrived, made))
        value = decode(code) + decode(arrived[0])
        if len(masks) == 3:
            value = value + (decode(arrived[1]) + decode(arrived[2]))
        mask *= 1 + len(masks)
    grad_load, grad_bias = made
    return (value, grad_load[None], grad_bias)


def solution(mesh):
    placed = (
        P("region", "neuron", None),
        P(None, "neuron"),
        P("region", None, "neuron"),
        P("region", "neuron"),
        P("region", None),
        P("region"),
    )
    return jax.shard_map(
        functools.partial(per_device, mesh.shape["region"], mesh.shape["neuron"]),
        mesh=mesh,
        in_specs=placed,
        out_specs=(P(None, "neuron"), P("region", None, "neuron"), P("region", "neuron")),
        check_vma=False,
    )
```

```python
import functools

import jax
import jax.numpy as jnp
from jax import lax
from jax.experimental import pallas as pl
from jax.experimental.pallas import tpu as pltpu
from jax.sharding import PartitionSpec as P

LANES = 128
EXTRA = 16
F32 = jnp.float32
BF16 = jnp.bfloat16


def shift_tiles(tiles, delay, forward):
    lane = lax.broadcasted_iota(jnp.int32, delay.shape, 1)
    source = lane - delay if forward else lane + delay
    inside = source >= 0 if forward else source < LANES
    source = source & (LANES - 1)
    turned = [jnp.take_along_axis(tile, source, axis=1, mode="promise_in_bounds") for tile in tiles]
    nothing = [jnp.zeros_like(tiles[0])]
    others = nothing + turned[:-1] if forward else turned[1:] + nothing
    return [jnp.where(inside, tile, other) for tile, other in zip(turned, others)]


def expected(load_part, piece):
    return jnp.exp(jnp.dot(load_part, piece, preferred_element_type=F32))


def fetch(counts_hbm, counts_ref, first, chunk, sems):
    copies = []
    for index in range(counts_ref.shape[0] // chunk):
        source = counts_hbm.at[pl.ds(first + index * chunk, chunk)]
        copies.append(pltpu.make_async_copy(source, counts_ref.at[pl.ds(index * chunk, chunk)], sems.at[index]))
        copies[-1].start()
    return copies


def shift_kernel(parts, order, axis, chunk, step, *refs):
    pack_ref, counts_hbm = refs[:2]
    arrived = refs[2 : 1 + parts]
    outs = refs[1 + parts : 1 + 2 * parts]
    turned, shifted, whole, counts_ref, held, resid_low, load_ext, grad_shift, counts_sems = refs[1 + 2 * parts :]
    me = lax.axis_index(axis)
    lats, total = grad_shift.shape
    early = held.shape[0]
    neurons = counts_ref.shape[0]
    width = total // parts
    copies = fetch(counts_hbm, counts_ref, 0, chunk, counts_sems)

    for k in range(parts):
        start = pl.multiple_of((me ^ k) * width, width)
        whole[:, pl.ds(start, width)] = arrived[order.index(k)][...] if k else pack_ref[0:lats, neurons:].astype(BF16)
    diagonal = lax.broadcasted_iota(jnp.int32, (lats, LANES), 0) == lax.broadcasted_iota(jnp.int32, (lats, LANES), 1)
    spread = jnp.broadcast_to(pack_ref[lats + 1 : lats + 2, 0:LANES], (lats, LANES))
    column = jnp.sum(jnp.where(diagonal, spread, 0.0), axis=1, keepdims=True)
    delay = jnp.broadcast_to(column, (lats, LANES)).astype(jnp.int32)
    length = pack_ref[lats + 2 : lats + 3, 0:1].astype(jnp.int32)
    tiles = [whole[:, j * LANES : (j + 1) * LANES].astype(F32) for j in range(total // LANES)]
    for j, tile in enumerate(shift_tiles(tiles, delay, True)):
        shifted[0:lats, j * LANES : (j + 1) * LANES] = tile.astype(BF16)
    row = lax.broadcasted_iota(jnp.int32, (EXTRA, total), 0)
    shifted[lats:, :] = jnp.where(row < 3, 1.0, 0.0).astype(BF16)

    load_ext[0:lats, :] = pack_ref[0:lats, 0:neurons].astype(BF16)
    bias = pack_ref[lats : lats + 1, 0:neurons]
    high = bias.astype(BF16).astype(F32)
    middle = (bias - high).astype(BF16).astype(F32)
    low = bias - high - middle
    row = lax.broadcasted_iota(jnp.int32, (EXTRA, neurons), 0)
    below = jnp.where(row == 0, high, jnp.where(row == 1, middle, jnp.where(row == 2, low, 0.0)))
    load_ext[lats:, :] = below.astype(BF16)
    turned[...] = load_ext[...].astype(F32).T.astype(BF16)

    blocks = [
        (slice(first, first + chunk), slice(begin, begin + step))
        for first in range(0, neurons, chunk)
        for begin in range(0, total, step)
    ]
    for rows, span in blocks:
        if rows.start < early:
            held[rows, span] = expected(turned[rows, :], shifted[:, span])
    for copy in copies:
        copy.wait()
    for rows, span in blocks:
        rate = held[rows, span] if rows.start < early else expected(turned[rows, :], shifted[:, span])
        resid_low[rows, span] = (rate - counts_ref[rows, span].astype(F32)).astype(BF16)
    for begin in range(0, total, step):
        span = slice(begin, begin + step)
        grad_shift[:, span] = jnp.dot(load_ext[0:lats, :], resid_low[:, span], preferred_element_type=F32)

    bins = lax.broadcasted_iota(jnp.int32, (1, total), 1)
    tiles = []
    for j in range(total // LANES):
        span = slice(j * LANES, (j + 1) * LANES)
        tiles.append(jnp.where(bins[:, span] < length, grad_shift[:, span], 0.0))
    for j, tile in enumerate(shift_tiles(tiles, delay, False)):
        grad_shift[:, j * LANES : (j + 1) * LANES] = tile
    for k in range(parts):
        start = pl.multiple_of((me ^ k) * width, width)
        outs[k][...] = grad_shift[:, pl.ds(start, width)].astype(outs[k].dtype)


def load_kernel(lats, first, chunk, step, *refs):
    pack_ref, turned, shifted, counts_hbm = refs[:4]
    load_hbm, bias_hbm, counts_ref, held, load_ref, bias_ref, counts_sems, sems = refs[-8:]
    count, total = counts_ref.shape
    copies = fetch(counts_hbm, counts_ref, first, chunk, counts_sems)
    length = pack_ref[lats + 2 : lats + 3, 0:1].astype(jnp.int32)
    bins = lax.broadcasted_iota(jnp.int32, (1, total), 1)
    blocks = [(slice(begin, begin + chunk), range(0, total, step)) for begin in range(0, count, chunk)]
    for rows, starts in blocks:
        for at in starts:
            load_part = turned[first + rows.start : first + rows.stop, :]
            held[rows, at : at + step] = expected(load_part, shifted[:, at : at + step])
    for copy in copies:
        copy.wait()
    outward = []
    for index, (rows, starts) in enumerate(blocks):
        sums = jnp.zeros((chunk, LANES), F32)
        grad = jnp.zeros((chunk, lats), F32)
        for at in starts:
            span = slice(at, at + step)
            resid = jnp.where(bins[:, span] < length, held[rows, span] - counts_ref[rows, span].astype(F32), 0.0)
            for j in range(step // LANES):
                sums = sums + resid[:, j * LANES : (j + 1) * LANES]
            grad = grad + lax.dot_general(
                resid.astype(BF16), shifted[0:lats, span], (((1,), (1,)), ((), ())), preferred_element_type=F32
            )
        load_ref[:, rows] = grad.T
        bias_ref[:, rows] = jnp.sum(sums.T, axis=0, keepdims=True)
        place = pl.ds(first + rows.start, chunk)
        outward.append(pltpu.make_async_copy(load_ref.at[:, rows], load_hbm.at[:, place], sems.at[2 * index]))
        outward.append(pltpu.make_async_copy(bias_ref.at[:, rows], bias_hbm.at[:, place], sems.at[2 * index + 1]))
        for copy in outward[-2:]:
            copy.start()
    for copy in outward:
        copy.wait()


def encode(value):
    top = jnp.maximum(jnp.max(jnp.abs(value), axis=0, keepdims=True), 2.0**-100)
    power = jnp.ceil(jnp.log2(top)) - 14.0
    rows = jnp.broadcast_to(power, (8, value.shape[1]))
    return jnp.concatenate([value * jnp.exp2(-power), rows], axis=0).astype(jnp.float16)


def decode(code):
    power = code[-8:-7].astype(F32)
    return code[:-8].astype(F32) * jnp.exp2(power)


def per_device(region_count, neuron_count, counts, latents, loadings, bias, delays, recorded):
    neurons, total = counts.shape[1:]
    lats, width = latents.shape
    chunk, step = 256, 512
    vmem = pl.BlockSpec(memory_space=pltpu.VMEM)
    hbm = pl.BlockSpec(memory_space=pltpu.HBM)
    params = pltpu.CompilerParams(vmem_limit_bytes=52 * 1024 * 1024)

    def swap(value, axis, count, mask):
        return lax.ppermute(value, axis, [(i, i ^ mask) for i in range(count)])

    order = sorted(range(1, neuron_count), key=lambda k: (k != 2, k))
    arrived = [swap(latents, "neuron", neuron_count, k) for k in order]
    row = lax.broadcasted_iota(jnp.int32, (lats + 8, neurons + width), 0)
    lines = jnp.pad(delays, ((lats + 1, 6), (0, neurons + width - lats)))
    lines = jnp.where(row == lats + 2, jnp.broadcast_to(recorded[:, None], lines.shape), lines)
    pack = jnp.pad(bias, ((lats, 7), (0, width))) + lines.astype(F32)
    pack = pack + jnp.pad(loadings[0], ((0, 8), (0, width))).astype(F32)
    pack = pack + jnp.pad(latents, ((0, 8), (neurons, 0))).astype(F32)

    *outs, turned, shifted = pl.pallas_call(
        functools.partial(shift_kernel, neuron_count, order, "neuron", chunk, step),
        out_shape=[jax.ShapeDtypeStruct((lats, width), BF16 if k > 1 else F32) for k in range(neuron_count)]
        + [jax.ShapeDtypeStruct((neurons, lats + EXTRA), BF16), jax.ShapeDtypeStruct((lats + EXTRA, total), BF16)],
        in_specs=[vmem, hbm] + [vmem] * (neuron_count - 1),
        out_specs=[vmem] * (neuron_count + 2),
        scratch_shapes=[
            pltpu.VMEM((lats, total), BF16),
            pltpu.VMEM((neurons, total), BF16),
            pltpu.VMEM((4 * chunk, total), F32),
            pltpu.VMEM((neurons, total), BF16),
            pltpu.VMEM((lats + EXTRA, neurons), BF16),
            pltpu.VMEM((lats, total), F32),
            pltpu.SemaphoreType.DMA((neurons // chunk,)),
        ],
        compiler_params=params,
    )(pack, counts[0], *arrived)

    shares = [(0, 2 * chunk), (2 * chunk, neurons - 2 * chunk)]
    made = []

    def make(before):
        first, count = shares.pop(0)
        before, start_load = lax.optimization_barrier((before, turned))
        out = pl.pallas_call(
            functools.partial(load_kernel, lats, first, chunk, step),
            out_shape=[jax.ShapeDtypeStruct((lats, neurons), F32), jax.ShapeDtypeStruct((1, neurons), F32)],
            in_specs=[vmem, vmem, vmem, hbm] + [hbm] * len(made),
            out_specs=[hbm, hbm],
            scratch_shapes=[
                pltpu.VMEM((count, total), BF16),
                pltpu.VMEM((count, total), F32),
                pltpu.VMEM((lats, count), F32),
                pltpu.VMEM((1, count), F32),
                pltpu.SemaphoreType.DMA((count // chunk,)),
                pltpu.SemaphoreType.DMA((2 * (count // chunk),)),
            ],
            input_output_aliases={4 + i: i for i in range(len(made))},
            compiler_params=params,
            cost_estimate=pl.CostEstimate(
                flops=4 * lats * count * total, bytes_accessed=2 * count * total, transcendentals=count * total
            ),
        )(pack, start_load, shifted, counts[0], *made)
        return before, out

    outs, made = make(outs)
    arrived = [swap(outs[k], "neuron", neuron_count, k) for k in [*range(2, neuron_count), 1]]
    arrived, made = lax.optimization_barrier((arrived, made))
    value = functools.reduce(jnp.add, [outs[0]] + [block.astype(F32) for block in arrived])
    mask = 1
    while mask < region_count:
        masks = [mask, 2 * mask, 3 * mask] if 2 * mask < region_count else [mask]
        code = lax.optimization_barrier(encode(value))
        if shares:
            code, made = make(code)
        arrived = [swap(code, "region", region_count, k) for k in masks]
        arrived, made = lax.optimization_barrier((arrived, made))
        value = decode(code) + decode(arrived[0])
        if len(masks) == 3:
            value = value + (decode(arrived[1]) + decode(arrived[2]))
        mask *= 1 + len(masks)
    grad_load, grad_bias = made
    return (value, grad_load[None], grad_bias)


def solution(mesh):
    placed = (
        P("region", "neuron", None),
        P(None, "neuron"),
        P("region", None, "neuron"),
        P("region", "neuron"),
        P("region", None),
        P("region"),
    )
    return jax.shard_map(
        functools.partial(per_device, mesh.shape["region"], mesh.shape["neuron"]),
        mesh=mesh,
        in_specs=placed,
        out_specs=(P(None, "neuron"), P("region", None, "neuron"), P("region", "neuron")),
        check_vma=False,
    )
```

```python
import functools

import jax
import jax.numpy as jnp
from jax import lax
from jax.experimental import pallas as pl
from jax.experimental.pallas import tpu as pltpu
from jax.sharding import PartitionSpec as P

LANES = 128
EXTRA = 16
F32 = jnp.float32
BF16 = jnp.bfloat16


def shift_tiles(tiles, delay, forward):
    lane = lax.broadcasted_iota(jnp.int32, delay.shape, 1)
    source = lane - delay if forward else lane + delay
    inside = source >= 0 if forward else source < LANES
    source = source & (LANES - 1)
    turned = [jnp.take_along_axis(tile, source, axis=1, mode="promise_in_bounds") for tile in tiles]
    nothing = [jnp.zeros_like(tiles[0])]
    others = nothing + turned[:-1] if forward else turned[1:] + nothing
    return [jnp.where(inside, tile, other) for tile, other in zip(turned, others)]


def expected(load_part, piece):
    eta = lax.dot_general(load_part, piece, (((0,), (0,)), ((), ())), preferred_element_type=F32)
    return jnp.exp(eta)


def shift_kernel(parts, order, targets, axis, chunk, step, *refs):
    pack_ref, counts_hbm = refs[:2]
    arrived = refs[2 : 1 + parts]
    outs = refs[1 + parts : 1 + 2 * parts]
    load_ext, shifted, whole, counts_ref, held, resid_low, grad_shift, counts_sem = refs[1 + 2 * parts :]
    me = lax.axis_index(axis)
    lats, total = grad_shift.shape
    early = held.shape[0]
    neurons = counts_ref.shape[0]
    width = total // parts
    counts_copy = pltpu.make_async_copy(counts_hbm, counts_ref, counts_sem)
    counts_copy.start()

    for k in range(parts):
        start = pl.multiple_of((me ^ k) * width, width)
        whole[:, pl.ds(start, width)] = arrived[order.index(k)][...] if k else pack_ref[0:lats, neurons:].astype(BF16)
    diagonal = lax.broadcasted_iota(jnp.int32, (lats, LANES), 0) == lax.broadcasted_iota(jnp.int32, (lats, LANES), 1)
    spread = jnp.broadcast_to(pack_ref[lats + 1 : lats + 2, 0:LANES], (lats, LANES))
    column = jnp.sum(jnp.where(diagonal, spread, 0.0), axis=1, keepdims=True)
    delay = jnp.broadcast_to(column, (lats, LANES)).astype(jnp.int32)
    length = pack_ref[lats + 2 : lats + 3, 0:1].astype(jnp.int32)
    tiles = [whole[:, j * LANES : (j + 1) * LANES].astype(F32) for j in range(total // LANES)]
    for j, tile in enumerate(shift_tiles(tiles, delay, True)):
        shifted[0:lats, j * LANES : (j + 1) * LANES] = tile.astype(BF16)
    row = lax.broadcasted_iota(jnp.int32, (EXTRA, total), 0)
    shifted[lats:, :] = jnp.where(row < 3, 1.0, 0.0).astype(BF16)

    load_ext[0:lats, :] = pack_ref[0:lats, 0:neurons].astype(BF16)
    bias = pack_ref[lats : lats + 1, 0:neurons]
    high = bias.astype(BF16).astype(F32)
    middle = (bias - high).astype(BF16).astype(F32)
    low = bias - high - middle
    row = lax.broadcasted_iota(jnp.int32, (EXTRA, neurons), 0)
    below = jnp.where(row == 0, high, jnp.where(row == 1, middle, jnp.where(row == 2, low, 0.0)))
    load_ext[lats:, :] = below.astype(BF16)

    blocks = [
        (slice(first, first + chunk), slice(begin, begin + step))
        for first in range(0, neurons, chunk)
        for begin in range(0, total, step)
    ]
    for rows, span in blocks:
        if rows.start < early:
            held[rows, span] = expected(load_ext[:, rows], shifted[:, span])
    counts_copy.wait()
    for rows, span in blocks:
        rate = held[rows, span] if rows.start < early else expected(load_ext[:, rows], shifted[:, span])
        resid_low[rows, span] = (rate - counts_ref[rows, span].astype(F32)).astype(BF16)
    for begin in range(0, total, step):
        span = slice(begin, begin + step)
        grad_shift[:, span] = jnp.dot(load_ext[0:lats, :], resid_low[:, span], preferred_element_type=F32)

    bins = lax.broadcasted_iota(jnp.int32, (1, total), 1)
    tiles = []
    for j in range(total // LANES):
        span = slice(j * LANES, (j + 1) * LANES)
        tiles.append(jnp.where(bins[:, span] < length, grad_shift[:, span], 0.0))
    for j, tile in enumerate(shift_tiles(tiles, delay, False)):
        grad_shift[:, j * LANES : (j + 1) * LANES] = tile
    for k, out in zip(targets, outs):
        start = pl.multiple_of((me ^ k) * width, width)
        out[...] = grad_shift[:, pl.ds(start, width)].astype(out.dtype)


def load_kernel(lats, first, chunk, step, *refs):
    pack_ref, load_ext, shifted, counts_hbm = refs[:4]
    load_hbm, bias_hbm, counts_ref, held, load_ref, bias_ref, sems = refs[-7:]
    count, total = counts_ref.shape
    place = pl.ds(first, count)
    counts_copy = pltpu.make_async_copy(counts_hbm.at[place], counts_ref, sems.at[0])
    counts_copy.start()
    length = pack_ref[lats + 2 : lats + 3, 0:1].astype(jnp.int32)
    bins = lax.broadcasted_iota(jnp.int32, (1, total), 1)
    blocks = [(slice(begin, begin + chunk), range(0, total, step)) for begin in range(0, count, chunk)]
    for rows, starts in blocks:
        for at in starts:
            load_part = load_ext[:, first + rows.start : first + rows.stop]
            held[rows, at : at + step] = expected(load_part, shifted[:, at : at + step])
    counts_copy.wait()
    outward = []
    for index, (rows, starts) in enumerate(blocks):
        sums = jnp.zeros((chunk, LANES), F32)
        grad = jnp.zeros((chunk, lats), F32)
        for at in starts:
            span = slice(at, at + step)
            resid = jnp.where(bins[:, span] < length, held[rows, span] - counts_ref[rows, span].astype(F32), 0.0)
            for j in range(step // LANES):
                sums = sums + resid[:, j * LANES : (j + 1) * LANES]
            grad = grad + lax.dot_general(
                resid.astype(BF16), shifted[0:lats, span], (((1,), (1,)), ((), ())), preferred_element_type=F32
            )
        load_ref[:, rows] = grad.T
        bias_ref[:, rows] = jnp.sum(sums.T, axis=0, keepdims=True)
        place = pl.ds(first + rows.start, chunk)
        outward.append(pltpu.make_async_copy(load_ref.at[:, rows], load_hbm.at[:, place], sems.at[2 * index + 1]))
        outward.append(pltpu.make_async_copy(bias_ref.at[:, rows], bias_hbm.at[:, place], sems.at[2 * index + 2]))
        for copy in outward[-2:]:
            copy.start()
    for copy in outward:
        copy.wait()


def encode(value):
    top = jnp.maximum(jnp.max(jnp.abs(value), axis=0, keepdims=True), 2.0**-100)
    power = jnp.ceil(jnp.log2(top)) - 14.0
    rows = jnp.broadcast_to(power, (8, value.shape[1]))
    return jnp.concatenate([value * jnp.exp2(-power), rows], axis=0).astype(jnp.float16)


def decode(code):
    power = code[-8:-7].astype(F32)
    return code[:-8].astype(F32) * jnp.exp2(power)


def per_device(region_count, neuron_count, counts, latents, loadings, bias, delays, recorded):
    neurons, total = counts.shape[1:]
    lats, width = latents.shape
    chunk, step = 256, 512
    vmem = pl.BlockSpec(memory_space=pltpu.VMEM)
    hbm = pl.BlockSpec(memory_space=pltpu.HBM)
    params = pltpu.CompilerParams(vmem_limit_bytes=52 * 1024 * 1024)

    def swap(value, axis, count, mask):
        return lax.ppermute(value, axis, [(i, i ^ mask) for i in range(count)])

    order = [*range(2, neuron_count), 1]
    arrived = [swap(latents, "neuron", neuron_count, k) for k in order]
    row = lax.broadcasted_iota(jnp.int32, (lats + 8, neurons + width), 0)
    lines = jnp.pad(delays, ((lats + 1, 6), (0, neurons + width - lats)))
    lines = jnp.where(row == lats + 2, jnp.broadcast_to(recorded[:, None], lines.shape), lines)
    pack = jnp.pad(bias, ((lats, 7), (0, width))) + lines.astype(F32)
    pack = pack + jnp.pad(loadings[0], ((0, 8), (0, width))).astype(F32)
    pack = pack + jnp.pad(latents, ((0, 8), (neurons, 0))).astype(F32)

    targets = [0, *order]
    *outs, load_ext, shifted = pl.pallas_call(
        functools.partial(shift_kernel, neuron_count, order, targets, "neuron", chunk, step),
        out_shape=[jax.ShapeDtypeStruct((lats, width), BF16 if k else F32) for k in targets]
        + [jax.ShapeDtypeStruct((lats + EXTRA, neurons), BF16), jax.ShapeDtypeStruct((lats + EXTRA, total), BF16)],
        in_specs=[vmem, hbm] + [vmem] * (neuron_count - 1),
        out_specs=[vmem] * (neuron_count + 2),
        scratch_shapes=[
            pltpu.VMEM((lats, total), BF16),
            pltpu.VMEM((neurons, total), BF16),
            pltpu.VMEM((2 * chunk, total), F32),
            pltpu.VMEM((neurons, total), BF16),
            pltpu.VMEM((lats, total), F32),
            pltpu.SemaphoreType.DMA,
        ],
        compiler_params=params,
    )(pack, counts[0], *arrived)

    shares = [(0, 2 * chunk), (2 * chunk, neurons - 2 * chunk)]
    made = []

    def make(before):
        first, count = shares.pop(0)
        before, start_load = lax.optimization_barrier((before, load_ext))
        out = pl.pallas_call(
            functools.partial(load_kernel, lats, first, chunk, step),
            out_shape=[jax.ShapeDtypeStruct((lats, neurons), F32), jax.ShapeDtypeStruct((1, neurons), F32)],
            in_specs=[vmem, vmem, vmem, hbm] + [hbm] * len(made),
            out_specs=[hbm, hbm],
            scratch_shapes=[
                pltpu.VMEM((count, total), BF16),
                pltpu.VMEM((count, total), F32),
                pltpu.VMEM((lats, count), F32),
                pltpu.VMEM((1, count), F32),
                pltpu.SemaphoreType.DMA((1 + 2 * (count // chunk),)),
            ],
            input_output_aliases={4 + i: i for i in range(len(made))},
            compiler_params=params,
            cost_estimate=pl.CostEstimate(
                flops=4 * lats * count * total, bytes_accessed=2 * count * total, transcendentals=count * total
            ),
        )(pack, start_load, shifted, counts[0], *made)
        return before, out

    outs, made = make(outs)
    arrived = [swap(out, "neuron", neuron_count, k) for k, out in zip(targets[1:], outs[1:])]
    arrived, made = lax.optimization_barrier((arrived, made))
    value = functools.reduce(jnp.add, [outs[0]] + [block.astype(F32) for block in arrived])
    mask = 1
    while mask < region_count:
        masks = [mask, 2 * mask, 3 * mask] if 2 * mask < region_count else [mask]
        code = lax.optimization_barrier(encode(value))
        if shares:
            code, made = make(code)
        arrived = [swap(code, "region", region_count, k) for k in masks]
        arrived, made = lax.optimization_barrier((arrived, made))
        value = decode(code) + decode(arrived[0])
        if len(masks) == 3:
            value = value + (decode(arrived[1]) + decode(arrived[2]))
        mask *= 1 + len(masks)
    grad_load, grad_bias = made
    return (value, grad_load[None], grad_bias)


def solution(mesh):
    placed = (
        P("region", "neuron", None),
        P(None, "neuron"),
        P("region", None, "neuron"),
        P("region", "neuron"),
        P("region", None),
        P("region"),
    )
    return jax.shard_map(
        functools.partial(per_device, mesh.shape["region"], mesh.shape["neuron"]),
        mesh=mesh,
        in_specs=placed,
        out_specs=(P(None, "neuron"), P("region", None, "neuron"), P("region", "neuron")),
        check_vma=False,
    )
```

```python
import functools

import jax
import jax.numpy as jnp
from jax import lax
from jax.experimental import pallas as pl
from jax.experimental.pallas import tpu as pltpu
from jax.sharding import PartitionSpec as P

LANES = 128
EXTRA = 16
F32 = jnp.float32
BF16 = jnp.bfloat16


def shift_tiles(tiles, delay, forward):
    lane = lax.broadcasted_iota(jnp.int32, delay.shape, 1)
    source = lane - delay if forward else lane + delay
    inside = source >= 0 if forward else source < LANES
    source = source & (LANES - 1)
    turned = [jnp.take_along_axis(tile, source, axis=1, mode="promise_in_bounds") for tile in tiles]
    nothing = [jnp.zeros_like(tiles[0])]
    others = nothing + turned[:-1] if forward else turned[1:] + nothing
    return [jnp.where(inside, tile, other) for tile, other in zip(turned, others)]


def expected(load_part, piece):
    eta = lax.dot_general(load_part, piece, (((0,), (0,)), ((), ())), preferred_element_type=F32)
    return jnp.exp(eta)


def shift_kernel(parts, order, axis, chunk, step, *refs):
    pack_ref, counts_hbm = refs[:2]
    arrived = refs[2 : 1 + parts]
    outs = refs[1 + parts : 1 + 2 * parts]
    load_ext, shifted, whole, counts_ref, held, resid_low, grad_shift, counts_sem = refs[1 + 2 * parts :]
    me = lax.axis_index(axis)
    lats, total = grad_shift.shape
    neurons = counts_ref.shape[0]
    width = total // parts
    counts_copy = pltpu.make_async_copy(counts_hbm, counts_ref, counts_sem)
    counts_copy.start()

    for k in range(parts):
        start = pl.multiple_of((me ^ k) * width, width)
        whole[:, pl.ds(start, width)] = arrived[order.index(k)][...] if k else pack_ref[0:lats, neurons:].astype(BF16)
    diagonal = lax.broadcasted_iota(jnp.int32, (lats, LANES), 0) == lax.broadcasted_iota(jnp.int32, (lats, LANES), 1)
    spread = jnp.broadcast_to(pack_ref[lats + 1 : lats + 2, 0:LANES], (lats, LANES))
    column = jnp.sum(jnp.where(diagonal, spread, 0.0), axis=1, keepdims=True)
    delay = jnp.broadcast_to(column, (lats, LANES)).astype(jnp.int32)
    length = pack_ref[lats + 2 : lats + 3, 0:1].astype(jnp.int32)
    tiles = [whole[:, j * LANES : (j + 1) * LANES].astype(F32) for j in range(total // LANES)]
    for j, tile in enumerate(shift_tiles(tiles, delay, True)):
        shifted[0:lats, j * LANES : (j + 1) * LANES] = tile.astype(BF16)
    row = lax.broadcasted_iota(jnp.int32, (EXTRA, total), 0)
    shifted[lats:, :] = jnp.where(row < 3, 1.0, 0.0).astype(BF16)

    load_ext[0:lats, :] = pack_ref[0:lats, 0:neurons].astype(BF16)
    bias = pack_ref[lats : lats + 1, 0:neurons]
    high = bias.astype(BF16).astype(F32)
    middle = (bias - high).astype(BF16).astype(F32)
    low = bias - high - middle
    row = lax.broadcasted_iota(jnp.int32, (EXTRA, neurons), 0)
    below = jnp.where(row == 0, high, jnp.where(row == 1, middle, jnp.where(row == 2, low, 0.0)))
    load_ext[lats:, :] = below.astype(BF16)

    blocks = [
        (slice(first, first + chunk), slice(begin, begin + step))
        for first in range(0, neurons, chunk)
        for begin in range(0, total, step)
    ]
    for rows, span in blocks:
        held[rows, span] = expected(load_ext[:, rows], shifted[:, span])
    counts_copy.wait()
    for rows, span in blocks:
        resid_low[rows, span] = (held[rows, span] - counts_ref[rows, span].astype(F32)).astype(BF16)
    for begin in range(0, total, step):
        span = slice(begin, begin + step)
        grad_shift[:, span] = jnp.dot(load_ext[0:lats, :], resid_low[:, span], preferred_element_type=F32)

    bins = lax.broadcasted_iota(jnp.int32, (1, total), 1)
    tiles = []
    for j in range(total // LANES):
        span = slice(j * LANES, (j + 1) * LANES)
        tiles.append(jnp.where(bins[:, span] < length, grad_shift[:, span], 0.0))
    for j, tile in enumerate(shift_tiles(tiles, delay, False)):
        grad_shift[:, j * LANES : (j + 1) * LANES] = tile
    for k in range(parts):
        start = pl.multiple_of((me ^ k) * width, width)
        outs[k][...] = grad_shift[:, pl.ds(start, width)].astype(outs[k].dtype)


def load_kernel(lats, first, chunk, step, *refs):
    pack_ref, load_ext, shifted, counts_hbm = refs[:4]
    load_hbm, bias_hbm, counts_ref, held, load_ref, bias_ref, sems = refs[-7:]
    count, total = counts_ref.shape
    place = pl.ds(first, count)
    counts_copy = pltpu.make_async_copy(counts_hbm.at[place], counts_ref, sems.at[0])
    counts_copy.start()
    length = pack_ref[lats + 2 : lats + 3, 0:1].astype(jnp.int32)
    bins = lax.broadcasted_iota(jnp.int32, (1, total), 1)
    blocks = [(slice(begin, begin + chunk), range(0, total, step)) for begin in range(0, count, chunk)]
    for rows, starts in blocks:
        for at in starts:
            load_part = load_ext[:, first + rows.start : first + rows.stop]
            held[rows, at : at + step] = expected(load_part, shifted[:, at : at + step])
    counts_copy.wait()
    outward = []
    for index, (rows, starts) in enumerate(blocks):
        sums = jnp.zeros((chunk, LANES), F32)
        grad = jnp.zeros((chunk, lats), F32)
        for at in starts:
            span = slice(at, at + step)
            resid = jnp.where(bins[:, span] < length, held[rows, span] - counts_ref[rows, span].astype(F32), 0.0)
            for j in range(step // LANES):
                sums = sums + resid[:, j * LANES : (j + 1) * LANES]
            grad = grad + lax.dot_general(
                resid.astype(BF16), shifted[0:lats, span], (((1,), (1,)), ((), ())), preferred_element_type=F32
            )
        load_ref[:, rows] = grad.T
        bias_ref[:, rows] = jnp.sum(sums.T, axis=0, keepdims=True)
        place = pl.ds(first + rows.start, chunk)
        outward.append(pltpu.make_async_copy(load_ref.at[:, rows], load_hbm.at[:, place], sems.at[2 * index + 1]))
        outward.append(pltpu.make_async_copy(bias_ref.at[:, rows], bias_hbm.at[:, place], sems.at[2 * index + 2]))
        for copy in outward[-2:]:
            copy.start()
    for copy in outward:
        copy.wait()


def encode(value):
    top = jnp.maximum(jnp.max(jnp.abs(value), axis=0, keepdims=True), 2.0**-100)
    power = jnp.ceil(jnp.log2(top)) - 14.0
    rows = jnp.broadcast_to(power, (8, value.shape[1]))
    return jnp.concatenate([value * jnp.exp2(-power), rows], axis=0).astype(jnp.float16)


def decode(code):
    power = code[-8:-7].astype(F32)
    return code[:-8].astype(F32) * jnp.exp2(power)


def per_device(region_count, neuron_count, counts, latents, loadings, bias, delays, recorded):
    neurons, total = counts.shape[1:]
    lats, width = latents.shape
    chunk, step = 256, 512
    vmem = pl.BlockSpec(memory_space=pltpu.VMEM)
    hbm = pl.BlockSpec(memory_space=pltpu.HBM)
    params = pltpu.CompilerParams(vmem_limit_bytes=52 * 1024 * 1024)

    def swap(value, axis, count, mask):
        return lax.ppermute(value, axis, [(i, i ^ mask) for i in range(count)])

    order = sorted(range(1, neuron_count), key=lambda k: (k != 2, k))
    arrived = [swap(latents, "neuron", neuron_count, k) for k in order]
    row = lax.broadcasted_iota(jnp.int32, (lats + 8, neurons + width), 0)
    lines = jnp.pad(delays, ((lats + 1, 6), (0, neurons + width - lats)))
    lines = jnp.where(row == lats + 2, jnp.broadcast_to(recorded[:, None], lines.shape), lines)
    pack = jnp.pad(bias, ((lats, 7), (0, width))) + lines.astype(F32)
    pack = pack + jnp.pad(loadings[0], ((0, 8), (0, width))).astype(F32)
    pack = pack + jnp.pad(latents, ((0, 8), (neurons, 0))).astype(F32)

    *outs, load_ext, shifted = pl.pallas_call(
        functools.partial(shift_kernel, neuron_count, order, "neuron", chunk, step),
        out_shape=[jax.ShapeDtypeStruct((lats, width), BF16 if k > 1 else F32) for k in range(neuron_count)]
        + [jax.ShapeDtypeStruct((lats + EXTRA, neurons), BF16), jax.ShapeDtypeStruct((lats + EXTRA, total), BF16)],
        in_specs=[vmem, hbm] + [vmem] * (neuron_count - 1),
        out_specs=[vmem] * (neuron_count + 2),
        scratch_shapes=[
            pltpu.VMEM((lats, total), BF16),
            pltpu.VMEM((neurons, total), BF16),
            pltpu.VMEM((neurons, total), F32),
            pltpu.VMEM((neurons, total), BF16),
            pltpu.VMEM((lats, total), F32),
            pltpu.SemaphoreType.DMA,
        ],
        compiler_params=params,
    )(pack, counts[0], *arrived)

    shares = [(0, 2 * chunk), (2 * chunk, neurons - 2 * chunk)]
    made = []

    def make(before):
        first, count = shares.pop(0)
        before, start_load = lax.optimization_barrier((before, load_ext))
        out = pl.pallas_call(
            functools.partial(load_kernel, lats, first, chunk, step),
            out_shape=[jax.ShapeDtypeStruct((lats, neurons), F32), jax.ShapeDtypeStruct((1, neurons), F32)],
            in_specs=[vmem, vmem, vmem, hbm] + [hbm] * len(made),
            out_specs=[hbm, hbm],
            scratch_shapes=[
                pltpu.VMEM((count, total), BF16),
                pltpu.VMEM((count, total), F32),
                pltpu.VMEM((lats, count), F32),
                pltpu.VMEM((1, count), F32),
                pltpu.SemaphoreType.DMA((1 + 2 * (count // chunk),)),
            ],
            input_output_aliases={4 + i: i for i in range(len(made))},
            compiler_params=params,
            cost_estimate=pl.CostEstimate(
                flops=4 * lats * count * total, bytes_accessed=2 * count * total, transcendentals=count * total
            ),
        )(pack, start_load, shifted, counts[0], *made)
        return before, out

    outs, made = make(outs)
    arrived = [swap(outs[k], "neuron", neuron_count, k) for k in [*range(2, neuron_count), 1]]
    arrived, made = lax.optimization_barrier((arrived, made))
    value = functools.reduce(jnp.add, [outs[0]] + [block.astype(F32) for block in arrived])
    mask = 1
    while mask < region_count:
        masks = [mask, 2 * mask, 3 * mask] if 2 * mask < region_count else [mask]
        if len(masks) == 3:
            value = lax.reduce_precision(value, 8, 7)
            sent, read = value.astype(BF16), lambda block: block.astype(F32)
        else:
            sent, read = lax.optimization_barrier(encode(value)), decode
            value = decode(sent)
        if shares:
            (value, sent), made = make((value, sent))
        arrived = [swap(sent, "region", region_count, k) for k in masks]
        arrived, made = lax.optimization_barrier((arrived, made))
        value = value + read(arrived[0])
        if len(masks) == 3:
            value = value + (read(arrived[1]) + read(arrived[2]))
        mask *= 1 + len(masks)
    grad_load, grad_bias = made
    return (value, grad_load[None], grad_bias)


def solution(mesh):
    placed = (
        P("region", "neuron", None),
        P(None, "neuron"),
        P("region", None, "neuron"),
        P("region", "neuron"),
        P("region", None),
        P("region"),
    )
    return jax.shard_map(
        functools.partial(per_device, mesh.shape["region"], mesh.shape["neuron"]),
        mesh=mesh,
        in_specs=placed,
        out_specs=(P(None, "neuron"), P("region", None, "neuron"), P("region", "neuron")),
        check_vma=False,
    )
```

```python
import functools

import jax
import jax.numpy as jnp
from jax import lax
from jax.experimental import pallas as pl
from jax.experimental.pallas import tpu as pltpu
from jax.sharding import PartitionSpec as P

LANES = 128
EXTRA = 16
F32 = jnp.float32
BF16 = jnp.bfloat16


def shift_tiles(tiles, delay, forward):
    lane = lax.broadcasted_iota(jnp.int32, delay.shape, 1)
    source = lane - delay if forward else lane + delay
    inside = source >= 0 if forward else source < LANES
    source = source & (LANES - 1)
    turned = [jnp.take_along_axis(tile, source, axis=1, mode="promise_in_bounds") for tile in tiles]
    nothing = [jnp.zeros_like(tiles[0])]
    others = nothing + turned[:-1] if forward else turned[1:] + nothing
    return [jnp.where(inside, tile, other) for tile, other in zip(turned, others)]


def expected(load_part, piece):
    eta = lax.dot_general(load_part, piece, (((0,), (0,)), ((), ())), preferred_element_type=F32)
    return jnp.exp(eta)


def shift_kernel(parts, order, axis, chunk, step, *refs):
    pack_ref, counts_hbm = refs[:2]
    arrived = refs[2 : 1 + parts]
    outs = refs[1 + parts : 1 + 2 * parts]
    load_ext, shifted, whole, counts_ref, held, resid_low, grad_shift, counts_sem = refs[1 + 2 * parts :]
    me = lax.axis_index(axis)
    lats, total = grad_shift.shape
    early = held.shape[0]
    neurons = counts_ref.shape[0]
    width = total // parts
    counts_copy = pltpu.make_async_copy(counts_hbm, counts_ref, counts_sem)
    counts_copy.start()

    for k in range(parts):
        start = pl.multiple_of((me ^ k) * width, width)
        whole[:, pl.ds(start, width)] = arrived[order.index(k)][...] if k else pack_ref[0:lats, neurons:].astype(BF16)
    diagonal = lax.broadcasted_iota(jnp.int32, (lats, LANES), 0) == lax.broadcasted_iota(jnp.int32, (lats, LANES), 1)
    spread = jnp.broadcast_to(pack_ref[lats + 1 : lats + 2, 0:LANES], (lats, LANES))
    column = jnp.sum(jnp.where(diagonal, spread, 0.0), axis=1, keepdims=True)
    delay = jnp.broadcast_to(column, (lats, LANES)).astype(jnp.int32)
    length = pack_ref[lats + 2 : lats + 3, 0:1].astype(jnp.int32)
    tiles = [whole[:, j * LANES : (j + 1) * LANES].astype(F32) for j in range(total // LANES)]
    for j, tile in enumerate(shift_tiles(tiles, delay, True)):
        shifted[0:lats, j * LANES : (j + 1) * LANES] = tile.astype(BF16)
    row = lax.broadcasted_iota(jnp.int32, (EXTRA, total), 0)
    shifted[lats:, :] = jnp.where(row < 3, 1.0, 0.0).astype(BF16)

    load_ext[0:lats, :] = pack_ref[0:lats, 0:neurons].astype(BF16)
    bias = pack_ref[lats : lats + 1, 0:neurons]
    high = bias.astype(BF16).astype(F32)
    middle = (bias - high).astype(BF16).astype(F32)
    low = bias - high - middle
    row = lax.broadcasted_iota(jnp.int32, (EXTRA, neurons), 0)
    below = jnp.where(row == 0, high, jnp.where(row == 1, middle, jnp.where(row == 2, low, 0.0)))
    load_ext[lats:, :] = below.astype(BF16)

    blocks = [
        (slice(first, first + chunk), slice(begin, begin + step))
        for first in range(0, neurons, chunk)
        for begin in range(0, total, step)
    ]
    for rows, span in blocks:
        if rows.start < early:
            held[rows, span] = expected(load_ext[:, rows], shifted[:, span])
    counts_copy.wait()
    for rows, span in blocks:
        rate = held[rows, span] if rows.start < early else expected(load_ext[:, rows], shifted[:, span])
        resid_low[rows, span] = (rate - counts_ref[rows, span].astype(F32)).astype(BF16)
    for begin in range(0, total, step):
        span = slice(begin, begin + step)
        grad_shift[:, span] = jnp.dot(load_ext[0:lats, :], resid_low[:, span], preferred_element_type=F32)

    bins = lax.broadcasted_iota(jnp.int32, (1, total), 1)
    tiles = []
    for j in range(total // LANES):
        span = slice(j * LANES, (j + 1) * LANES)
        tiles.append(jnp.where(bins[:, span] < length, grad_shift[:, span], 0.0))
    for j, tile in enumerate(shift_tiles(tiles, delay, False)):
        grad_shift[:, j * LANES : (j + 1) * LANES] = tile
    for k in range(parts):
        start = pl.multiple_of((me ^ k) * width, width)
        outs[k][...] = grad_shift[:, pl.ds(start, width)].astype(outs[k].dtype)


def load_kernel(lats, first, chunk, step, *refs):
    pack_ref, load_ext, shifted, counts_hbm = refs[:4]
    load_hbm, bias_hbm, counts_ref, held, load_ref, bias_ref, sems = refs[-7:]
    count, total = counts_ref.shape
    place = pl.ds(first, count)
    counts_copy = pltpu.make_async_copy(counts_hbm.at[place], counts_ref, sems.at[0])
    counts_copy.start()
    length = pack_ref[lats + 2 : lats + 3, 0:1].astype(jnp.int32)
    bins = lax.broadcasted_iota(jnp.int32, (1, total), 1)
    blocks = [(slice(begin, begin + chunk), range(0, total, step)) for begin in range(0, count, chunk)]
    for rows, starts in blocks:
        for at in starts:
            load_part = load_ext[:, first + rows.start : first + rows.stop]
            held[rows, at : at + step] = expected(load_part, shifted[:, at : at + step])
    counts_copy.wait()
    outward = []
    for index, (rows, starts) in enumerate(blocks):
        sums = jnp.zeros((chunk, LANES), F32)
        grad = jnp.zeros((chunk, lats), F32)
        for at in starts:
            span = slice(at, at + step)
            resid = jnp.where(bins[:, span] < length, held[rows, span] - counts_ref[rows, span].astype(F32), 0.0)
            for j in range(step // LANES):
                sums = sums + resid[:, j * LANES : (j + 1) * LANES]
            grad = grad + lax.dot_general(
                resid.astype(BF16), shifted[0:lats, span], (((1,), (1,)), ((), ())), preferred_element_type=F32
            )
        load_ref[:, rows] = grad.T
        bias_ref[:, rows] = jnp.sum(sums.T, axis=0, keepdims=True)
        place = pl.ds(first + rows.start, chunk)
        outward.append(pltpu.make_async_copy(load_ref.at[:, rows], load_hbm.at[:, place], sems.at[2 * index + 1]))
        outward.append(pltpu.make_async_copy(bias_ref.at[:, rows], bias_hbm.at[:, place], sems.at[2 * index + 2]))
        for copy in outward[-2:]:
            copy.start()
    for copy in outward:
        copy.wait()


def encode(value):
    top = jnp.maximum(jnp.max(jnp.abs(value), axis=0, keepdims=True), 2.0**-100)
    power = jnp.ceil(jnp.log2(top)) - 14.0
    rows = jnp.broadcast_to(power, (8, value.shape[1]))
    return jnp.concatenate([value * jnp.exp2(-power), rows], axis=0).astype(jnp.float16)


def decode(code):
    power = code[-8:-7].astype(F32)
    return code[:-8].astype(F32) * jnp.exp2(power)


def per_device(region_count, neuron_count, counts, latents, loadings, bias, delays, recorded):
    neurons, total = counts.shape[1:]
    lats, width = latents.shape
    chunk, step = 256, 512
    vmem = pl.BlockSpec(memory_space=pltpu.VMEM)
    hbm = pl.BlockSpec(memory_space=pltpu.HBM)
    params = pltpu.CompilerParams(vmem_limit_bytes=52 * 1024 * 1024)

    def swap(value, axis, count, mask):
        return lax.ppermute(value, axis, [(i, i ^ mask) for i in range(count)])

    order = sorted(range(1, neuron_count), key=lambda k: (k != 2, k))
    arrived = [swap(latents, "neuron", neuron_count, k) for k in order]
    row = lax.broadcasted_iota(jnp.int32, (lats + 8, neurons + width), 0)
    lines = jnp.pad(delays, ((lats + 1, 6), (0, neurons + width - lats)))
    lines = jnp.where(row == lats + 2, jnp.broadcast_to(recorded[:, None], lines.shape), lines)
    pack = jnp.pad(bias, ((lats, 7), (0, width))) + lines.astype(F32)
    pack = pack + jnp.pad(loadings[0], ((0, 8), (0, width))).astype(F32)
    pack = pack + jnp.pad(latents, ((0, 8), (neurons, 0))).astype(F32)

    *outs, load_ext, shifted = pl.pallas_call(
        functools.partial(shift_kernel, neuron_count, order, "neuron", chunk, step),
        out_shape=[jax.ShapeDtypeStruct((lats, width), BF16 if k > 1 else F32) for k in range(neuron_count)]
        + [jax.ShapeDtypeStruct((lats + EXTRA, neurons), BF16), jax.ShapeDtypeStruct((lats + EXTRA, total), BF16)],
        in_specs=[vmem, hbm] + [vmem] * (neuron_count - 1),
        out_specs=[vmem] * (neuron_count + 2),
        scratch_shapes=[
            pltpu.VMEM((lats, total), BF16),
            pltpu.VMEM((neurons, total), BF16),
            pltpu.VMEM((3 * chunk, total), F32),
            pltpu.VMEM((neurons, total), BF16),
            pltpu.VMEM((lats, total), F32),
            pltpu.SemaphoreType.DMA,
        ],
        compiler_params=params,
    )(pack, counts[0], *arrived)

    shares = [(0, 2 * chunk), (2 * chunk, neurons - 2 * chunk)]
    made = []

    def make(before):
        first, count = shares.pop(0)
        before, start_load = lax.optimization_barrier((before, load_ext))
        out = pl.pallas_call(
            functools.partial(load_kernel, lats, first, chunk, step),
            out_shape=[jax.ShapeDtypeStruct((lats, neurons), F32), jax.ShapeDtypeStruct((1, neurons), F32)],
            in_specs=[vmem, vmem, vmem, hbm] + [hbm] * len(made),
            out_specs=[hbm, hbm],
            scratch_shapes=[
                pltpu.VMEM((count, total), BF16),
                pltpu.VMEM((count, total), F32),
                pltpu.VMEM((lats, count), F32),
                pltpu.VMEM((1, count), F32),
                pltpu.SemaphoreType.DMA((1 + 2 * (count // chunk),)),
            ],
            input_output_aliases={4 + i: i for i in range(len(made))},
            compiler_params=params,
            cost_estimate=pl.CostEstimate(
                flops=4 * lats * count * total, bytes_accessed=2 * count * total, transcendentals=count * total
            ),
        )(pack, start_load, shifted, counts[0], *made)
        return before, out

    outs, made = make(outs)
    arrived = [swap(outs[k], "neuron", neuron_count, k) for k in [*range(2, neuron_count), 1]]
    arrived, made = lax.optimization_barrier((arrived, made))
    value = functools.reduce(jnp.add, [outs[0]] + [block.astype(F32) for block in arrived])
    mask = 1
    while mask < region_count:
        masks = [mask, 2 * mask, 3 * mask] if 2 * mask < region_count else [mask]
        if len(masks) == 3:
            value = lax.reduce_precision(value, 8, 7)
            sent, read = value.astype(BF16), lambda block: block.astype(F32)
        else:
            sent, read = lax.optimization_barrier(encode(value)), decode
            value = decode(sent)
        if shares:
            (value, sent), made = make((value, sent))
        arrived = [swap(sent, "region", region_count, k) for k in masks]
        arrived, made = lax.optimization_barrier((arrived, made))
        value = value + read(arrived[0])
        if len(masks) == 3:
            value = value + (read(arrived[1]) + read(arrived[2]))
        mask *= 1 + len(masks)
    grad_load, grad_bias = made
    return (value, grad_load[None], grad_bias)


def solution(mesh):
    placed = (
        P("region", "neuron", None),
        P(None, "neuron"),
        P("region", None, "neuron"),
        P("region", "neuron"),
        P("region", None),
        P("region"),
    )
    return jax.shard_map(
        functools.partial(per_device, mesh.shape["region"], mesh.shape["neuron"]),
        mesh=mesh,
        in_specs=placed,
        out_specs=(P(None, "neuron"), P("region", None, "neuron"), P("region", "neuron")),
        check_vma=False,
    )
```

```python
import functools

import jax
import jax.numpy as jnp
from jax import lax
from jax.experimental import pallas as pl
from jax.experimental.pallas import tpu as pltpu
from jax.sharding import PartitionSpec as P

LANES = 128
EXTRA = 16
F32 = jnp.float32
BF16 = jnp.bfloat16


def shift_tiles(tiles, delay, forward):
    lane = lax.broadcasted_iota(jnp.int32, delay.shape, 1)
    source = lane - delay if forward else lane + delay
    inside = source >= 0 if forward else source < LANES
    source = source & (LANES - 1)
    turned = [jnp.take_along_axis(tile, source, axis=1, mode="promise_in_bounds") for tile in tiles]
    nothing = [jnp.zeros_like(tiles[0])]
    others = nothing + turned[:-1] if forward else turned[1:] + nothing
    return [jnp.where(inside, tile, other) for tile, other in zip(turned, others)]


def expected(load_part, piece):
    eta = lax.dot_general(load_part, piece, (((0,), (0,)), ((), ())), preferred_element_type=F32)
    return jnp.exp(eta)


def shift_kernel(parts, order, axis, chunk, step, *refs):
    pack_ref, counts_hbm = refs[:2]
    arrived = refs[2 : 1 + parts]
    outs = refs[1 + parts : 1 + 2 * parts]
    load_ext, shifted, whole, counts_ref, held, resid_low, grad_shift, counts_sem = refs[1 + 2 * parts :]
    me = lax.axis_index(axis)
    lats, total = grad_shift.shape
    early = held.shape[0]
    neurons = counts_ref.shape[0]
    width = total // parts
    counts_copy = pltpu.make_async_copy(counts_hbm, counts_ref, counts_sem)
    counts_copy.start()

    for k in range(parts):
        start = pl.multiple_of((me ^ k) * width, width)
        whole[:, pl.ds(start, width)] = arrived[order.index(k)][...] if k else pack_ref[0:lats, neurons:].astype(BF16)
    diagonal = lax.broadcasted_iota(jnp.int32, (lats, LANES), 0) == lax.broadcasted_iota(jnp.int32, (lats, LANES), 1)
    spread = jnp.broadcast_to(pack_ref[lats + 1 : lats + 2, 0:LANES], (lats, LANES))
    column = jnp.sum(jnp.where(diagonal, spread, 0.0), axis=1, keepdims=True)
    delay = jnp.broadcast_to(column, (lats, LANES)).astype(jnp.int32)
    length = pack_ref[lats + 2 : lats + 3, 0:1].astype(jnp.int32)
    tiles = [whole[:, j * LANES : (j + 1) * LANES].astype(F32) for j in range(total // LANES)]
    for j, tile in enumerate(shift_tiles(tiles, delay, True)):
        shifted[0:lats, j * LANES : (j + 1) * LANES] = tile.astype(BF16)
    row = lax.broadcasted_iota(jnp.int32, (EXTRA, total), 0)
    shifted[lats:, :] = jnp.where(row < 3, 1.0, 0.0).astype(BF16)

    load_ext[0:lats, :] = pack_ref[0:lats, 0:neurons].astype(BF16)
    bias = pack_ref[lats : lats + 1, 0:neurons]
    high = bias.astype(BF16).astype(F32)
    middle = (bias - high).astype(BF16).astype(F32)
    low = bias - high - middle
    row = lax.broadcasted_iota(jnp.int32, (EXTRA, neurons), 0)
    below = jnp.where(row == 0, high, jnp.where(row == 1, middle, jnp.where(row == 2, low, 0.0)))
    load_ext[lats:, :] = below.astype(BF16)

    blocks = [
        (slice(first, first + chunk), slice(begin, begin + step))
        for first in range(0, neurons, chunk)
        for begin in range(0, total, step)
    ]
    for rows, span in blocks:
        if rows.start < early:
            held[rows, span] = expected(load_ext[:, rows], shifted[:, span])
    counts_copy.wait()
    for rows, span in blocks:
        rate = held[rows, span] if rows.start < early else expected(load_ext[:, rows], shifted[:, span])
        resid_low[rows, span] = (rate - counts_ref[rows, span].astype(F32)).astype(BF16)
    for begin in range(0, total, step):
        span = slice(begin, begin + step)
        grad_shift[:, span] = jnp.dot(load_ext[0:lats, :], resid_low[:, span], preferred_element_type=F32)

    bins = lax.broadcasted_iota(jnp.int32, (1, total), 1)
    tiles = []
    for j in range(total // LANES):
        span = slice(j * LANES, (j + 1) * LANES)
        tiles.append(jnp.where(bins[:, span] < length, grad_shift[:, span], 0.0))
    for j, tile in enumerate(shift_tiles(tiles, delay, False)):
        grad_shift[:, j * LANES : (j + 1) * LANES] = tile
    for k in range(parts):
        start = pl.multiple_of((me ^ k) * width, width)
        outs[k][...] = grad_shift[:, pl.ds(start, width)].astype(outs[k].dtype)


def load_kernel(lats, first, chunk, step, *refs):
    pack_ref, load_ext, shifted, counts_hbm = refs[:4]
    load_hbm, bias_hbm, counts_ref, held, load_ref, bias_ref, sems = refs[-7:]
    count, total = counts_ref.shape
    place = pl.ds(first, count)
    counts_copy = pltpu.make_async_copy(counts_hbm.at[place], counts_ref, sems.at[0])
    counts_copy.start()
    length = pack_ref[lats + 2 : lats + 3, 0:1].astype(jnp.int32)
    bins = lax.broadcasted_iota(jnp.int32, (1, total), 1)
    blocks = [(slice(begin, begin + chunk), range(0, total, step)) for begin in range(0, count, chunk)]
    for rows, starts in blocks:
        for at in starts:
            load_part = load_ext[:, first + rows.start : first + rows.stop]
            held[rows, at : at + step] = expected(load_part, shifted[:, at : at + step])
    counts_copy.wait()
    outward = []
    for index, (rows, starts) in enumerate(blocks):
        sums = jnp.zeros((chunk, LANES), F32)
        grad = jnp.zeros((chunk, lats), F32)
        for at in starts:
            span = slice(at, at + step)
            resid = jnp.where(bins[:, span] < length, held[rows, span] - counts_ref[rows, span].astype(F32), 0.0)
            for j in range(step // LANES):
                sums = sums + resid[:, j * LANES : (j + 1) * LANES]
            grad = grad + lax.dot_general(
                resid.astype(BF16), shifted[0:lats, span], (((1,), (1,)), ((), ())), preferred_element_type=F32
            )
        load_ref[:, rows] = grad.T
        bias_ref[:, rows] = jnp.sum(sums.T, axis=0, keepdims=True)
        place = pl.ds(first + rows.start, chunk)
        outward.append(pltpu.make_async_copy(load_ref.at[:, rows], load_hbm.at[:, place], sems.at[2 * index + 1]))
        outward.append(pltpu.make_async_copy(bias_ref.at[:, rows], bias_hbm.at[:, place], sems.at[2 * index + 2]))
        for copy in outward[-2:]:
            copy.start()
    for copy in outward:
        copy.wait()


def encode(value):
    top = jnp.maximum(jnp.max(jnp.abs(value), axis=0, keepdims=True), 2.0**-100)
    power = jnp.ceil(jnp.log2(top)) - 14.0
    rows = jnp.broadcast_to(power, (8, value.shape[1]))
    return jnp.concatenate([value * jnp.exp2(-power), rows], axis=0).astype(jnp.float16)


def decode(code):
    power = code[-8:-7].astype(F32)
    return code[:-8].astype(F32) * jnp.exp2(power)


def per_device(region_count, neuron_count, counts, latents, loadings, bias, delays, recorded):
    neurons, total = counts.shape[1:]
    lats, width = latents.shape
    chunk, step = 256, 512
    vmem = pl.BlockSpec(memory_space=pltpu.VMEM)
    hbm = pl.BlockSpec(memory_space=pltpu.HBM)
    params = pltpu.CompilerParams(vmem_limit_bytes=52 * 1024 * 1024)

    def swap(value, axis, count, mask):
        return lax.ppermute(value, axis, [(i, i ^ mask) for i in range(count)])

    order = sorted(range(1, neuron_count), key=lambda k: (k != 2, k))
    arrived = [swap(latents, "neuron", neuron_count, k) for k in order]
    row = lax.broadcasted_iota(jnp.int32, (lats + 8, neurons + width), 0)
    lines = jnp.pad(delays, ((lats + 1, 6), (0, neurons + width - lats)))
    lines = jnp.where(row == lats + 2, jnp.broadcast_to(recorded[:, None], lines.shape), lines)
    pack = jnp.pad(bias, ((lats, 7), (0, width))) + lines.astype(F32)
    pack = pack + jnp.pad(loadings[0], ((0, 8), (0, width))).astype(F32)
    pack = pack + jnp.pad(latents, ((0, 8), (neurons, 0))).astype(F32)

    *outs, load_ext, shifted = pl.pallas_call(
        functools.partial(shift_kernel, neuron_count, order, "neuron", chunk, step),
        out_shape=[jax.ShapeDtypeStruct((lats, width), BF16)] * neuron_count
        + [jax.ShapeDtypeStruct((lats + EXTRA, neurons), BF16), jax.ShapeDtypeStruct((lats + EXTRA, total), BF16)],
        in_specs=[vmem, hbm] + [vmem] * (neuron_count - 1),
        out_specs=[vmem] * (neuron_count + 2),
        scratch_shapes=[
            pltpu.VMEM((lats, total), BF16),
            pltpu.VMEM((neurons, total), BF16),
            pltpu.VMEM((4 * chunk, total), F32),
            pltpu.VMEM((neurons, total), BF16),
            pltpu.VMEM((lats, total), F32),
            pltpu.SemaphoreType.DMA,
        ],
        compiler_params=params,
    )(pack, counts[0], *arrived)

    shares = [(0, 3 * chunk), (3 * chunk, neurons - 3 * chunk)]
    made = []

    def make(before):
        first, count = shares.pop(0)
        before, start_load = lax.optimization_barrier((before, load_ext))
        out = pl.pallas_call(
            functools.partial(load_kernel, lats, first, chunk, step),
            out_shape=[jax.ShapeDtypeStruct((lats, neurons), F32), jax.ShapeDtypeStruct((1, neurons), F32)],
            in_specs=[vmem, vmem, vmem, hbm] + [hbm] * len(made),
            out_specs=[hbm, hbm],
            scratch_shapes=[
                pltpu.VMEM((count, total), BF16),
                pltpu.VMEM((count, total), F32),
                pltpu.VMEM((lats, count), F32),
                pltpu.VMEM((1, count), F32),
                pltpu.SemaphoreType.DMA((1 + 2 * (count // chunk),)),
            ],
            input_output_aliases={4 + i: i for i in range(len(made))},
            compiler_params=params,
            cost_estimate=pl.CostEstimate(
                flops=4 * lats * count * total, bytes_accessed=2 * count * total, transcendentals=count * total
            ),
        )(pack, start_load, shifted, counts[0], *made)
        return before, out

    near = min(2, region_count)
    outs, made = make(outs)
    arrived = {(0, 0): outs[0]}
    for flip, k in [(f, k) for f in range(near) for k in range(neuron_count)][1:]:
        pairs = [
            (r * neuron_count + n, (r ^ flip) * neuron_count + (n ^ k))
            for r in range(region_count)
            for n in range(neuron_count)
        ]
        arrived[flip, k] = lax.ppermute(outs[k], ("region", "neuron"), pairs)
    arrived, made = lax.optimization_barrier((arrived, made))
    pair_sums = [
        functools.reduce(jnp.add, [arrived[flip, k].astype(F32) for flip in range(near)])
        for k in range(neuron_count - 1, -1, -1)
    ]
    value = functools.reduce(jnp.add, pair_sums)

    mask = near
    while mask < region_count:
        masks = [mask, 2 * mask, 3 * mask] if 2 * mask < region_count else [mask]
        code = lax.optimization_barrier(encode(value))
        if shares:
            code, made = make(code)
        arrived = [swap(code, "region", region_count, k) for k in masks]
        arrived, made = lax.optimization_barrier((arrived, made))
        value = decode(code) + decode(arrived[0])
        if len(masks) == 3:
            value = value + (decode(arrived[1]) + decode(arrived[2]))
        mask *= 1 + len(masks)
    grad_load, grad_bias = made
    return (value, grad_load[None], grad_bias)


def solution(mesh):
    placed = (
        P("region", "neuron", None),
        P(None, "neuron"),
        P("region", None, "neuron"),
        P("region", "neuron"),
        P("region", None),
        P("region"),
    )
    return jax.shard_map(
        functools.partial(per_device, mesh.shape["region"], mesh.shape["neuron"]),
        mesh=mesh,
        in_specs=placed,
        out_specs=(P(None, "neuron"), P("region", None, "neuron"), P("region", "neuron")),
        check_vma=False,
    )
```

```python
import functools

import jax
import jax.numpy as jnp
from jax import lax
from jax.experimental import pallas as pl
from jax.experimental.pallas import tpu as pltpu
from jax.sharding import PartitionSpec as P

LANES = 128
EXTRA = 16
F32 = jnp.float32
BF16 = jnp.bfloat16


def shift_tiles(tiles, delay, forward):
    lane = lax.broadcasted_iota(jnp.int32, delay.shape, 1)
    source = lane - delay if forward else lane + delay
    inside = source >= 0 if forward else source < LANES
    source = source & (LANES - 1)
    turned = [jnp.take_along_axis(tile, source, axis=1, mode="promise_in_bounds") for tile in tiles]
    nothing = [jnp.zeros_like(tiles[0])]
    others = nothing + turned[:-1] if forward else turned[1:] + nothing
    return [jnp.where(inside, tile, other) for tile, other in zip(turned, others)]


def expected(load_part, piece):
    eta = lax.dot_general(load_part, piece, (((0,), (0,)), ((), ())), preferred_element_type=F32)
    return jnp.exp(eta)


def shift_kernel(parts, order, axis, chunk, step, *refs):
    pack_ref, counts_hbm = refs[:2]
    arrived = refs[2 : 1 + parts]
    outs = refs[1 + parts : 1 + 2 * parts]
    load_ext, shifted, whole, counts_ref, held, resid_low, grad_shift, counts_sem = refs[1 + 2 * parts :]
    me = lax.axis_index(axis)
    lats, total = grad_shift.shape
    early = held.shape[0]
    neurons = counts_ref.shape[0]
    width = total // parts
    counts_copy = pltpu.make_async_copy(counts_hbm, counts_ref, counts_sem)
    counts_copy.start()

    for k in range(parts):
        start = pl.multiple_of((me ^ k) * width, width)
        whole[:, pl.ds(start, width)] = arrived[order.index(k)][...] if k else pack_ref[0:lats, neurons:].astype(BF16)
    diagonal = lax.broadcasted_iota(jnp.int32, (lats, LANES), 0) == lax.broadcasted_iota(jnp.int32, (lats, LANES), 1)
    spread = jnp.broadcast_to(pack_ref[lats + 1 : lats + 2, 0:LANES], (lats, LANES))
    column = jnp.sum(jnp.where(diagonal, spread, 0.0), axis=1, keepdims=True)
    delay = jnp.broadcast_to(column, (lats, LANES)).astype(jnp.int32)
    length = pack_ref[lats + 2 : lats + 3, 0:1].astype(jnp.int32)
    tiles = [whole[:, j * LANES : (j + 1) * LANES].astype(F32) for j in range(total // LANES)]
    for j, tile in enumerate(shift_tiles(tiles, delay, True)):
        shifted[0:lats, j * LANES : (j + 1) * LANES] = tile.astype(BF16)
    row = lax.broadcasted_iota(jnp.int32, (EXTRA, total), 0)
    shifted[lats:, :] = jnp.where(row < 3, 1.0, 0.0).astype(BF16)

    load_ext[0:lats, :] = pack_ref[0:lats, 0:neurons].astype(BF16)
    bias = pack_ref[lats : lats + 1, 0:neurons]
    high = bias.astype(BF16).astype(F32)
    middle = (bias - high).astype(BF16).astype(F32)
    low = bias - high - middle
    row = lax.broadcasted_iota(jnp.int32, (EXTRA, neurons), 0)
    below = jnp.where(row == 0, high, jnp.where(row == 1, middle, jnp.where(row == 2, low, 0.0)))
    load_ext[lats:, :] = below.astype(BF16)

    blocks = [
        (slice(first, first + chunk), slice(begin, begin + step))
        for first in range(0, neurons, chunk)
        for begin in range(0, total, step)
    ]
    for rows, span in blocks:
        if rows.start < early:
            held[rows, span] = expected(load_ext[:, rows], shifted[:, span])
    counts_copy.wait()
    for rows, span in blocks:
        rate = held[rows, span] if rows.start < early else expected(load_ext[:, rows], shifted[:, span])
        resid_low[rows, span] = (rate - counts_ref[rows, span].astype(F32)).astype(BF16)
    for begin in range(0, total, step):
        span = slice(begin, begin + step)
        grad_shift[:, span] = jnp.dot(load_ext[0:lats, :], resid_low[:, span], preferred_element_type=F32)

    bins = lax.broadcasted_iota(jnp.int32, (1, total), 1)
    tiles = []
    for j in range(total // LANES):
        span = slice(j * LANES, (j + 1) * LANES)
        tiles.append(jnp.where(bins[:, span] < length, grad_shift[:, span], 0.0))
    for j, tile in enumerate(shift_tiles(tiles, delay, False)):
        grad_shift[:, j * LANES : (j + 1) * LANES] = tile
    for k in range(parts):
        start = pl.multiple_of((me ^ k) * width, width)
        outs[k][...] = grad_shift[:, pl.ds(start, width)].astype(outs[k].dtype)


def load_kernel(lats, first, chunk, step, *refs):
    pack_ref, load_ext, shifted, counts_hbm = refs[:4]
    load_hbm, bias_hbm, counts_ref, held, load_ref, bias_ref, sems = refs[-7:]
    count, total = counts_ref.shape
    place = pl.ds(first, count)
    counts_copy = pltpu.make_async_copy(counts_hbm.at[place], counts_ref, sems.at[0])
    counts_copy.start()
    length = pack_ref[lats + 2 : lats + 3, 0:1].astype(jnp.int32)
    bins = lax.broadcasted_iota(jnp.int32, (1, total), 1)
    blocks = [(slice(begin, begin + chunk), range(0, total, step)) for begin in range(0, count, chunk)]
    for rows, starts in blocks:
        for at in starts:
            load_part = load_ext[:, first + rows.start : first + rows.stop]
            held[rows, at : at + step] = expected(load_part, shifted[:, at : at + step])
    counts_copy.wait()
    outward = []
    for index, (rows, starts) in enumerate(blocks):
        sums = jnp.zeros((chunk, LANES), F32)
        grad = jnp.zeros((chunk, lats), F32)
        for at in starts:
            span = slice(at, at + step)
            resid = jnp.where(bins[:, span] < length, held[rows, span] - counts_ref[rows, span].astype(F32), 0.0)
            for j in range(step // LANES):
                sums = sums + resid[:, j * LANES : (j + 1) * LANES]
            grad = grad + lax.dot_general(
                resid.astype(BF16), shifted[0:lats, span], (((1,), (1,)), ((), ())), preferred_element_type=F32
            )
        load_ref[:, rows] = grad.T
        bias_ref[:, rows] = jnp.sum(sums.T, axis=0, keepdims=True)
        place = pl.ds(first + rows.start, chunk)
        outward.append(pltpu.make_async_copy(load_ref.at[:, rows], load_hbm.at[:, place], sems.at[2 * index + 1]))
        outward.append(pltpu.make_async_copy(bias_ref.at[:, rows], bias_hbm.at[:, place], sems.at[2 * index + 2]))
        for copy in outward[-2:]:
            copy.start()
    for copy in outward:
        copy.wait()


def encode(value):
    top = jnp.maximum(jnp.max(jnp.abs(value), axis=0, keepdims=True), 2.0**-100)
    power = jnp.ceil(jnp.log2(top)) - 14.0
    rows = jnp.broadcast_to(power, (8, value.shape[1]))
    return jnp.concatenate([value * jnp.exp2(-power), rows], axis=0).astype(jnp.float16)


def decode(code):
    power = code[-8:-7].astype(F32)
    return code[:-8].astype(F32) * jnp.exp2(power)


def per_device(region_count, neuron_count, counts, latents, loadings, bias, delays, recorded):
    neurons, total = counts.shape[1:]
    lats, width = latents.shape
    chunk, step = 256, 512
    vmem = pl.BlockSpec(memory_space=pltpu.VMEM)
    hbm = pl.BlockSpec(memory_space=pltpu.HBM)
    params = pltpu.CompilerParams(vmem_limit_bytes=52 * 1024 * 1024)

    def swap(value, axis, count, mask):
        return lax.ppermute(value, axis, [(i, i ^ mask) for i in range(count)])

    order = sorted(range(1, neuron_count), key=lambda k: (k != 2, k))
    arrived = [swap(latents, "neuron", neuron_count, k) for k in order]
    row = lax.broadcasted_iota(jnp.int32, (lats + 8, neurons + width), 0)
    lines = jnp.pad(delays, ((lats + 1, 6), (0, neurons + width - lats)))
    lines = jnp.where(row == lats + 2, jnp.broadcast_to(recorded[:, None], lines.shape), lines)
    pack = jnp.pad(bias, ((lats, 7), (0, width))) + lines.astype(F32)
    pack = pack + jnp.pad(loadings[0], ((0, 8), (0, width))).astype(F32)
    pack = pack + jnp.pad(latents, ((0, 8), (neurons, 0))).astype(F32)

    *outs, load_ext, shifted = pl.pallas_call(
        functools.partial(shift_kernel, neuron_count, order, "neuron", chunk, step),
        out_shape=[jax.ShapeDtypeStruct((lats, width), BF16 if k > 1 else F32) for k in range(neuron_count)]
        + [jax.ShapeDtypeStruct((lats + EXTRA, neurons), BF16), jax.ShapeDtypeStruct((lats + EXTRA, total), BF16)],
        in_specs=[vmem, hbm] + [vmem] * (neuron_count - 1),
        out_specs=[vmem] * (neuron_count + 2),
        scratch_shapes=[
            pltpu.VMEM((lats, total), BF16),
            pltpu.VMEM((neurons, total), BF16),
            pltpu.VMEM((4 * chunk, total), F32),
            pltpu.VMEM((neurons, total), BF16),
            pltpu.VMEM((lats, total), F32),
            pltpu.SemaphoreType.DMA,
        ],
        compiler_params=params,
    )(pack, counts[0], *arrived)

    shares = [(0, 2 * chunk), (2 * chunk, neurons - 2 * chunk)]
    made = []

    def make(before):
        first, count = shares.pop(0)
        before, start_load = lax.optimization_barrier((before, load_ext))
        out = pl.pallas_call(
            functools.partial(load_kernel, lats, first, chunk, step),
            out_shape=[jax.ShapeDtypeStruct((lats, neurons), F32), jax.ShapeDtypeStruct((1, neurons), F32)],
            in_specs=[vmem, vmem, vmem, hbm] + [hbm] * len(made),
            out_specs=[hbm, hbm],
            scratch_shapes=[
                pltpu.VMEM((count, total), BF16),
                pltpu.VMEM((count, total), F32),
                pltpu.VMEM((lats, count), F32),
                pltpu.VMEM((1, count), F32),
                pltpu.SemaphoreType.DMA((1 + 2 * (count // chunk),)),
            ],
            input_output_aliases={4 + i: i for i in range(len(made))},
            compiler_params=params,
            cost_estimate=pl.CostEstimate(
                flops=4 * lats * count * total, bytes_accessed=2 * count * total, transcendentals=count * total
            ),
        )(pack, start_load, shifted, counts[0], *made)
        return before, out

    outs, made = make(outs)
    arrived = [swap(outs[k], "neuron", neuron_count, k) for k in [*range(2, neuron_count), 1]]
    arrived, made = lax.optimization_barrier((arrived, made))
    value = functools.reduce(jnp.add, [outs[0]] + [block.astype(F32) for block in arrived])
    mask = 1
    while mask < region_count:
        masks = [mask, 2 * mask, 3 * mask] if 2 * mask < region_count else [mask]
        if len(masks) == 3:
            value = lax.reduce_precision(value, 8, 7)
            sent, read = value.astype(BF16), lambda block: block.astype(F32)
        else:
            sent, read = lax.optimization_barrier(encode(value)), decode
            value = decode(sent)
        if shares:
            (value, sent), made = make((value, sent))
        arrived = [swap(sent, "region", region_count, k) for k in masks]
        arrived, made = lax.optimization_barrier((arrived, made))
        value = value + read(arrived[0])
        if len(masks) == 3:
            value = value + (read(arrived[1]) + read(arrived[2]))
        mask *= 1 + len(masks)
    grad_load, grad_bias = made
    return (value, grad_load[None], grad_bias)


def solution(mesh):
    placed = (
        P("region", "neuron", None),
        P(None, "neuron"),
        P("region", None, "neuron"),
        P("region", "neuron"),
        P("region", None),
        P("region"),
    )
    return jax.shard_map(
        functools.partial(per_device, mesh.shape["region"], mesh.shape["neuron"]),
        mesh=mesh,
        in_specs=placed,
        out_specs=(P(None, "neuron"), P("region", None, "neuron"), P("region", "neuron")),
        check_vma=False,
    )
```

```python
import functools

import jax
import jax.numpy as jnp
from jax import lax
from jax.experimental import pallas as pl
from jax.experimental.pallas import tpu as pltpu
from jax.sharding import PartitionSpec as P

LANES = 128
EXTRA = 16
F32 = jnp.float32
BF16 = jnp.bfloat16


def shift_tiles(tiles, delay, forward):
    lane = lax.broadcasted_iota(jnp.int32, delay.shape, 1)
    source = lane - delay if forward else lane + delay
    inside = source >= 0 if forward else source < LANES
    source = source & (LANES - 1)
    turned = [jnp.take_along_axis(tile, source, axis=1, mode="promise_in_bounds") for tile in tiles]
    nothing = [jnp.zeros_like(tiles[0])]
    others = nothing + turned[:-1] if forward else turned[1:] + nothing
    return [jnp.where(inside, tile, other) for tile, other in zip(turned, others)]


def expected(load_part, piece):
    eta = lax.dot_general(load_part, piece, (((0,), (0,)), ((), ())), preferred_element_type=F32)
    return jnp.exp(eta)


def shift_kernel(parts, order, axis, chunk, step, *refs):
    pack_ref, counts_hbm = refs[:2]
    arrived = refs[2 : 1 + parts]
    outs = refs[1 + parts : 1 + 2 * parts]
    load_ext, shifted, whole, counts_ref, held, resid_low, grad_shift, counts_sems = refs[1 + 2 * parts :]
    me = lax.axis_index(axis)
    lats, total = grad_shift.shape
    early = held.shape[0]
    neurons = counts_ref.shape[0]
    width = total // parts
    cut = early - chunk
    places = [pl.ds(0, cut), pl.ds(cut, neurons - cut)]
    copies = [
        pltpu.make_async_copy(counts_hbm.at[place], counts_ref.at[place], counts_sems.at[index])
        for index, place in enumerate(places)
    ]
    copies[0].start()

    for k in range(parts):
        start = pl.multiple_of((me ^ k) * width, width)
        whole[:, pl.ds(start, width)] = arrived[order.index(k)][...] if k else pack_ref[0:lats, neurons:].astype(BF16)
    diagonal = lax.broadcasted_iota(jnp.int32, (lats, LANES), 0) == lax.broadcasted_iota(jnp.int32, (lats, LANES), 1)
    spread = jnp.broadcast_to(pack_ref[lats + 1 : lats + 2, 0:LANES], (lats, LANES))
    column = jnp.sum(jnp.where(diagonal, spread, 0.0), axis=1, keepdims=True)
    delay = jnp.broadcast_to(column, (lats, LANES)).astype(jnp.int32)
    length = pack_ref[lats + 2 : lats + 3, 0:1].astype(jnp.int32)
    tiles = [whole[:, j * LANES : (j + 1) * LANES].astype(F32) for j in range(total // LANES)]
    for j, tile in enumerate(shift_tiles(tiles, delay, True)):
        shifted[0:lats, j * LANES : (j + 1) * LANES] = tile.astype(BF16)
    row = lax.broadcasted_iota(jnp.int32, (EXTRA, total), 0)
    shifted[lats:, :] = jnp.where(row < 3, 1.0, 0.0).astype(BF16)

    copies[1].start()

    load_ext[0:lats, :] = pack_ref[0:lats, 0:neurons].astype(BF16)
    bias = pack_ref[lats : lats + 1, 0:neurons]
    high = bias.astype(BF16).astype(F32)
    middle = (bias - high).astype(BF16).astype(F32)
    low = bias - high - middle
    row = lax.broadcasted_iota(jnp.int32, (EXTRA, neurons), 0)
    below = jnp.where(row == 0, high, jnp.where(row == 1, middle, jnp.where(row == 2, low, 0.0)))
    load_ext[lats:, :] = below.astype(BF16)

    blocks = [
        (slice(first, first + chunk), slice(begin, begin + step))
        for first in range(0, neurons, chunk)
        for begin in range(0, total, step)
    ]
    for rows, span in blocks:
        if rows.start < early:
            held[rows, span] = expected(load_ext[:, rows], shifted[:, span])
    spans = [slice(begin, begin + step) for begin in range(0, total, step)]
    for copy, place in zip(copies, [slice(0, cut), slice(cut, neurons)]):
        copy.wait()
        for rows, span in blocks:
            if place.start <= rows.start < place.stop:
                rate = held[rows, span] if rows.start < early else expected(load_ext[:, rows], shifted[:, span])
                resid_low[rows, span] = (rate - counts_ref[rows, span].astype(F32)).astype(BF16)
        for span in spans:
            part = jnp.dot(load_ext[0:lats, place], resid_low[place, span], preferred_element_type=F32)
            grad_shift[:, span] = grad_shift[:, span] + part if place.start else part

    bins = lax.broadcasted_iota(jnp.int32, (1, total), 1)
    tiles = []
    for j in range(total // LANES):
        span = slice(j * LANES, (j + 1) * LANES)
        tiles.append(jnp.where(bins[:, span] < length, grad_shift[:, span], 0.0))
    for j, tile in enumerate(shift_tiles(tiles, delay, False)):
        grad_shift[:, j * LANES : (j + 1) * LANES] = tile
    for k in range(parts):
        start = pl.multiple_of((me ^ k) * width, width)
        outs[k][...] = grad_shift[:, pl.ds(start, width)].astype(outs[k].dtype)


def load_kernel(lats, first, chunk, step, *refs):
    pack_ref, load_ext, shifted, counts_hbm = refs[:4]
    load_hbm, bias_hbm, counts_ref, held, load_ref, bias_ref, sems = refs[-7:]
    count, total = counts_ref.shape
    place = pl.ds(first, count)
    counts_copy = pltpu.make_async_copy(counts_hbm.at[place], counts_ref, sems.at[0])
    counts_copy.start()
    length = pack_ref[lats + 2 : lats + 3, 0:1].astype(jnp.int32)
    bins = lax.broadcasted_iota(jnp.int32, (1, total), 1)
    blocks = [(slice(begin, begin + chunk), range(0, total, step)) for begin in range(0, count, chunk)]

    def rate(rows, span):
        return expected(load_ext[:, first + rows.start : first + rows.stop], shifted[:, span])

    for rows, starts in blocks[:-1]:
        for at in starts:
            held[rows, at : at + step] = rate(rows, slice(at, at + step))
    counts_copy.wait()
    outward = []
    for index, (rows, starts) in enumerate(blocks):
        sums = jnp.zeros((chunk, LANES), F32)
        grad = jnp.zeros((chunk, lats), F32)
        for at in starts:
            span = slice(at, at + step)
            made = held[rows, span] if index < len(blocks) - 1 else rate(rows, span)
            resid = jnp.where(bins[:, span] < length, made - counts_ref[rows, span].astype(F32), 0.0)
            for j in range(step // LANES):
                sums = sums + resid[:, j * LANES : (j + 1) * LANES]
            grad = grad + lax.dot_general(
                resid.astype(BF16), shifted[0:lats, span], (((1,), (1,)), ((), ())), preferred_element_type=F32
            )
        load_ref[:, rows] = grad.T
        bias_ref[:, rows] = jnp.sum(sums.T, axis=0, keepdims=True)
        place = pl.ds(first + rows.start, chunk)
        outward.append(pltpu.make_async_copy(load_ref.at[:, rows], load_hbm.at[:, place], sems.at[2 * index + 1]))
        outward.append(pltpu.make_async_copy(bias_ref.at[:, rows], bias_hbm.at[:, place], sems.at[2 * index + 2]))
        for copy in outward[-2:]:
            copy.start()
    for copy in outward:
        copy.wait()


def encode(value):
    top = jnp.maximum(jnp.max(jnp.abs(value), axis=0, keepdims=True), 2.0**-100)
    power = jnp.ceil(jnp.log2(top)) - 14.0
    rows = jnp.broadcast_to(power, (8, value.shape[1]))
    return jnp.concatenate([value * jnp.exp2(-power), rows], axis=0).astype(jnp.float16)


def decode(code):
    power = code[-8:-7].astype(F32)
    return code[:-8].astype(F32) * jnp.exp2(power)


def per_device(region_count, neuron_count, counts, latents, loadings, bias, delays, recorded):
    neurons, total = counts.shape[1:]
    lats, width = latents.shape
    chunk, step = 256, 512
    vmem = pl.BlockSpec(memory_space=pltpu.VMEM)
    hbm = pl.BlockSpec(memory_space=pltpu.HBM)
    params = pltpu.CompilerParams(vmem_limit_bytes=52 * 1024 * 1024)

    def swap(value, axis, count, mask):
        return lax.ppermute(value, axis, [(i, i ^ mask) for i in range(count)])

    order = sorted(range(1, neuron_count), key=lambda k: (k != 2, k))
    arrived = [swap(latents, "neuron", neuron_count, k) for k in order]
    row = lax.broadcasted_iota(jnp.int32, (lats + 8, neurons + width), 0)
    lines = jnp.pad(delays, ((lats + 1, 6), (0, neurons + width - lats)))
    lines = jnp.where(row == lats + 2, jnp.broadcast_to(recorded[:, None], lines.shape), lines)
    pack = jnp.pad(bias, ((lats, 7), (0, width))) + lines.astype(F32)
    pack = pack + jnp.pad(loadings[0], ((0, 8), (0, width))).astype(F32)
    pack = pack + jnp.pad(latents, ((0, 8), (neurons, 0))).astype(F32)

    *outs, load_ext, shifted = pl.pallas_call(
        functools.partial(shift_kernel, neuron_count, order, "neuron", chunk, step),
        out_shape=[jax.ShapeDtypeStruct((lats, width), BF16 if k > 1 else F32) for k in range(neuron_count)]
        + [jax.ShapeDtypeStruct((lats + EXTRA, neurons), BF16), jax.ShapeDtypeStruct((lats + EXTRA, total), BF16)],
        in_specs=[vmem, hbm] + [vmem] * (neuron_count - 1),
        out_specs=[vmem] * (neuron_count + 2),
        scratch_shapes=[
            pltpu.VMEM((lats, total), BF16),
            pltpu.VMEM((neurons, total), BF16),
            pltpu.VMEM((4 * chunk, total), F32),
            pltpu.VMEM((neurons, total), BF16),
            pltpu.VMEM((lats, total), F32),
            pltpu.SemaphoreType.DMA((2,)),
        ],
        compiler_params=params,
    )(pack, counts[0], *arrived)

    shares = [(0, 2 * chunk), (2 * chunk, neurons - 2 * chunk)]
    made = []

    def make(before):
        first, count = shares.pop(0)
        before, start_load = lax.optimization_barrier((before, load_ext))
        out = pl.pallas_call(
            functools.partial(load_kernel, lats, first, chunk, step),
            out_shape=[jax.ShapeDtypeStruct((lats, neurons), F32), jax.ShapeDtypeStruct((1, neurons), F32)],
            in_specs=[vmem, vmem, vmem, hbm] + [hbm] * len(made),
            out_specs=[hbm, hbm],
            scratch_shapes=[
                pltpu.VMEM((count, total), BF16),
                pltpu.VMEM((count, total), F32),
                pltpu.VMEM((lats, count), F32),
                pltpu.VMEM((1, count), F32),
                pltpu.SemaphoreType.DMA((1 + 2 * (count // chunk),)),
            ],
            input_output_aliases={4 + i: i for i in range(len(made))},
            compiler_params=params,
            cost_estimate=pl.CostEstimate(
                flops=4 * lats * count * total, bytes_accessed=2 * count * total, transcendentals=count * total
            ),
        )(pack, start_load, shifted, counts[0], *made)
        return before, out

    outs, made = make(outs)
    arrived = [swap(outs[k], "neuron", neuron_count, k) for k in [*range(2, neuron_count), 1]]
    arrived, made = lax.optimization_barrier((arrived, made))
    value = functools.reduce(jnp.add, [outs[0]] + [block.astype(F32) for block in arrived])
    mask = 1
    while mask < region_count:
        masks = [mask, 2 * mask, 3 * mask] if 2 * mask < region_count else [mask]
        if len(masks) == 3:
            value = lax.reduce_precision(value, 8, 7)
            sent, read = value.astype(BF16), lambda block: block.astype(F32)
        else:
            sent, read = lax.optimization_barrier(encode(value)), decode
            value = decode(sent)
        if shares:
            (value, sent), made = make((value, sent))
        arrived = [swap(sent, "region", region_count, k) for k in masks]
        arrived, made = lax.optimization_barrier((arrived, made))
        value = value + read(arrived[0])
        if len(masks) == 3:
            value = value + (read(arrived[1]) + read(arrived[2]))
        mask *= 1 + len(masks)
    grad_load, grad_bias = made
    return (value, grad_load[None], grad_bias)


def solution(mesh):
    placed = (
        P("region", "neuron", None),
        P(None, "neuron"),
        P("region", None, "neuron"),
        P("region", "neuron"),
        P("region", None),
        P("region"),
    )
    return jax.shard_map(
        functools.partial(per_device, mesh.shape["region"], mesh.shape["neuron"]),
        mesh=mesh,
        in_specs=placed,
        out_specs=(P(None, "neuron"), P("region", None, "neuron"), P("region", "neuron")),
        check_vma=False,
    )
```

```python
import functools

import jax
import jax.numpy as jnp
from jax import lax
from jax.experimental import pallas as pl
from jax.experimental.pallas import tpu as pltpu
from jax.sharding import PartitionSpec as P

LANES = 128
EXTRA = 16
F32 = jnp.float32
BF16 = jnp.bfloat16


def shift_tiles(tiles, delay, forward):
    lane = lax.broadcasted_iota(jnp.int32, delay.shape, 1)
    source = lane - delay if forward else lane + delay
    inside = source >= 0 if forward else source < LANES
    source = source & (LANES - 1)
    turned = [jnp.take_along_axis(tile, source, axis=1, mode="promise_in_bounds") for tile in tiles]
    nothing = [jnp.zeros_like(tiles[0])]
    others = nothing + turned[:-1] if forward else turned[1:] + nothing
    return [jnp.where(inside, tile, other) for tile, other in zip(turned, others)]


def expected(load_part, piece):
    eta = lax.dot_general(load_part, piece, (((0,), (0,)), ((), ())), preferred_element_type=F32)
    return jnp.exp(eta)


def shift_kernel(parts, order, axis, chunk, step, *refs):
    pack_ref, counts_hbm = refs[:2]
    arrived = refs[2 : 1 + parts]
    outs = refs[1 + parts : 1 + 2 * parts]
    load_ext, shifted, whole, counts_ref, held, resid_low, grad_shift, counts_sems = refs[1 + 2 * parts :]
    me = lax.axis_index(axis)
    lats, total = grad_shift.shape
    early = held.shape[0]
    neurons = counts_ref.shape[0]
    width = total // parts
    cut = 2 * chunk
    places = [pl.ds(0, cut), pl.ds(cut, neurons - cut)]
    copies = [
        pltpu.make_async_copy(counts_hbm.at[place], counts_ref.at[place], counts_sems.at[index])
        for index, place in enumerate(places)
    ]
    copies[0].start()

    for k in range(parts):
        start = pl.multiple_of((me ^ k) * width, width)
        whole[:, pl.ds(start, width)] = arrived[order.index(k)][...] if k else pack_ref[0:lats, neurons:].astype(BF16)
    diagonal = lax.broadcasted_iota(jnp.int32, (lats, LANES), 0) == lax.broadcasted_iota(jnp.int32, (lats, LANES), 1)
    spread = jnp.broadcast_to(pack_ref[lats + 1 : lats + 2, 0:LANES], (lats, LANES))
    column = jnp.sum(jnp.where(diagonal, spread, 0.0), axis=1, keepdims=True)
    delay = jnp.broadcast_to(column, (lats, LANES)).astype(jnp.int32)
    length = pack_ref[lats + 2 : lats + 3, 0:1].astype(jnp.int32)
    tiles = [whole[:, j * LANES : (j + 1) * LANES].astype(F32) for j in range(total // LANES)]
    for j, tile in enumerate(shift_tiles(tiles, delay, True)):
        shifted[0:lats, j * LANES : (j + 1) * LANES] = tile.astype(BF16)
    row = lax.broadcasted_iota(jnp.int32, (EXTRA, total), 0)
    shifted[lats:, :] = jnp.where(row < 3, 1.0, 0.0).astype(BF16)

    copies[1].start()

    load_ext[0:lats, :] = pack_ref[0:lats, 0:neurons].astype(BF16)
    bias = pack_ref[lats : lats + 1, 0:neurons]
    high = bias.astype(BF16).astype(F32)
    middle = (bias - high).astype(BF16).astype(F32)
    low = bias - high - middle
    row = lax.broadcasted_iota(jnp.int32, (EXTRA, neurons), 0)
    below = jnp.where(row == 0, high, jnp.where(row == 1, middle, jnp.where(row == 2, low, 0.0)))
    load_ext[lats:, :] = below.astype(BF16)

    blocks = [
        (slice(first, first + chunk), slice(begin, begin + step))
        for first in range(0, neurons, chunk)
        for begin in range(0, total, step)
    ]
    for rows, span in blocks:
        if rows.start < early:
            held[rows, span] = expected(load_ext[:, rows], shifted[:, span])
    spans = [slice(begin, begin + step) for begin in range(0, total, step)]
    for copy, place in zip(copies, [slice(0, cut), slice(cut, neurons)]):
        copy.wait()
        for rows, span in blocks:
            if place.start <= rows.start < place.stop:
                rate = held[rows, span] if rows.start < early else expected(load_ext[:, rows], shifted[:, span])
                resid_low[rows, span] = (rate - counts_ref[rows, span].astype(F32)).astype(BF16)
        for span in spans:
            part = jnp.dot(load_ext[0:lats, place], resid_low[place, span], preferred_element_type=F32)
            grad_shift[:, span] = grad_shift[:, span] + part if place.start else part

    bins = lax.broadcasted_iota(jnp.int32, (1, total), 1)
    tiles = []
    for j in range(total // LANES):
        span = slice(j * LANES, (j + 1) * LANES)
        tiles.append(jnp.where(bins[:, span] < length, grad_shift[:, span], 0.0))
    for j, tile in enumerate(shift_tiles(tiles, delay, False)):
        grad_shift[:, j * LANES : (j + 1) * LANES] = tile
    for k in range(parts):
        start = pl.multiple_of((me ^ k) * width, width)
        outs[k][...] = grad_shift[:, pl.ds(start, width)].astype(outs[k].dtype)


def load_kernel(lats, first, chunk, step, *refs):
    pack_ref, load_ext, shifted, counts_hbm = refs[:4]
    load_hbm, bias_hbm, counts_ref, held, load_ref, bias_ref, sems = refs[-7:]
    count, total = counts_ref.shape
    place = pl.ds(first, count)
    counts_copy = pltpu.make_async_copy(counts_hbm.at[place], counts_ref, sems.at[0])
    counts_copy.start()
    length = pack_ref[lats + 2 : lats + 3, 0:1].astype(jnp.int32)
    bins = lax.broadcasted_iota(jnp.int32, (1, total), 1)
    blocks = [(slice(begin, begin + chunk), range(0, total, step)) for begin in range(0, count, chunk)]

    def rate(rows, span):
        return expected(load_ext[:, first + rows.start : first + rows.stop], shifted[:, span])

    early = blocks[:-1] if len(blocks) > 2 else blocks
    for rows, starts in early:
        for at in starts:
            held[rows, at : at + step] = rate(rows, slice(at, at + step))
    counts_copy.wait()
    outward = []
    for index, (rows, starts) in enumerate(blocks):
        sums = jnp.zeros((chunk, LANES), F32)
        grad = jnp.zeros((chunk, lats), F32)
        for at in starts:
            span = slice(at, at + step)
            made = held[rows, span] if index < len(early) else rate(rows, span)
            resid = jnp.where(bins[:, span] < length, made - counts_ref[rows, span].astype(F32), 0.0)
            for j in range(step // LANES):
                sums = sums + resid[:, j * LANES : (j + 1) * LANES]
            grad = grad + lax.dot_general(
                resid.astype(BF16), shifted[0:lats, span], (((1,), (1,)), ((), ())), preferred_element_type=F32
            )
        load_ref[:, rows] = grad.T
        bias_ref[:, rows] = jnp.sum(sums.T, axis=0, keepdims=True)
        place = pl.ds(first + rows.start, chunk)
        outward.append(pltpu.make_async_copy(load_ref.at[:, rows], load_hbm.at[:, place], sems.at[2 * index + 1]))
        outward.append(pltpu.make_async_copy(bias_ref.at[:, rows], bias_hbm.at[:, place], sems.at[2 * index + 2]))
        for copy in outward[-2:]:
            copy.start()
    for copy in outward:
        copy.wait()


def encode(value):
    top = jnp.maximum(jnp.max(jnp.abs(value), axis=0, keepdims=True), 2.0**-100)
    power = jnp.ceil(jnp.log2(top)) - 14.0
    rows = jnp.broadcast_to(power, (8, value.shape[1]))
    return jnp.concatenate([value * jnp.exp2(-power), rows], axis=0).astype(jnp.float16)


def decode(code):
    power = code[-8:-7].astype(F32)
    return code[:-8].astype(F32) * jnp.exp2(power)


def per_device(region_count, neuron_count, counts, latents, loadings, bias, delays, recorded):
    neurons, total = counts.shape[1:]
    lats, width = latents.shape
    chunk, step = 256, 512
    vmem = pl.BlockSpec(memory_space=pltpu.VMEM)
    hbm = pl.BlockSpec(memory_space=pltpu.HBM)
    params = pltpu.CompilerParams(vmem_limit_bytes=52 * 1024 * 1024)

    def swap(value, axis, count, mask):
        return lax.ppermute(value, axis, [(i, i ^ mask) for i in range(count)])

    order = sorted(range(1, neuron_count), key=lambda k: (k != 2, k))
    arrived = [swap(latents, "neuron", neuron_count, k) for k in order]
    row = lax.broadcasted_iota(jnp.int32, (lats + 8, neurons + width), 0)
    lines = jnp.pad(delays, ((lats + 1, 6), (0, neurons + width - lats)))
    lines = jnp.where(row == lats + 2, jnp.broadcast_to(recorded[:, None], lines.shape), lines)
    pack = jnp.pad(bias, ((lats, 7), (0, width))) + lines.astype(F32)
    pack = pack + jnp.pad(loadings[0], ((0, 8), (0, width))).astype(F32)
    pack = pack + jnp.pad(latents, ((0, 8), (neurons, 0))).astype(F32)

    *outs, load_ext, shifted = pl.pallas_call(
        functools.partial(shift_kernel, neuron_count, order, "neuron", chunk, step),
        out_shape=[jax.ShapeDtypeStruct((lats, width), BF16 if k > 1 else F32) for k in range(neuron_count)]
        + [jax.ShapeDtypeStruct((lats + EXTRA, neurons), BF16), jax.ShapeDtypeStruct((lats + EXTRA, total), BF16)],
        in_specs=[vmem, hbm] + [vmem] * (neuron_count - 1),
        out_specs=[vmem] * (neuron_count + 2),
        scratch_shapes=[
            pltpu.VMEM((lats, total), BF16),
            pltpu.VMEM((neurons, total), BF16),
            pltpu.VMEM((3 * chunk, total), F32),
            pltpu.VMEM((neurons, total), BF16),
            pltpu.VMEM((lats, total), F32),
            pltpu.SemaphoreType.DMA((2,)),
        ],
        compiler_params=params,
    )(pack, counts[0], *arrived)

    shares = [(0, 2 * chunk), (2 * chunk, neurons - 2 * chunk)]
    made = []

    def make(before):
        first, count = shares.pop(0)
        before, start_load = lax.optimization_barrier((before, load_ext))
        out = pl.pallas_call(
            functools.partial(load_kernel, lats, first, chunk, step),
            out_shape=[jax.ShapeDtypeStruct((lats, neurons), F32), jax.ShapeDtypeStruct((1, neurons), F32)],
            in_specs=[vmem, vmem, vmem, hbm] + [hbm] * len(made),
            out_specs=[hbm, hbm],
            scratch_shapes=[
                pltpu.VMEM((count, total), BF16),
                pltpu.VMEM((count, total), F32),
                pltpu.VMEM((lats, count), F32),
                pltpu.VMEM((1, count), F32),
                pltpu.SemaphoreType.DMA((1 + 2 * (count // chunk),)),
            ],
            input_output_aliases={4 + i: i for i in range(len(made))},
            compiler_params=params,
            cost_estimate=pl.CostEstimate(
                flops=4 * lats * count * total, bytes_accessed=2 * count * total, transcendentals=count * total
            ),
        )(pack, start_load, shifted, counts[0], *made)
        return before, out

    outs, made = make(outs)
    arrived = [swap(outs[k], "neuron", neuron_count, k) for k in [*range(2, neuron_count), 1]]
    arrived, made = lax.optimization_barrier((arrived, made))
    value = functools.reduce(jnp.add, [outs[0]] + [block.astype(F32) for block in arrived])
    mask = 1
    while mask < region_count:
        masks = [mask, 2 * mask, 3 * mask] if 2 * mask < region_count else [mask]
        if len(masks) == 3:
            value = lax.reduce_precision(value, 8, 7)
            sent, read = value.astype(BF16), lambda block: block.astype(F32)
        else:
            sent, read = lax.optimization_barrier(encode(value)), decode
            value = decode(sent)
        if shares:
            (value, sent), made = make((value, sent))
        arrived = [swap(sent, "region", region_count, k) for k in masks]
        arrived, made = lax.optimization_barrier((arrived, made))
        value = value + read(arrived[0])
        if len(masks) == 3:
            value = value + (read(arrived[1]) + read(arrived[2]))
        mask *= 1 + len(masks)
    grad_load, grad_bias = made
    return (value, grad_load[None], grad_bias)


def solution(mesh):
    placed = (
        P("region", "neuron", None),
        P(None, "neuron"),
        P("region", None, "neuron"),
        P("region", "neuron"),
        P("region", None),
        P("region"),
    )
    return jax.shard_map(
        functools.partial(per_device, mesh.shape["region"], mesh.shape["neuron"]),
        mesh=mesh,
        in_specs=placed,
        out_specs=(P(None, "neuron"), P("region", None, "neuron"), P("region", "neuron")),
        check_vma=False,
    )
```

```python
import functools

import jax
import jax.numpy as jnp
from jax import lax
from jax.experimental import pallas as pl
from jax.experimental.pallas import tpu as pltpu
from jax.sharding import PartitionSpec as P

LANES = 128
EXTRA = 16
F32 = jnp.float32
BF16 = jnp.bfloat16


def shift_tiles(tiles, delay, forward):
    lane = lax.broadcasted_iota(jnp.int32, delay.shape, 1)
    source = lane - delay if forward else lane + delay
    inside = source >= 0 if forward else source < LANES
    source = source & (LANES - 1)
    turned = [jnp.take_along_axis(tile, source, axis=1, mode="promise_in_bounds") for tile in tiles]
    nothing = [jnp.zeros_like(tiles[0])]
    others = nothing + turned[:-1] if forward else turned[1:] + nothing
    return [jnp.where(inside, tile, other) for tile, other in zip(turned, others)]


def expected(load_part, piece):
    eta = lax.dot_general(load_part, piece, (((0,), (0,)), ((), ())), preferred_element_type=F32)
    return jnp.exp(eta)


def shift_kernel(parts, order, axis, chunk, step, *refs):
    pack_ref, counts_hbm = refs[:2]
    arrived = refs[2 : 1 + parts]
    outs = refs[1 + parts : 1 + 2 * parts]
    load_ext, shifted, whole, counts_ref, held, resid_low, grad_shift, counts_sems = refs[1 + 2 * parts :]
    me = lax.axis_index(axis)
    lats, total = grad_shift.shape
    early = held.shape[0]
    neurons = counts_ref.shape[0]
    width = total // parts
    cut = 3 * chunk
    places = [pl.ds(0, cut), pl.ds(cut, neurons - cut)]
    copies = [
        pltpu.make_async_copy(counts_hbm.at[place], counts_ref.at[place], counts_sems.at[index])
        for index, place in enumerate(places)
    ]
    copies[0].start()

    for k in range(parts):
        start = pl.multiple_of((me ^ k) * width, width)
        whole[:, pl.ds(start, width)] = arrived[order.index(k)][...] if k else pack_ref[0:lats, neurons:].astype(BF16)
    diagonal = lax.broadcasted_iota(jnp.int32, (lats, LANES), 0) == lax.broadcasted_iota(jnp.int32, (lats, LANES), 1)
    spread = jnp.broadcast_to(pack_ref[lats + 1 : lats + 2, 0:LANES], (lats, LANES))
    column = jnp.sum(jnp.where(diagonal, spread, 0.0), axis=1, keepdims=True)
    delay = jnp.broadcast_to(column, (lats, LANES)).astype(jnp.int32)
    length = pack_ref[lats + 2 : lats + 3, 0:1].astype(jnp.int32)
    tiles = [whole[:, j * LANES : (j + 1) * LANES].astype(F32) for j in range(total // LANES)]
    for j, tile in enumerate(shift_tiles(tiles, delay, True)):
        shifted[0:lats, j * LANES : (j + 1) * LANES] = tile.astype(BF16)
    row = lax.broadcasted_iota(jnp.int32, (EXTRA, total), 0)
    shifted[lats:, :] = jnp.where(row < 3, 1.0, 0.0).astype(BF16)

    copies[1].start()

    load_ext[0:lats, :] = pack_ref[0:lats, 0:neurons].astype(BF16)
    bias = pack_ref[lats : lats + 1, 0:neurons]
    high = bias.astype(BF16).astype(F32)
    middle = (bias - high).astype(BF16).astype(F32)
    low = bias - high - middle
    row = lax.broadcasted_iota(jnp.int32, (EXTRA, neurons), 0)
    below = jnp.where(row == 0, high, jnp.where(row == 1, middle, jnp.where(row == 2, low, 0.0)))
    load_ext[lats:, :] = below.astype(BF16)

    blocks = [
        (slice(first, first + chunk), slice(begin, begin + step))
        for first in range(0, neurons, chunk)
        for begin in range(0, total, step)
    ]
    for rows, span in blocks:
        if rows.start < early:
            held[rows, span] = expected(load_ext[:, rows], shifted[:, span])
    spans = [slice(begin, begin + step) for begin in range(0, total, step)]
    for copy, place in zip(copies, [slice(0, cut), slice(cut, neurons)]):
        copy.wait()
        for rows, span in blocks:
            if place.start <= rows.start < place.stop:
                rate = held[rows, span] if rows.start < early else expected(load_ext[:, rows], shifted[:, span])
                resid_low[rows, span] = (rate - counts_ref[rows, span].astype(F32)).astype(BF16)
        for span in spans:
            part = jnp.dot(load_ext[0:lats, place], resid_low[place, span], preferred_element_type=F32)
            grad_shift[:, span] = grad_shift[:, span] + part if place.start else part

    bins = lax.broadcasted_iota(jnp.int32, (1, total), 1)
    tiles = []
    for j in range(total // LANES):
        span = slice(j * LANES, (j + 1) * LANES)
        tiles.append(jnp.where(bins[:, span] < length, grad_shift[:, span], 0.0))
    for j, tile in enumerate(shift_tiles(tiles, delay, False)):
        grad_shift[:, j * LANES : (j + 1) * LANES] = tile
    for k in range(parts):
        start = pl.multiple_of((me ^ k) * width, width)
        outs[k][...] = grad_shift[:, pl.ds(start, width)].astype(outs[k].dtype)


def load_kernel(lats, first, chunk, step, *refs):
    pack_ref, load_ext, shifted, counts_hbm = refs[:4]
    load_hbm, bias_hbm, counts_ref, held, load_ref, bias_ref, sems = refs[-7:]
    count, total = counts_ref.shape
    place = pl.ds(first, count)
    counts_copy = pltpu.make_async_copy(counts_hbm.at[place], counts_ref, sems.at[0])
    counts_copy.start()
    length = pack_ref[lats + 2 : lats + 3, 0:1].astype(jnp.int32)
    bins = lax.broadcasted_iota(jnp.int32, (1, total), 1)
    blocks = [(slice(begin, begin + chunk), range(0, total, step)) for begin in range(0, count, chunk)]

    def rate(rows, span):
        return expected(load_ext[:, first + rows.start : first + rows.stop], shifted[:, span])

    early = blocks[:-1] if len(blocks) > 2 else blocks
    for rows, starts in early:
        for at in starts:
            held[rows, at : at + step] = rate(rows, slice(at, at + step))
    counts_copy.wait()
    outward = []
    for index, (rows, starts) in enumerate(blocks):
        sums = jnp.zeros((chunk, LANES), F32)
        grad = jnp.zeros((chunk, lats), F32)
        for at in starts:
            span = slice(at, at + step)
            made = held[rows, span] if index < len(early) else rate(rows, span)
            resid = jnp.where(bins[:, span] < length, made - counts_ref[rows, span].astype(F32), 0.0)
            for j in range(step // LANES):
                sums = sums + resid[:, j * LANES : (j + 1) * LANES]
            grad = grad + lax.dot_general(
                resid.astype(BF16), shifted[0:lats, span], (((1,), (1,)), ((), ())), preferred_element_type=F32
            )
        load_ref[:, rows] = grad.T
        bias_ref[:, rows] = jnp.sum(sums.T, axis=0, keepdims=True)
        place = pl.ds(first + rows.start, chunk)
        outward.append(pltpu.make_async_copy(load_ref.at[:, rows], load_hbm.at[:, place], sems.at[2 * index + 1]))
        outward.append(pltpu.make_async_copy(bias_ref.at[:, rows], bias_hbm.at[:, place], sems.at[2 * index + 2]))
        for copy in outward[-2:]:
            copy.start()
    for copy in outward:
        copy.wait()


def encode(value):
    top = jnp.maximum(jnp.max(jnp.abs(value), axis=0, keepdims=True), 2.0**-100)
    power = jnp.ceil(jnp.log2(top)) - 14.0
    rows = jnp.broadcast_to(power, (8, value.shape[1]))
    return jnp.concatenate([value * jnp.exp2(-power), rows], axis=0).astype(jnp.float16)


def decode(code):
    power = code[-8:-7].astype(F32)
    return code[:-8].astype(F32) * jnp.exp2(power)


def per_device(region_count, neuron_count, counts, latents, loadings, bias, delays, recorded):
    neurons, total = counts.shape[1:]
    lats, width = latents.shape
    chunk, step = 256, 512
    vmem = pl.BlockSpec(memory_space=pltpu.VMEM)
    hbm = pl.BlockSpec(memory_space=pltpu.HBM)
    params = pltpu.CompilerParams(vmem_limit_bytes=52 * 1024 * 1024)

    def swap(value, axis, count, mask):
        return lax.ppermute(value, axis, [(i, i ^ mask) for i in range(count)])

    order = sorted(range(1, neuron_count), key=lambda k: (k != 2, k))
    arrived = [swap(latents, "neuron", neuron_count, k) for k in order]
    row = lax.broadcasted_iota(jnp.int32, (lats + 8, neurons + width), 0)
    lines = jnp.pad(delays, ((lats + 1, 6), (0, neurons + width - lats)))
    lines = jnp.where(row == lats + 2, jnp.broadcast_to(recorded[:, None], lines.shape), lines)
    pack = jnp.pad(bias, ((lats, 7), (0, width))) + lines.astype(F32)
    pack = pack + jnp.pad(loadings[0], ((0, 8), (0, width))).astype(F32)
    pack = pack + jnp.pad(latents, ((0, 8), (neurons, 0))).astype(F32)

    *outs, load_ext, shifted = pl.pallas_call(
        functools.partial(shift_kernel, neuron_count, order, "neuron", chunk, step),
        out_shape=[jax.ShapeDtypeStruct((lats, width), BF16 if k > 1 else F32) for k in range(neuron_count)]
        + [jax.ShapeDtypeStruct((lats + EXTRA, neurons), BF16), jax.ShapeDtypeStruct((lats + EXTRA, total), BF16)],
        in_specs=[vmem, hbm] + [vmem] * (neuron_count - 1),
        out_specs=[vmem] * (neuron_count + 2),
        scratch_shapes=[
            pltpu.VMEM((lats, total), BF16),
            pltpu.VMEM((neurons, total), BF16),
            pltpu.VMEM((4 * chunk, total), F32),
            pltpu.VMEM((neurons, total), BF16),
            pltpu.VMEM((lats, total), F32),
            pltpu.SemaphoreType.DMA((2,)),
        ],
        compiler_params=params,
    )(pack, counts[0], *arrived)

    shares = [(0, 2 * chunk), (2 * chunk, neurons - 2 * chunk)]
    made = []

    def make(before):
        first, count = shares.pop(0)
        before, start_load = lax.optimization_barrier((before, load_ext))
        out = pl.pallas_call(
            functools.partial(load_kernel, lats, first, chunk, step),
            out_shape=[jax.ShapeDtypeStruct((lats, neurons), F32), jax.ShapeDtypeStruct((1, neurons), F32)],
            in_specs=[vmem, vmem, vmem, hbm] + [hbm] * len(made),
            out_specs=[hbm, hbm],
            scratch_shapes=[
                pltpu.VMEM((count, total), BF16),
                pltpu.VMEM((count, total), F32),
                pltpu.VMEM((lats, count), F32),
                pltpu.VMEM((1, count), F32),
                pltpu.SemaphoreType.DMA((1 + 2 * (count // chunk),)),
            ],
            input_output_aliases={4 + i: i for i in range(len(made))},
            compiler_params=params,
            cost_estimate=pl.CostEstimate(
                flops=4 * lats * count * total, bytes_accessed=2 * count * total, transcendentals=count * total
            ),
        )(pack, start_load, shifted, counts[0], *made)
        return before, out

    outs, made = make(outs)
    arrived = [swap(outs[k], "neuron", neuron_count, k) for k in [*range(2, neuron_count), 1]]
    arrived, made = lax.optimization_barrier((arrived, made))
    value = functools.reduce(jnp.add, [outs[0]] + [block.astype(F32) for block in arrived])
    mask = 1
    while mask < region_count:
        masks = [mask, 2 * mask, 3 * mask] if 2 * mask < region_count else [mask]
        if len(masks) == 3:
            value = lax.reduce_precision(value, 8, 7)
            sent, read = value.astype(BF16), lambda block: block.astype(F32)
        else:
            sent, read = lax.optimization_barrier(encode(value)), decode
            value = decode(sent)
        if shares:
            (value, sent), made = make((value, sent))
        arrived = [swap(sent, "region", region_count, k) for k in masks]
        arrived, made = lax.optimization_barrier((arrived, made))
        value = value + read(arrived[0])
        if len(masks) == 3:
            value = value + (read(arrived[1]) + read(arrived[2]))
        mask *= 1 + len(masks)
    grad_load, grad_bias = made
    return (value, grad_load[None], grad_bias)


def solution(mesh):
    placed = (
        P("region", "neuron", None),
        P(None, "neuron"),
        P("region", None, "neuron"),
        P("region", "neuron"),
        P("region", None),
        P("region"),
    )
    return jax.shard_map(
        functools.partial(per_device, mesh.shape["region"], mesh.shape["neuron"]),
        mesh=mesh,
        in_specs=placed,
        out_specs=(P(None, "neuron"), P("region", None, "neuron"), P("region", "neuron")),
        check_vma=False,
    )
```

```python
import functools

import jax
import jax.numpy as jnp
from jax import lax
from jax.experimental import pallas as pl
from jax.experimental.pallas import tpu as pltpu
from jax.sharding import PartitionSpec as P

LANES = 128
EXTRA = 16
F32 = jnp.float32
BF16 = jnp.bfloat16


def shift_tiles(tiles, delay, forward):
    lane = lax.broadcasted_iota(jnp.int32, delay.shape, 1)
    source = lane - delay if forward else lane + delay
    inside = source >= 0 if forward else source < LANES
    source = source & (LANES - 1)
    turned = [jnp.take_along_axis(tile, source, axis=1, mode="promise_in_bounds") for tile in tiles]
    nothing = [jnp.zeros_like(tiles[0])]
    others = nothing + turned[:-1] if forward else turned[1:] + nothing
    return [jnp.where(inside, tile, other) for tile, other in zip(turned, others)]


def expected(load_part, piece):
    eta = lax.dot_general(load_part, piece, (((0,), (0,)), ((), ())), preferred_element_type=F32)
    return jnp.exp(eta)


def shift_kernel(parts, order, axis, chunk, step, *refs):
    pack_ref, counts_hbm = refs[:2]
    arrived = refs[2 : 1 + parts]
    outs = refs[1 + parts : 1 + 2 * parts]
    load_ext, shifted, whole, counts_ref, held, resid_low, grad_shift, counts_sems = refs[1 + 2 * parts :]
    me = lax.axis_index(axis)
    lats, total = grad_shift.shape
    early = held.shape[0]
    neurons = counts_ref.shape[0]
    width = total // parts
    cut = 3 * chunk
    places = [pl.ds(0, cut), pl.ds(cut, neurons - cut)]
    copies = [
        pltpu.make_async_copy(counts_hbm.at[place], counts_ref.at[place], counts_sems.at[index])
        for index, place in enumerate(places)
    ]
    copies[0].start()

    for k in range(parts):
        start = pl.multiple_of((me ^ k) * width, width)
        whole[:, pl.ds(start, width)] = arrived[order.index(k)][...] if k else pack_ref[0:lats, neurons:].astype(BF16)
    diagonal = lax.broadcasted_iota(jnp.int32, (lats, LANES), 0) == lax.broadcasted_iota(jnp.int32, (lats, LANES), 1)
    spread = jnp.broadcast_to(pack_ref[lats + 1 : lats + 2, 0:LANES], (lats, LANES))
    column = jnp.sum(jnp.where(diagonal, spread, 0.0), axis=1, keepdims=True)
    delay = jnp.broadcast_to(column, (lats, LANES)).astype(jnp.int32)
    length = pack_ref[lats + 2 : lats + 3, 0:1].astype(jnp.int32)
    tiles = [whole[:, j * LANES : (j + 1) * LANES].astype(F32) for j in range(total // LANES)]
    for j, tile in enumerate(shift_tiles(tiles, delay, True)):
        shifted[0:lats, j * LANES : (j + 1) * LANES] = tile.astype(BF16)
    row = lax.broadcasted_iota(jnp.int32, (EXTRA, total), 0)
    shifted[lats:, :] = jnp.where(row < 3, 1.0, 0.0).astype(BF16)

    copies[1].start()

    load_ext[0:lats, :] = pack_ref[0:lats, 0:neurons].astype(BF16)
    bias = pack_ref[lats : lats + 1, 0:neurons]
    high = bias.astype(BF16).astype(F32)
    middle = (bias - high).astype(BF16).astype(F32)
    low = bias - high - middle
    row = lax.broadcasted_iota(jnp.int32, (EXTRA, neurons), 0)
    below = jnp.where(row == 0, high, jnp.where(row == 1, middle, jnp.where(row == 2, low, 0.0)))
    load_ext[lats:, :] = below.astype(BF16)

    blocks = [
        (slice(first, first + chunk), slice(begin, begin + step))
        for first in range(0, neurons, chunk)
        for begin in range(0, total, step)
    ]
    for rows, span in blocks:
        if rows.start < early:
            held[rows, span] = expected(load_ext[:, rows], shifted[:, span])
    spans = [slice(begin, begin + step) for begin in range(0, total, step)]
    for copy, place in zip(copies, [slice(0, cut), slice(cut, neurons)]):
        copy.wait()
        for rows, span in blocks:
            if place.start <= rows.start < place.stop:
                rate = held[rows, span] if rows.start < early else expected(load_ext[:, rows], shifted[:, span])
                resid_low[rows, span] = (rate - counts_ref[rows, span].astype(F32)).astype(BF16)
        for span in spans:
            part = jnp.dot(load_ext[0:lats, place], resid_low[place, span], preferred_element_type=F32)
            grad_shift[:, span] = grad_shift[:, span] + part if place.start else part

    bins = lax.broadcasted_iota(jnp.int32, (1, total), 1)
    tiles = []
    for j in range(total // LANES):
        span = slice(j * LANES, (j + 1) * LANES)
        tiles.append(jnp.where(bins[:, span] < length, grad_shift[:, span], 0.0))
    for j, tile in enumerate(shift_tiles(tiles, delay, False)):
        grad_shift[:, j * LANES : (j + 1) * LANES] = tile
    for k in range(parts):
        start = pl.multiple_of((me ^ k) * width, width)
        outs[k][...] = grad_shift[:, pl.ds(start, width)].astype(outs[k].dtype)


def load_kernel(lats, first, chunk, step, *refs):
    pack_ref, load_ext, shifted, counts_hbm = refs[:4]
    load_hbm, bias_hbm, counts_ref, held, load_ref, bias_ref, sems = refs[-7:]
    count, total = counts_ref.shape
    place = pl.ds(first, count)
    counts_copy = pltpu.make_async_copy(counts_hbm.at[place], counts_ref, sems.at[0])
    counts_copy.start()
    length = pack_ref[lats + 2 : lats + 3, 0:1].astype(jnp.int32)
    bins = lax.broadcasted_iota(jnp.int32, (1, total), 1)
    blocks = [(slice(begin, begin + chunk), range(0, total, step)) for begin in range(0, count, chunk)]

    def rate(rows, span):
        return expected(load_ext[:, first + rows.start : first + rows.stop], shifted[:, span])

    early = blocks[:-1] if len(blocks) > 2 else blocks
    for rows, starts in early:
        for at in starts:
            held[rows, at : at + step] = rate(rows, slice(at, at + step))
    counts_copy.wait()
    outward = []
    for index, (rows, starts) in enumerate(blocks):
        sums = jnp.zeros((chunk, LANES), F32)
        grad = jnp.zeros((chunk, lats), F32)
        for at in starts:
            span = slice(at, at + step)
            made = held[rows, span] if index < len(early) else rate(rows, span)
            resid = jnp.where(bins[:, span] < length, made - counts_ref[rows, span].astype(F32), 0.0)
            for j in range(step // LANES):
                sums = sums + resid[:, j * LANES : (j + 1) * LANES]
            grad = grad + lax.dot_general(
                resid.astype(BF16), shifted[0:lats, span], (((1,), (1,)), ((), ())), preferred_element_type=F32
            )
        load_ref[:, rows] = grad.T
        bias_ref[:, rows] = jnp.sum(sums.T, axis=0, keepdims=True)
        place = pl.ds(first + rows.start, chunk)
        outward.append(pltpu.make_async_copy(load_ref.at[:, rows], load_hbm.at[:, place], sems.at[2 * index + 1]))
        outward.append(pltpu.make_async_copy(bias_ref.at[:, rows], bias_hbm.at[:, place], sems.at[2 * index + 2]))
        for copy in outward[-2:]:
            copy.start()
    for copy in outward:
        copy.wait()


def encode(value):
    top = jnp.maximum(jnp.max(jnp.abs(value), axis=0, keepdims=True), 2.0**-100)
    power = jnp.ceil(jnp.log2(top)) - 14.0
    rows = jnp.broadcast_to(power, (8, value.shape[1]))
    return jnp.concatenate([value * jnp.exp2(-power), rows], axis=0).astype(jnp.float16)


def decode(code):
    power = code[-8:-7].astype(F32)
    return code[:-8].astype(F32) * jnp.exp2(power)


def per_device(region_count, neuron_count, counts, latents, loadings, bias, delays, recorded):
    neurons, total = counts.shape[1:]
    lats, width = latents.shape
    chunk, step = 256, 512
    vmem = pl.BlockSpec(memory_space=pltpu.VMEM)
    hbm = pl.BlockSpec(memory_space=pltpu.HBM)
    params = pltpu.CompilerParams(vmem_limit_bytes=52 * 1024 * 1024)

    def swap(value, axis, count, mask):
        return lax.ppermute(value, axis, [(i, i ^ mask) for i in range(count)])

    order = sorted(range(1, neuron_count), key=lambda k: (k != 2, k))
    arrived = [swap(latents, "neuron", neuron_count, k) for k in order]
    row = lax.broadcasted_iota(jnp.int32, (lats + 8, neurons + width), 0)
    lines = jnp.pad(delays, ((lats + 1, 6), (0, neurons + width - lats)))
    lines = jnp.where(row == lats + 2, jnp.broadcast_to(recorded[:, None], lines.shape), lines)
    pack = jnp.pad(bias, ((lats, 7), (0, width))) + lines.astype(F32)
    pack = pack + jnp.pad(loadings[0], ((0, 8), (0, width))).astype(F32)
    pack = pack + jnp.pad(latents, ((0, 8), (neurons, 0))).astype(F32)

    *outs, load_ext, shifted = pl.pallas_call(
        functools.partial(shift_kernel, neuron_count, order, "neuron", chunk, 2 * step),
        out_shape=[jax.ShapeDtypeStruct((lats, width), BF16 if k > 1 else F32) for k in range(neuron_count)]
        + [jax.ShapeDtypeStruct((lats + EXTRA, neurons), BF16), jax.ShapeDtypeStruct((lats + EXTRA, total), BF16)],
        in_specs=[vmem, hbm] + [vmem] * (neuron_count - 1),
        out_specs=[vmem] * (neuron_count + 2),
        scratch_shapes=[
            pltpu.VMEM((lats, total), BF16),
            pltpu.VMEM((neurons, total), BF16),
            pltpu.VMEM((4 * chunk, total), F32),
            pltpu.VMEM((neurons, total), BF16),
            pltpu.VMEM((lats, total), F32),
            pltpu.SemaphoreType.DMA((2,)),
        ],
        compiler_params=params,
    )(pack, counts[0], *arrived)

    shares = [(0, 2 * chunk), (2 * chunk, neurons - 2 * chunk)]
    made = []

    def make(before):
        first, count = shares.pop(0)
        before, start_load = lax.optimization_barrier((before, load_ext))
        out = pl.pallas_call(
            functools.partial(load_kernel, lats, first, chunk, step),
            out_shape=[jax.ShapeDtypeStruct((lats, neurons), F32), jax.ShapeDtypeStruct((1, neurons), F32)],
            in_specs=[vmem, vmem, vmem, hbm] + [hbm] * len(made),
            out_specs=[hbm, hbm],
            scratch_shapes=[
                pltpu.VMEM((count, total), BF16),
                pltpu.VMEM((count, total), F32),
                pltpu.VMEM((lats, count), F32),
                pltpu.VMEM((1, count), F32),
                pltpu.SemaphoreType.DMA((1 + 2 * (count // chunk),)),
            ],
            input_output_aliases={4 + i: i for i in range(len(made))},
            compiler_params=params,
            cost_estimate=pl.CostEstimate(
                flops=4 * lats * count * total, bytes_accessed=2 * count * total, transcendentals=count * total
            ),
        )(pack, start_load, shifted, counts[0], *made)
        return before, out

    outs, made = make(outs)
    arrived = [swap(outs[k], "neuron", neuron_count, k) for k in range(neuron_count - 1, 0, -1)]
    arrived, made = lax.optimization_barrier((arrived, made))
    value = functools.reduce(jnp.add, [outs[0]] + [block.astype(F32) for block in arrived])
    mask = 1
    while mask < region_count:
        masks = [mask, 2 * mask, 3 * mask] if 2 * mask < region_count else [mask]
        if len(masks) == 3:
            value = lax.reduce_precision(value, 8, 7)
            sent, read = value.astype(BF16), lambda block: block.astype(F32)
        else:
            sent, read = lax.optimization_barrier(encode(value)), decode
            value = decode(sent)
        if shares:
            (value, sent), made = make((value, sent))
        arrived = [swap(sent, "region", region_count, k) for k in masks]
        arrived, made = lax.optimization_barrier((arrived, made))
        value = value + read(arrived[0])
        if len(masks) == 3:
            value = value + (read(arrived[1]) + read(arrived[2]))
        mask *= 1 + len(masks)
    grad_load, grad_bias = made
    return (value, grad_load[None], grad_bias)


def solution(mesh):
    placed = (
        P("region", "neuron", None),
        P(None, "neuron"),
        P("region", None, "neuron"),
        P("region", "neuron"),
        P("region", None),
        P("region"),
    )
    return jax.shard_map(
        functools.partial(per_device, mesh.shape["region"], mesh.shape["neuron"]),
        mesh=mesh,
        in_specs=placed,
        out_specs=(P(None, "neuron"), P("region", None, "neuron"), P("region", "neuron")),
        check_vma=False,
    )
```

```python
import functools

import jax
import jax.numpy as jnp
from jax import lax
from jax.experimental import pallas as pl
from jax.experimental.pallas import tpu as pltpu
from jax.sharding import PartitionSpec as P

LANES = 128
EXTRA = 16
F32 = jnp.float32
BF16 = jnp.bfloat16


def shift_tiles(tiles, delay, forward):
    lane = lax.broadcasted_iota(jnp.int32, delay.shape, 1)
    source = lane - delay if forward else lane + delay
    inside = source >= 0 if forward else source < LANES
    source = source & (LANES - 1)
    turned = [jnp.take_along_axis(tile, source, axis=1, mode="promise_in_bounds") for tile in tiles]
    nothing = [jnp.zeros_like(tiles[0])]
    others = nothing + turned[:-1] if forward else turned[1:] + nothing
    return [jnp.where(inside, tile, other) for tile, other in zip(turned, others)]


def expected(load_part, piece):
    eta = lax.dot_general(load_part, piece, (((0,), (0,)), ((), ())), preferred_element_type=F32)
    return jnp.exp(eta)


def shift_kernel(parts, order, axis, chunk, step, *refs):
    pack_ref, counts_hbm = refs[:2]
    arrived = refs[2 : 1 + parts]
    outs = refs[1 + parts : 1 + 2 * parts]
    load_ext, shifted, whole, counts_ref, held, resid_low, grad_shift, counts_sems = refs[1 + 2 * parts :]
    me = lax.axis_index(axis)
    lats, total = grad_shift.shape
    early = held.shape[0]
    neurons = counts_ref.shape[0]
    width = total // parts
    cut = 3 * chunk
    places = [pl.ds(0, cut), pl.ds(cut, neurons - cut)]
    copies = [
        pltpu.make_async_copy(counts_hbm.at[place], counts_ref.at[place], counts_sems.at[index])
        for index, place in enumerate(places)
    ]
    copies[0].start()

    for k in range(parts):
        start = pl.multiple_of((me ^ k) * width, width)
        whole[:, pl.ds(start, width)] = arrived[order.index(k)][...] if k else pack_ref[0:lats, neurons:].astype(BF16)
    diagonal = lax.broadcasted_iota(jnp.int32, (lats, LANES), 0) == lax.broadcasted_iota(jnp.int32, (lats, LANES), 1)
    spread = jnp.broadcast_to(pack_ref[lats + 1 : lats + 2, 0:LANES], (lats, LANES))
    column = jnp.sum(jnp.where(diagonal, spread, 0.0), axis=1, keepdims=True)
    delay = jnp.broadcast_to(column, (lats, LANES)).astype(jnp.int32)
    length = pack_ref[lats + 2 : lats + 3, 0:1].astype(jnp.int32)
    tiles = [whole[:, j * LANES : (j + 1) * LANES].astype(F32) for j in range(total // LANES)]
    for j, tile in enumerate(shift_tiles(tiles, delay, True)):
        shifted[0:lats, j * LANES : (j + 1) * LANES] = tile.astype(BF16)
    row = lax.broadcasted_iota(jnp.int32, (EXTRA, total), 0)
    shifted[lats:, :] = jnp.where(row < 3, 1.0, 0.0).astype(BF16)

    copies[1].start()

    load_ext[0:lats, :] = pack_ref[0:lats, 0:neurons].astype(BF16)
    bias = pack_ref[lats : lats + 1, 0:neurons]
    high = bias.astype(BF16).astype(F32)
    middle = (bias - high).astype(BF16).astype(F32)
    low = bias - high - middle
    row = lax.broadcasted_iota(jnp.int32, (EXTRA, neurons), 0)
    below = jnp.where(row == 0, high, jnp.where(row == 1, middle, jnp.where(row == 2, low, 0.0)))
    load_ext[lats:, :] = below.astype(BF16)

    blocks = [
        (slice(first, first + chunk), slice(begin, begin + step))
        for first in range(0, neurons, chunk)
        for begin in range(0, total, step)
    ]
    for rows, span in blocks:
        if rows.start < early:
            held[rows, span] = expected(load_ext[:, rows], shifted[:, span])
    spans = [slice(begin, begin + step) for begin in range(0, total, step)]
    for copy, place in zip(copies, [slice(0, cut), slice(cut, neurons)]):
        copy.wait()
        for rows, span in blocks:
            if place.start <= rows.start < place.stop:
                rate = held[rows, span] if rows.start < early else expected(load_ext[:, rows], shifted[:, span])
                resid_low[rows, span] = (rate - counts_ref[rows, span].astype(F32)).astype(BF16)
        for span in spans:
            part = jnp.dot(load_ext[0:lats, place], resid_low[place, span], preferred_element_type=F32)
            grad_shift[:, span] = grad_shift[:, span] + part if place.start else part

    bins = lax.broadcasted_iota(jnp.int32, (1, total), 1)
    tiles = []
    for j in range(total // LANES):
        span = slice(j * LANES, (j + 1) * LANES)
        tiles.append(jnp.where(bins[:, span] < length, grad_shift[:, span], 0.0))
    for j, tile in enumerate(shift_tiles(tiles, delay, False)):
        grad_shift[:, j * LANES : (j + 1) * LANES] = tile
    for k in range(parts):
        start = pl.multiple_of((me ^ k) * width, width)
        outs[k][...] = grad_shift[:, pl.ds(start, width)].astype(outs[k].dtype)


def load_kernel(lats, first, chunk, step, *refs):
    pack_ref, load_ext, shifted, counts_hbm = refs[:4]
    load_hbm, bias_hbm, counts_ref, held, load_ref, bias_ref, sems = refs[-7:]
    count, total = counts_ref.shape
    place = pl.ds(first, count)
    counts_copy = pltpu.make_async_copy(counts_hbm.at[place], counts_ref, sems.at[0])
    counts_copy.start()
    length = pack_ref[lats + 2 : lats + 3, 0:1].astype(jnp.int32)
    bins = lax.broadcasted_iota(jnp.int32, (1, total), 1)
    blocks = [(slice(begin, begin + chunk), range(0, total, step)) for begin in range(0, count, chunk)]

    def rate(rows, span):
        return expected(load_ext[:, first + rows.start : first + rows.stop], shifted[:, span])

    early = blocks[:-1] if len(blocks) > 2 else blocks
    for rows, starts in early:
        for at in starts:
            held[rows, at : at + step] = rate(rows, slice(at, at + step))
    counts_copy.wait()
    outward = []
    for index, (rows, starts) in enumerate(blocks):
        sums = jnp.zeros((chunk, LANES), F32)
        grad = jnp.zeros((chunk, lats), F32)
        for at in starts:
            span = slice(at, at + step)
            made = held[rows, span] if index < len(early) else rate(rows, span)
            resid = jnp.where(bins[:, span] < length, made - counts_ref[rows, span].astype(F32), 0.0)
            for j in range(step // LANES):
                sums = sums + resid[:, j * LANES : (j + 1) * LANES]
            grad = grad + lax.dot_general(
                resid.astype(BF16), shifted[0:lats, span], (((1,), (1,)), ((), ())), preferred_element_type=F32
            )
        load_ref[:, rows] = grad.T
        bias_ref[:, rows] = jnp.sum(sums.T, axis=0, keepdims=True)
        place = pl.ds(first + rows.start, chunk)
        outward.append(pltpu.make_async_copy(load_ref.at[:, rows], load_hbm.at[:, place], sems.at[2 * index + 1]))
        outward.append(pltpu.make_async_copy(bias_ref.at[:, rows], bias_hbm.at[:, place], sems.at[2 * index + 2]))
        for copy in outward[-2:]:
            copy.start()
    for copy in outward:
        copy.wait()


def encode(value):
    top = jnp.maximum(jnp.max(jnp.abs(value), axis=0, keepdims=True), 2.0**-100)
    power = jnp.ceil(jnp.log2(top)) - 14.0
    rows = jnp.broadcast_to(power, (8, value.shape[1]))
    return jnp.concatenate([value * jnp.exp2(-power), rows], axis=0).astype(jnp.float16)


def decode(code):
    power = code[-8:-7].astype(F32)
    return code[:-8].astype(F32) * jnp.exp2(power)


def per_device(region_count, neuron_count, counts, latents, loadings, bias, delays, recorded):
    neurons, total = counts.shape[1:]
    lats, width = latents.shape
    chunk, step = 256, 512
    vmem = pl.BlockSpec(memory_space=pltpu.VMEM)
    hbm = pl.BlockSpec(memory_space=pltpu.HBM)
    params = pltpu.CompilerParams(vmem_limit_bytes=52 * 1024 * 1024)

    def swap(value, axis, count, mask):
        return lax.ppermute(value, axis, [(i, i ^ mask) for i in range(count)])

    order = sorted(range(1, neuron_count), key=lambda k: (k != 2, k))
    arrived = [swap(latents, "neuron", neuron_count, k) for k in order]
    row = lax.broadcasted_iota(jnp.int32, (lats + 8, neurons + width), 0)
    lines = jnp.pad(delays, ((lats + 1, 6), (0, neurons + width - lats)))
    lines = jnp.where(row == lats + 2, jnp.broadcast_to(recorded[:, None], lines.shape), lines)
    pack = jnp.pad(bias, ((lats, 7), (0, width))) + lines.astype(F32)
    pack = pack + jnp.pad(loadings[0], ((0, 8), (0, width))).astype(F32)
    pack = pack + jnp.pad(latents, ((0, 8), (neurons, 0))).astype(F32)

    *outs, load_ext, shifted = pl.pallas_call(
        functools.partial(shift_kernel, neuron_count, order, "neuron", chunk, step),
        out_shape=[jax.ShapeDtypeStruct((lats, width), BF16 if k > 1 else F32) for k in range(neuron_count)]
        + [jax.ShapeDtypeStruct((lats + EXTRA, neurons), BF16), jax.ShapeDtypeStruct((lats + EXTRA, total), BF16)],
        in_specs=[vmem, hbm] + [vmem] * (neuron_count - 1),
        out_specs=[vmem] * (neuron_count + 2),
        scratch_shapes=[
            pltpu.VMEM((lats, total), BF16),
            pltpu.VMEM((neurons, total), BF16),
            pltpu.VMEM((4 * chunk, total), F32),
            pltpu.VMEM((neurons, total), BF16),
            pltpu.VMEM((lats, total), F32),
            pltpu.SemaphoreType.DMA((2,)),
        ],
        compiler_params=params,
    )(pack, counts[0], *arrived)

    shares = [(0, 2 * chunk), (2 * chunk, neurons - 2 * chunk)]
    made = []

    def make(before):
        first, count = shares.pop(0)
        before, start_load = lax.optimization_barrier((before, load_ext))
        out = pl.pallas_call(
            functools.partial(load_kernel, lats, first, chunk, step),
            out_shape=[jax.ShapeDtypeStruct((lats, neurons), F32), jax.ShapeDtypeStruct((1, neurons), F32)],
            in_specs=[vmem, vmem, vmem, hbm] + [hbm] * len(made),
            out_specs=[hbm, hbm],
            scratch_shapes=[
                pltpu.VMEM((count, total), BF16),
                pltpu.VMEM((count, total), F32),
                pltpu.VMEM((lats, count), F32),
                pltpu.VMEM((1, count), F32),
                pltpu.SemaphoreType.DMA((1 + 2 * (count // chunk),)),
            ],
            input_output_aliases={4 + i: i for i in range(len(made))},
            compiler_params=params,
            cost_estimate=pl.CostEstimate(
                flops=4 * lats * count * total, bytes_accessed=2 * count * total, transcendentals=count * total
            ),
        )(pack, start_load, shifted, counts[0], *made)
        return before, out

    outs, made = make(outs)
    arrived = [swap(outs[k], "neuron", neuron_count, k) for k in [*range(2, neuron_count), 1]]
    arrived, made = lax.optimization_barrier((arrived, made))
    value = functools.reduce(jnp.add, [outs[0]] + [block.astype(F32) for block in arrived])
    mask = 1
    while mask < region_count:
        masks = [mask, 2 * mask, 3 * mask] if 2 * mask < region_count else [mask]
        if len(masks) == 3:
            value = lax.reduce_precision(value, 8, 7)
            sent, read = value.astype(BF16), lambda block: block.astype(F32)
        else:
            sent, read = lax.optimization_barrier(encode(value)), decode
            value = decode(sent)
        if shares:
            (value, sent), made = make((value, sent))
        arrived = [swap(sent, "region", region_count, k) for k in masks[::-1]]
        arrived, made = lax.optimization_barrier((arrived, made))
        arrived = arrived[::-1]
        value = value + read(arrived[0])
        if len(masks) == 3:
            value = value + (read(arrived[1]) + read(arrived[2]))
        mask *= 1 + len(masks)
    grad_load, grad_bias = made
    return (value, grad_load[None], grad_bias)


def solution(mesh):
    placed = (
        P("region", "neuron", None),
        P(None, "neuron"),
        P("region", None, "neuron"),
        P("region", "neuron"),
        P("region", None),
        P("region"),
    )
    return jax.shard_map(
        functools.partial(per_device, mesh.shape["region"], mesh.shape["neuron"]),
        mesh=mesh,
        in_specs=placed,
        out_specs=(P(None, "neuron"), P("region", None, "neuron"), P("region", "neuron")),
        check_vma=False,
    )
```

```python
import functools

import jax
import jax.numpy as jnp
from jax import lax
from jax.experimental import pallas as pl
from jax.experimental.pallas import tpu as pltpu
from jax.sharding import PartitionSpec as P

LANES = 128
EXTRA = 16
F32 = jnp.float32
BF16 = jnp.bfloat16


def shift_tiles(tiles, delay, forward):
    lane = lax.broadcasted_iota(jnp.int32, delay.shape, 1)
    source = lane - delay if forward else lane + delay
    inside = source >= 0 if forward else source < LANES
    source = source & (LANES - 1)
    turned = [jnp.take_along_axis(tile, source, axis=1, mode="promise_in_bounds") for tile in tiles]
    nothing = [jnp.zeros_like(tiles[0])]
    others = nothing + turned[:-1] if forward else turned[1:] + nothing
    return [jnp.where(inside, tile, other) for tile, other in zip(turned, others)]


def expected(load_part, piece):
    eta = lax.dot_general(load_part, piece, (((0,), (0,)), ((), ())), preferred_element_type=F32)
    return jnp.exp(eta)


def shift_kernel(parts, order, axis, chunk, step, *refs):
    pack_ref, counts_hbm = refs[:2]
    arrived = refs[2 : 1 + parts]
    outs = refs[1 + parts : 1 + 2 * parts]
    load_ext, shifted, whole, counts_ref, held, resid_low, grad_shift, counts_sems = refs[1 + 2 * parts :]
    me = lax.axis_index(axis)
    lats, total = grad_shift.shape
    early = held.shape[0]
    neurons = counts_ref.shape[0]
    width = total // parts
    cut = 3 * chunk
    places = [pl.ds(0, cut), pl.ds(cut, neurons - cut)]
    copies = [
        pltpu.make_async_copy(counts_hbm.at[place], counts_ref.at[place], counts_sems.at[index])
        for index, place in enumerate(places)
    ]
    copies[0].start()

    for k in range(parts):
        start = pl.multiple_of((me ^ k) * width, width)
        whole[:, pl.ds(start, width)] = arrived[order.index(k)][...] if k else pack_ref[0:lats, neurons:].astype(BF16)
    diagonal = lax.broadcasted_iota(jnp.int32, (lats, LANES), 0) == lax.broadcasted_iota(jnp.int32, (lats, LANES), 1)
    spread = jnp.broadcast_to(pack_ref[lats + 1 : lats + 2, 0:LANES], (lats, LANES))
    column = jnp.sum(jnp.where(diagonal, spread, 0.0), axis=1, keepdims=True)
    delay = jnp.broadcast_to(column, (lats, LANES)).astype(jnp.int32)
    length = pack_ref[lats + 2 : lats + 3, 0:1].astype(jnp.int32)
    tiles = [whole[:, j * LANES : (j + 1) * LANES].astype(F32) for j in range(total // LANES)]
    for j, tile in enumerate(shift_tiles(tiles, delay, True)):
        shifted[0:lats, j * LANES : (j + 1) * LANES] = tile.astype(BF16)
    row = lax.broadcasted_iota(jnp.int32, (EXTRA, total), 0)
    shifted[lats:, :] = jnp.where(row < 3, 1.0, 0.0).astype(BF16)

    copies[1].start()

    load_ext[0:lats, :] = pack_ref[0:lats, 0:neurons].astype(BF16)
    bias = pack_ref[lats : lats + 1, 0:neurons]
    high = bias.astype(BF16).astype(F32)
    middle = (bias - high).astype(BF16).astype(F32)
    low = bias - high - middle
    row = lax.broadcasted_iota(jnp.int32, (EXTRA, neurons), 0)
    below = jnp.where(row == 0, high, jnp.where(row == 1, middle, jnp.where(row == 2, low, 0.0)))
    load_ext[lats:, :] = below.astype(BF16)

    blocks = [
        (slice(first, first + chunk), slice(begin, begin + step))
        for first in range(0, neurons, chunk)
        for begin in range(0, total, step)
    ]
    for rows, span in blocks:
        if rows.start < early:
            held[rows, span] = expected(load_ext[:, rows], shifted[:, span])
    spans = [slice(begin, begin + step) for begin in range(0, total, step)]
    for copy, place in zip(copies, [slice(0, cut), slice(cut, neurons)]):
        copy.wait()
        for rows, span in blocks:
            if place.start <= rows.start < place.stop:
                rate = held[rows, span] if rows.start < early else expected(load_ext[:, rows], shifted[:, span])
                resid_low[rows, span] = (rate - counts_ref[rows, span].astype(F32)).astype(BF16)
        for span in spans:
            part = jnp.dot(load_ext[0:lats, place], resid_low[place, span], preferred_element_type=F32)
            grad_shift[:, span] = grad_shift[:, span] + part if place.start else part

    bins = lax.broadcasted_iota(jnp.int32, (1, total), 1)
    tiles = []
    for j in range(total // LANES):
        span = slice(j * LANES, (j + 1) * LANES)
        tiles.append(jnp.where(bins[:, span] < length, grad_shift[:, span], 0.0))
    for j, tile in enumerate(shift_tiles(tiles, delay, False)):
        grad_shift[:, j * LANES : (j + 1) * LANES] = tile
    for k in range(parts):
        start = pl.multiple_of((me ^ k) * width, width)
        outs[k][...] = grad_shift[:, pl.ds(start, width)].astype(outs[k].dtype)


def load_kernel(lats, first, chunk, step, *refs):
    pack_ref, load_ext, shifted, counts_hbm = refs[:4]
    load_hbm, bias_hbm, counts_ref, held, load_ref, bias_ref, sems = refs[-7:]
    count, total = counts_ref.shape
    place = pl.ds(first, count)
    counts_copy = pltpu.make_async_copy(counts_hbm.at[place], counts_ref, sems.at[0])
    counts_copy.start()
    length = pack_ref[lats + 2 : lats + 3, 0:1].astype(jnp.int32)
    bins = lax.broadcasted_iota(jnp.int32, (1, total), 1)
    blocks = [(slice(begin, begin + chunk), range(0, total, step)) for begin in range(0, count, chunk)]

    def rate(rows, span):
        return expected(load_ext[:, first + rows.start : first + rows.stop], shifted[:, span])

    early = blocks[:-1] if len(blocks) > 2 else blocks
    for rows, starts in early:
        for at in starts:
            held[rows, at : at + step] = rate(rows, slice(at, at + step))
    counts_copy.wait()
    outward = []
    for index, (rows, starts) in enumerate(blocks):
        sums = jnp.zeros((chunk, LANES), F32)
        grad = jnp.zeros((chunk, lats), F32)
        for at in starts:
            span = slice(at, at + step)
            made = held[rows, span] if index < len(early) else rate(rows, span)
            resid = jnp.where(bins[:, span] < length, made - counts_ref[rows, span].astype(F32), 0.0)
            for j in range(step // LANES):
                sums = sums + resid[:, j * LANES : (j + 1) * LANES]
            grad = grad + lax.dot_general(
                resid.astype(BF16), shifted[0:lats, span], (((1,), (1,)), ((), ())), preferred_element_type=F32
            )
        load_ref[:, rows] = grad.T
        bias_ref[:, rows] = jnp.sum(sums.T, axis=0, keepdims=True)
        place = pl.ds(first + rows.start, chunk)
        outward.append(pltpu.make_async_copy(load_ref.at[:, rows], load_hbm.at[:, place], sems.at[2 * index + 1]))
        outward.append(pltpu.make_async_copy(bias_ref.at[:, rows], bias_hbm.at[:, place], sems.at[2 * index + 2]))
        for copy in outward[-2:]:
            copy.start()
    for copy in outward:
        copy.wait()


def encode(value):
    top = jnp.maximum(jnp.max(jnp.abs(value), axis=0, keepdims=True), 2.0**-100)
    power = jnp.ceil(jnp.log2(top)) - 14.0
    rows = jnp.broadcast_to(power, (8, value.shape[1]))
    return jnp.concatenate([value * jnp.exp2(-power), rows], axis=0).astype(jnp.float16)


def decode(code):
    power = code[-8:-7].astype(F32)
    return code[:-8].astype(F32) * jnp.exp2(power)


def per_device(region_count, neuron_count, counts, latents, loadings, bias, delays, recorded):
    neurons, total = counts.shape[1:]
    lats, width = latents.shape
    chunk, step = 256, 512
    vmem = pl.BlockSpec(memory_space=pltpu.VMEM)
    hbm = pl.BlockSpec(memory_space=pltpu.HBM)
    params = pltpu.CompilerParams(vmem_limit_bytes=52 * 1024 * 1024)

    def swap(value, axis, count, mask):
        return lax.ppermute(value, axis, [(i, i ^ mask) for i in range(count)])

    order = [1, *range(neuron_count - 1, 1, -1)]
    arrived = [swap(latents, "neuron", neuron_count, k) for k in order]
    row = lax.broadcasted_iota(jnp.int32, (lats + 8, neurons + width), 0)
    lines = jnp.pad(delays, ((lats + 1, 6), (0, neurons + width - lats)))
    lines = jnp.where(row == lats + 2, jnp.broadcast_to(recorded[:, None], lines.shape), lines)
    pack = jnp.pad(bias, ((lats, 7), (0, width))) + lines.astype(F32)
    pack = pack + jnp.pad(loadings[0], ((0, 8), (0, width))).astype(F32)
    pack = pack + jnp.pad(latents, ((0, 8), (neurons, 0))).astype(F32)

    *outs, load_ext, shifted = pl.pallas_call(
        functools.partial(shift_kernel, neuron_count, order, "neuron", chunk, step),
        out_shape=[jax.ShapeDtypeStruct((lats, width), BF16 if k > 1 else F32) for k in range(neuron_count)]
        + [jax.ShapeDtypeStruct((lats + EXTRA, neurons), BF16), jax.ShapeDtypeStruct((lats + EXTRA, total), BF16)],
        in_specs=[vmem, hbm] + [vmem] * (neuron_count - 1),
        out_specs=[vmem] * (neuron_count + 2),
        scratch_shapes=[
            pltpu.VMEM((lats, total), BF16),
            pltpu.VMEM((neurons, total), BF16),
            pltpu.VMEM((4 * chunk, total), F32),
            pltpu.VMEM((neurons, total), BF16),
            pltpu.VMEM((lats, total), F32),
            pltpu.SemaphoreType.DMA((2,)),
        ],
        compiler_params=params,
    )(pack, counts[0], *arrived)

    shares = [(0, 2 * chunk), (2 * chunk, neurons - 2 * chunk)]
    made = []

    def make(before):
        first, count = shares.pop(0)
        before, start_load = lax.optimization_barrier((before, load_ext))
        out = pl.pallas_call(
            functools.partial(load_kernel, lats, first, chunk, step),
            out_shape=[jax.ShapeDtypeStruct((lats, neurons), F32), jax.ShapeDtypeStruct((1, neurons), F32)],
            in_specs=[vmem, vmem, vmem, hbm] + [hbm] * len(made),
            out_specs=[hbm, hbm],
            scratch_shapes=[
                pltpu.VMEM((count, total), BF16),
                pltpu.VMEM((count, total), F32),
                pltpu.VMEM((lats, count), F32),
                pltpu.VMEM((1, count), F32),
                pltpu.SemaphoreType.DMA((1 + 2 * (count // chunk),)),
            ],
            input_output_aliases={4 + i: i for i in range(len(made))},
            compiler_params=params,
            cost_estimate=pl.CostEstimate(
                flops=4 * lats * count * total, bytes_accessed=2 * count * total, transcendentals=count * total
            ),
        )(pack, start_load, shifted, counts[0], *made)
        return before, out

    outs, made = make(outs)
    arrived = [swap(outs[k], "neuron", neuron_count, k) for k in [*range(2, neuron_count), 1]]
    arrived, made = lax.optimization_barrier((arrived, made))
    value = functools.reduce(jnp.add, [outs[0]] + [block.astype(F32) for block in arrived])
    mask = 1
    while mask < region_count:
        masks = [mask, 2 * mask, 3 * mask] if 2 * mask < region_count else [mask]
        if len(masks) == 3:
            value = lax.reduce_precision(value, 8, 7)
            sent, read = value.astype(BF16), lambda block: block.astype(F32)
        else:
            sent, read = lax.optimization_barrier(encode(value)), decode
            value = decode(sent)
        if shares:
            (value, sent), made = make((value, sent))
        turns = sorted(masks, key=lambda k: (k != mask, -k))
        arrived = [swap(sent, "region", region_count, k) for k in turns]
        arrived, made = lax.optimization_barrier((arrived, made))
        arrived = [arrived[turns.index(k)] for k in masks]
        value = value + read(arrived[0])
        if len(masks) == 3:
            value = value + (read(arrived[1]) + read(arrived[2]))
        mask *= 1 + len(masks)
    grad_load, grad_bias = made
    return (value, grad_load[None], grad_bias)


def solution(mesh):
    placed = (
        P("region", "neuron", None),
        P(None, "neuron"),
        P("region", None, "neuron"),
        P("region", "neuron"),
        P("region", None),
        P("region"),
    )
    return jax.shard_map(
        functools.partial(per_device, mesh.shape["region"], mesh.shape["neuron"]),
        mesh=mesh,
        in_specs=placed,
        out_specs=(P(None, "neuron"), P("region", None, "neuron"), P("region", "neuron")),
        check_vma=False,
    )
```

```python
import functools

import jax
import jax.numpy as jnp
from jax import lax
from jax.experimental import pallas as pl
from jax.experimental.pallas import tpu as pltpu
from jax.sharding import PartitionSpec as P

LANES = 128
EXTRA = 16
F32 = jnp.float32
BF16 = jnp.bfloat16


def shift_tiles(tiles, delay, forward):
    lane = lax.broadcasted_iota(jnp.int32, delay.shape, 1)
    source = lane - delay if forward else lane + delay
    inside = source >= 0 if forward else source < LANES
    source = source & (LANES - 1)
    turned = [jnp.take_along_axis(tile, source, axis=1, mode="promise_in_bounds") for tile in tiles]
    nothing = [jnp.zeros_like(tiles[0])]
    others = nothing + turned[:-1] if forward else turned[1:] + nothing
    return [jnp.where(inside, tile, other) for tile, other in zip(turned, others)]


def expected(load_part, piece):
    eta = lax.dot_general(load_part, piece, (((0,), (0,)), ((), ())), preferred_element_type=F32)
    return jnp.exp(eta)


def shift_kernel(parts, order, axis, chunk, step, *refs):
    pack_ref, counts_hbm = refs[:2]
    arrived = refs[2 : 1 + parts]
    outs = refs[1 + parts : 1 + 2 * parts]
    load_ext, shifted, whole, counts_ref, held, resid_low, grad_shift, counts_sems = refs[1 + 2 * parts :]
    me = lax.axis_index(axis)
    lats, total = grad_shift.shape
    early = held.shape[0]
    neurons = counts_ref.shape[0]
    width = total // parts
    cut = 3 * chunk
    places = [pl.ds(0, cut), pl.ds(cut, neurons - cut)]
    copies = [
        pltpu.make_async_copy(counts_hbm.at[place], counts_ref.at[place], counts_sems.at[index])
        for index, place in enumerate(places)
    ]
    copies[0].start()

    for k in range(parts):
        start = pl.multiple_of((me ^ k) * width, width)
        whole[:, pl.ds(start, width)] = arrived[order.index(k)][...] if k else pack_ref[0:lats, neurons:].astype(BF16)
    diagonal = lax.broadcasted_iota(jnp.int32, (lats, LANES), 0) == lax.broadcasted_iota(jnp.int32, (lats, LANES), 1)
    spread = jnp.broadcast_to(pack_ref[lats + 1 : lats + 2, 0:LANES], (lats, LANES))
    column = jnp.sum(jnp.where(diagonal, spread, 0.0), axis=1, keepdims=True)
    delay = jnp.broadcast_to(column, (lats, LANES)).astype(jnp.int32)
    length = pack_ref[lats + 2 : lats + 3, 0:1].astype(jnp.int32)
    tiles = [whole[:, j * LANES : (j + 1) * LANES].astype(F32) for j in range(total // LANES)]
    for j, tile in enumerate(shift_tiles(tiles, delay, True)):
        shifted[0:lats, j * LANES : (j + 1) * LANES] = tile.astype(BF16)
    row = lax.broadcasted_iota(jnp.int32, (EXTRA, total), 0)
    shifted[lats:, :] = jnp.where(row < 3, 1.0, 0.0).astype(BF16)

    copies[1].start()

    load_ext[0:lats, :] = pack_ref[0:lats, 0:neurons].astype(BF16)
    bias = pack_ref[lats : lats + 1, 0:neurons]
    high = bias.astype(BF16).astype(F32)
    middle = (bias - high).astype(BF16).astype(F32)
    low = bias - high - middle
    row = lax.broadcasted_iota(jnp.int32, (EXTRA, neurons), 0)
    below = jnp.where(row == 0, high, jnp.where(row == 1, middle, jnp.where(row == 2, low, 0.0)))
    load_ext[lats:, :] = below.astype(BF16)

    blocks = [
        (slice(first, first + chunk), slice(begin, begin + step))
        for first in range(0, neurons, chunk)
        for begin in range(0, total, step)
    ]
    for rows, span in blocks:
        if rows.start < early:
            held[rows, span] = expected(load_ext[:, rows], shifted[:, span])
    spans = [slice(begin, begin + step) for begin in range(0, total, step)]
    for copy, place in zip(copies, [slice(0, cut), slice(cut, neurons)]):
        copy.wait()
        for rows, span in blocks:
            if place.start <= rows.start < place.stop:
                rate = held[rows, span] if rows.start < early else expected(load_ext[:, rows], shifted[:, span])
                resid_low[rows, span] = (rate - counts_ref[rows, span].astype(F32)).astype(BF16)
        for span in spans:
            part = jnp.dot(load_ext[0:lats, place], resid_low[place, span], preferred_element_type=F32)
            grad_shift[:, span] = grad_shift[:, span] + part if place.start else part

    bins = lax.broadcasted_iota(jnp.int32, (1, total), 1)
    tiles = []
    for j in range(total // LANES):
        span = slice(j * LANES, (j + 1) * LANES)
        tiles.append(jnp.where(bins[:, span] < length, grad_shift[:, span], 0.0))
    for j, tile in enumerate(shift_tiles(tiles, delay, False)):
        grad_shift[:, j * LANES : (j + 1) * LANES] = tile
    for k in range(parts):
        start = pl.multiple_of((me ^ k) * width, width)
        outs[k][...] = grad_shift[:, pl.ds(start, width)].astype(outs[k].dtype)


def load_kernel(lats, first, chunk, step, *refs):
    pack_ref, load_ext, shifted, counts_hbm = refs[:4]
    load_hbm, bias_hbm, counts_ref, held, load_ref, bias_ref, sems = refs[-7:]
    count, total = counts_ref.shape
    place = pl.ds(first, count)
    counts_copy = pltpu.make_async_copy(counts_hbm.at[place], counts_ref, sems.at[0])
    counts_copy.start()
    length = pack_ref[lats + 2 : lats + 3, 0:1].astype(jnp.int32)
    bins = lax.broadcasted_iota(jnp.int32, (1, total), 1)
    blocks = [(slice(begin, begin + chunk), range(0, total, step)) for begin in range(0, count, chunk)]

    def rate(rows, span):
        return expected(load_ext[:, first + rows.start : first + rows.stop], shifted[:, span])

    early = blocks[:-1] if len(blocks) > 2 else blocks
    for rows, starts in early:
        for at in starts:
            held[rows, at : at + step] = rate(rows, slice(at, at + step))
    counts_copy.wait()
    outward = []
    for index, (rows, starts) in enumerate(blocks):
        sums = jnp.zeros((chunk, LANES), F32)
        grad = jnp.zeros((chunk, lats), F32)
        for at in starts:
            span = slice(at, at + step)
            made = held[rows, span] if index < len(early) else rate(rows, span)
            resid = jnp.where(bins[:, span] < length, made - counts_ref[rows, span].astype(F32), 0.0)
            for j in range(step // LANES):
                sums = sums + resid[:, j * LANES : (j + 1) * LANES]
            grad = grad + lax.dot_general(
                resid.astype(BF16), shifted[0:lats, span], (((1,), (1,)), ((), ())), preferred_element_type=F32
            )
        load_ref[:, rows] = grad.T
        bias_ref[:, rows] = jnp.sum(sums.T, axis=0, keepdims=True)
        place = pl.ds(first + rows.start, chunk)
        outward.append(pltpu.make_async_copy(load_ref.at[:, rows], load_hbm.at[:, place], sems.at[2 * index + 1]))
        outward.append(pltpu.make_async_copy(bias_ref.at[:, rows], bias_hbm.at[:, place], sems.at[2 * index + 2]))
        for copy in outward[-2:]:
            copy.start()
    for copy in outward:
        copy.wait()


def encode(value):
    top = jnp.maximum(jnp.max(jnp.abs(value), axis=0, keepdims=True), 2.0**-100)
    power = jnp.ceil(jnp.log2(top)) - 14.0
    rows = jnp.broadcast_to(power, (8, value.shape[1]))
    return jnp.concatenate([value * jnp.exp2(-power), rows], axis=0).astype(jnp.float16)


def decode(code):
    power = code[-8:-7].astype(F32)
    return code[:-8].astype(F32) * jnp.exp2(power)


def per_device(region_count, neuron_count, counts, latents, loadings, bias, delays, recorded):
    neurons, total = counts.shape[1:]
    lats, width = latents.shape
    chunk, step = 256, 512
    vmem = pl.BlockSpec(memory_space=pltpu.VMEM)
    hbm = pl.BlockSpec(memory_space=pltpu.HBM)
    params = pltpu.CompilerParams(vmem_limit_bytes=52 * 1024 * 1024)

    def swap(value, axis, count, mask):
        return lax.ppermute(value, axis, [(i, i ^ mask) for i in range(count)])

    order = [1, *range(neuron_count - 1, 1, -1)]
    arrived = [swap(latents, "neuron", neuron_count, k) for k in order]
    row = lax.broadcasted_iota(jnp.int32, (lats + 8, neurons + width), 0)
    lines = jnp.pad(delays, ((lats + 1, 6), (0, neurons + width - lats)))
    lines = jnp.where(row == lats + 2, jnp.broadcast_to(recorded[:, None], lines.shape), lines)
    pack = jnp.pad(bias, ((lats, 7), (0, width))) + lines.astype(F32)
    pack = pack + jnp.pad(loadings[0], ((0, 8), (0, width))).astype(F32)
    pack = pack + jnp.pad(latents, ((0, 8), (neurons, 0))).astype(F32)

    *outs, load_ext, shifted = pl.pallas_call(
        functools.partial(shift_kernel, neuron_count, order, "neuron", chunk, step),
        out_shape=[jax.ShapeDtypeStruct((lats, width), BF16 if k else F32) for k in range(neuron_count)]
        + [jax.ShapeDtypeStruct((lats + EXTRA, neurons), BF16), jax.ShapeDtypeStruct((lats + EXTRA, total), BF16)],
        in_specs=[vmem, hbm] + [vmem] * (neuron_count - 1),
        out_specs=[vmem] * (neuron_count + 2),
        scratch_shapes=[
            pltpu.VMEM((lats, total), BF16),
            pltpu.VMEM((neurons, total), BF16),
            pltpu.VMEM((4 * chunk, total), F32),
            pltpu.VMEM((neurons, total), BF16),
            pltpu.VMEM((lats, total), F32),
            pltpu.SemaphoreType.DMA((2,)),
        ],
        compiler_params=params,
    )(pack, counts[0], *arrived)

    shares = [(0, 2 * chunk), (2 * chunk, neurons - 2 * chunk)]
    made = []

    def make(before):
        first, count = shares.pop(0)
        before, start_load = lax.optimization_barrier((before, load_ext))
        out = pl.pallas_call(
            functools.partial(load_kernel, lats, first, chunk, step),
            out_shape=[jax.ShapeDtypeStruct((lats, neurons), F32), jax.ShapeDtypeStruct((1, neurons), F32)],
            in_specs=[vmem, vmem, vmem, hbm] + [hbm] * len(made),
            out_specs=[hbm, hbm],
            scratch_shapes=[
                pltpu.VMEM((count, total), BF16),
                pltpu.VMEM((count, total), F32),
                pltpu.VMEM((lats, count), F32),
                pltpu.VMEM((1, count), F32),
                pltpu.SemaphoreType.DMA((1 + 2 * (count // chunk),)),
            ],
            input_output_aliases={4 + i: i for i in range(len(made))},
            compiler_params=params,
            cost_estimate=pl.CostEstimate(
                flops=4 * lats * count * total, bytes_accessed=2 * count * total, transcendentals=count * total
            ),
        )(pack, start_load, shifted, counts[0], *made)
        return before, out

    outs, made = make(outs)
    arrived = [swap(outs[k], "neuron", neuron_count, k) for k in range(1, neuron_count)]
    arrived, made = lax.optimization_barrier((arrived, made))
    value = functools.reduce(jnp.add, [outs[0]] + [block.astype(F32) for block in arrived])
    mask = 1
    while mask < region_count:
        masks = [mask, 2 * mask, 3 * mask] if 2 * mask < region_count else [mask]
        if len(masks) == 3:
            value = lax.reduce_precision(value, 8, 7)
            sent, read = value.astype(BF16), lambda block: block.astype(F32)
        else:
            sent, read = lax.optimization_barrier(encode(value)), decode
            value = decode(sent)
        if shares:
            (value, sent), made = make((value, sent))
        turns = sorted(masks, key=lambda k: (k != mask, -k))
        arrived = [swap(sent, "region", region_count, k) for k in turns]
        arrived, made = lax.optimization_barrier((arrived, made))
        arrived = [arrived[turns.index(k)] for k in masks]
        value = value + read(arrived[0])
        if len(masks) == 3:
            value = value + (read(arrived[1]) + read(arrived[2]))
        mask *= 1 + len(masks)
    grad_load, grad_bias = made
    return (value, grad_load[None], grad_bias)


def solution(mesh):
    placed = (
        P("region", "neuron", None),
        P(None, "neuron"),
        P("region", None, "neuron"),
        P("region", "neuron"),
        P("region", None),
        P("region"),
    )
    return jax.shard_map(
        functools.partial(per_device, mesh.shape["region"], mesh.shape["neuron"]),
        mesh=mesh,
        in_specs=placed,
        out_specs=(P(None, "neuron"), P("region", None, "neuron"), P("region", "neuron")),
        check_vma=False,
    )
```

```python
import functools

import jax
import jax.numpy as jnp
from jax import lax
from jax.experimental import pallas as pl
from jax.experimental.pallas import tpu as pltpu
from jax.sharding import PartitionSpec as P

LANES = 128
EXTRA = 16
F32 = jnp.float32
BF16 = jnp.bfloat16


def shift_tiles(tiles, delay, forward):
    lane = lax.broadcasted_iota(jnp.int32, delay.shape, 1)
    source = lane - delay if forward else lane + delay
    inside = source >= 0 if forward else source < LANES
    source = source & (LANES - 1)
    turned = [jnp.take_along_axis(tile, source, axis=1, mode="promise_in_bounds") for tile in tiles]
    nothing = [jnp.zeros_like(tiles[0])]
    others = nothing + turned[:-1] if forward else turned[1:] + nothing
    return [jnp.where(inside, tile, other) for tile, other in zip(turned, others)]


def expected(load_part, piece):
    eta = lax.dot_general(load_part, piece, (((0,), (0,)), ((), ())), preferred_element_type=F32)
    return jnp.exp(eta)


def shift_kernel(parts, order, axis, chunk, step, *refs):
    pack_ref, counts_hbm = refs[:2]
    arrived = refs[2 : 1 + parts]
    outs = refs[1 + parts : 1 + 2 * parts]
    load_ext, shifted, whole, counts_ref, held, resid_low, grad_shift, counts_sems = refs[1 + 2 * parts :]
    me = lax.axis_index(axis)
    lats, total = grad_shift.shape
    neurons = counts_ref.shape[0]
    width = total // parts
    cut, late = 3 * chunk, chunk
    places = [pl.ds(0, cut), pl.ds(cut, neurons - cut)]
    copies = [
        pltpu.make_async_copy(counts_hbm.at[place], counts_ref.at[place], counts_sems.at[index])
        for index, place in enumerate(places)
    ]
    copies[0].start()

    for k in range(parts):
        start = pl.multiple_of((me ^ k) * width, width)
        whole[:, pl.ds(start, width)] = arrived[order.index(k)][...] if k else pack_ref[0:lats, neurons:].astype(BF16)
    diagonal = lax.broadcasted_iota(jnp.int32, (lats, LANES), 0) == lax.broadcasted_iota(jnp.int32, (lats, LANES), 1)
    spread = jnp.broadcast_to(pack_ref[lats + 1 : lats + 2, 0:LANES], (lats, LANES))
    column = jnp.sum(jnp.where(diagonal, spread, 0.0), axis=1, keepdims=True)
    delay = jnp.broadcast_to(column, (lats, LANES)).astype(jnp.int32)
    length = pack_ref[lats + 2 : lats + 3, 0:1].astype(jnp.int32)
    tiles = [whole[:, j * LANES : (j + 1) * LANES].astype(F32) for j in range(total // LANES)]
    for j, tile in enumerate(shift_tiles(tiles, delay, True)):
        shifted[0:lats, j * LANES : (j + 1) * LANES] = tile.astype(BF16)
    row = lax.broadcasted_iota(jnp.int32, (EXTRA, total), 0)
    shifted[lats:, :] = jnp.where(row < 3, 1.0, 0.0).astype(BF16)

    copies[1].start()

    load_ext[0:lats, :] = pack_ref[0:lats, 0:neurons].astype(BF16)
    bias = pack_ref[lats : lats + 1, 0:neurons]
    high = bias.astype(BF16).astype(F32)
    middle = (bias - high).astype(BF16).astype(F32)
    low = bias - high - middle
    row = lax.broadcasted_iota(jnp.int32, (EXTRA, neurons), 0)
    below = jnp.where(row == 0, high, jnp.where(row == 1, middle, jnp.where(row == 2, low, 0.0)))
    load_ext[lats:, :] = below.astype(BF16)

    blocks = [
        (slice(first, first + chunk), slice(begin, begin + step))
        for first in range(0, neurons, chunk)
        for begin in range(0, total, step)
    ]
    for rows, span in blocks:
        if rows.start >= late:
            held[rows, span] = expected(load_ext[:, rows], shifted[:, span])
    spans = [slice(begin, begin + step) for begin in range(0, total, step)]
    for copy, place in zip(copies, [slice(0, cut), slice(cut, neurons)]):
        copy.wait()
        for rows, span in blocks:
            if place.start <= rows.start < place.stop:
                rate = held[rows, span] if rows.start >= late else expected(load_ext[:, rows], shifted[:, span])
                resid_low[rows, span] = (rate - counts_ref[rows, span].astype(F32)).astype(BF16)
        for span in spans:
            part = jnp.dot(load_ext[0:lats, place], resid_low[place, span], preferred_element_type=F32)
            grad_shift[:, span] = grad_shift[:, span] + part if place.start else part

    bins = lax.broadcasted_iota(jnp.int32, (1, total), 1)
    tiles = []
    for j in range(total // LANES):
        span = slice(j * LANES, (j + 1) * LANES)
        tiles.append(jnp.where(bins[:, span] < length, grad_shift[:, span], 0.0))
    for j, tile in enumerate(shift_tiles(tiles, delay, False)):
        grad_shift[:, j * LANES : (j + 1) * LANES] = tile
    for k in range(parts):
        start = pl.multiple_of((me ^ k) * width, width)
        outs[k][...] = grad_shift[:, pl.ds(start, width)].astype(outs[k].dtype)


def load_kernel(lats, first, chunk, step, *refs):
    pack_ref, load_ext, shifted, counts_hbm = refs[:4]
    load_hbm, bias_hbm, counts_ref, held, load_ref, bias_ref, sems = refs[-7:]
    count, total = counts_ref.shape
    place = pl.ds(first, count)
    counts_copy = pltpu.make_async_copy(counts_hbm.at[place], counts_ref, sems.at[0])
    counts_copy.start()
    length = pack_ref[lats + 2 : lats + 3, 0:1].astype(jnp.int32)
    bins = lax.broadcasted_iota(jnp.int32, (1, total), 1)
    blocks = [(slice(begin, begin + chunk), range(0, total, step)) for begin in range(0, count, chunk)]

    def rate(rows, span):
        return expected(load_ext[:, first + rows.start : first + rows.stop], shifted[:, span])

    early = blocks[:-1] if len(blocks) > 2 else blocks
    for rows, starts in early:
        for at in starts:
            held[rows, at : at + step] = rate(rows, slice(at, at + step))
    counts_copy.wait()
    outward = []
    for index, (rows, starts) in enumerate(blocks):
        sums = jnp.zeros((chunk, LANES), F32)
        grad = jnp.zeros((chunk, lats), F32)
        for at in starts:
            span = slice(at, at + step)
            made = held[rows, span] if index < len(early) else rate(rows, span)
            resid = jnp.where(bins[:, span] < length, made - counts_ref[rows, span].astype(F32), 0.0)
            for j in range(step // LANES):
                sums = sums + resid[:, j * LANES : (j + 1) * LANES]
            grad = grad + lax.dot_general(
                resid.astype(BF16), shifted[0:lats, span], (((1,), (1,)), ((), ())), preferred_element_type=F32
            )
        load_ref[:, rows] = grad.T
        bias_ref[:, rows] = jnp.sum(sums.T, axis=0, keepdims=True)
        place = pl.ds(first + rows.start, chunk)
        outward.append(pltpu.make_async_copy(load_ref.at[:, rows], load_hbm.at[:, place], sems.at[2 * index + 1]))
        outward.append(pltpu.make_async_copy(bias_ref.at[:, rows], bias_hbm.at[:, place], sems.at[2 * index + 2]))
        for copy in outward[-2:]:
            copy.start()
    for copy in outward:
        copy.wait()


def encode(value):
    top = jnp.maximum(jnp.max(jnp.abs(value), axis=0, keepdims=True), 2.0**-100)
    power = jnp.ceil(jnp.log2(top)) - 14.0
    rows = jnp.broadcast_to(power, (8, value.shape[1]))
    return jnp.concatenate([value * jnp.exp2(-power), rows], axis=0).astype(jnp.float16)


def decode(code):
    power = code[-8:-7].astype(F32)
    return code[:-8].astype(F32) * jnp.exp2(power)


def per_device(region_count, neuron_count, counts, latents, loadings, bias, delays, recorded):
    neurons, total = counts.shape[1:]
    lats, width = latents.shape
    chunk, step = 256, 512
    vmem = pl.BlockSpec(memory_space=pltpu.VMEM)
    hbm = pl.BlockSpec(memory_space=pltpu.HBM)
    params = pltpu.CompilerParams(vmem_limit_bytes=52 * 1024 * 1024)

    def swap(value, axis, count, mask):
        return lax.ppermute(value, axis, [(i, i ^ mask) for i in range(count)])

    order = [1, *range(neuron_count - 1, 1, -1)]
    arrived = [swap(latents, "neuron", neuron_count, k) for k in order]
    row = lax.broadcasted_iota(jnp.int32, (lats + 8, neurons + width), 0)
    lines = jnp.pad(delays, ((lats + 1, 6), (0, neurons + width - lats)))
    lines = jnp.where(row == lats + 2, jnp.broadcast_to(recorded[:, None], lines.shape), lines)
    pack = jnp.pad(bias, ((lats, 7), (0, width))) + lines.astype(F32)
    pack = pack + jnp.pad(loadings[0], ((0, 8), (0, width))).astype(F32)
    pack = pack + jnp.pad(latents, ((0, 8), (neurons, 0))).astype(F32)

    *outs, load_ext, shifted = pl.pallas_call(
        functools.partial(shift_kernel, neuron_count, order, "neuron", chunk, step),
        out_shape=[jax.ShapeDtypeStruct((lats, width), BF16 if k > 1 else F32) for k in range(neuron_count)]
        + [jax.ShapeDtypeStruct((lats + EXTRA, neurons), BF16), jax.ShapeDtypeStruct((lats + EXTRA, total), BF16)],
        in_specs=[vmem, hbm] + [vmem] * (neuron_count - 1),
        out_specs=[vmem] * (neuron_count + 2),
        scratch_shapes=[
            pltpu.VMEM((lats, total), BF16),
            pltpu.VMEM((neurons, total), BF16),
            pltpu.VMEM((neurons, total), F32),
            pltpu.VMEM((neurons, total), BF16),
            pltpu.VMEM((lats, total), F32),
            pltpu.SemaphoreType.DMA((2,)),
        ],
        compiler_params=params,
    )(pack, counts[0], *arrived)

    shares = [(0, 2 * chunk), (2 * chunk, neurons - 2 * chunk)]
    made = []

    def make(before):
        first, count = shares.pop(0)
        before, start_load = lax.optimization_barrier((before, load_ext))
        out = pl.pallas_call(
            functools.partial(load_kernel, lats, first, chunk, step),
            out_shape=[jax.ShapeDtypeStruct((lats, neurons), F32), jax.ShapeDtypeStruct((1, neurons), F32)],
            in_specs=[vmem, vmem, vmem, hbm] + [hbm] * len(made),
            out_specs=[hbm, hbm],
            scratch_shapes=[
                pltpu.VMEM((count, total), BF16),
                pltpu.VMEM((count, total), F32),
                pltpu.VMEM((lats, count), F32),
                pltpu.VMEM((1, count), F32),
                pltpu.SemaphoreType.DMA((1 + 2 * (count // chunk),)),
            ],
            input_output_aliases={4 + i: i for i in range(len(made))},
            compiler_params=params,
            cost_estimate=pl.CostEstimate(
                flops=4 * lats * count * total, bytes_accessed=2 * count * total, transcendentals=count * total
            ),
        )(pack, start_load, shifted, counts[0], *made)
        return before, out

    outs, made = make(outs)
    arrived = [swap(outs[k], "neuron", neuron_count, k) for k in [*range(2, neuron_count), 1]]
    arrived, made = lax.optimization_barrier((arrived, made))
    value = functools.reduce(jnp.add, [outs[0]] + [block.astype(F32) for block in arrived])
    mask = 1
    while mask < region_count:
        masks = [mask, 2 * mask, 3 * mask] if 2 * mask < region_count else [mask]
        if len(masks) == 3:
            value = lax.reduce_precision(value, 8, 7)
            sent, read = value.astype(BF16), lambda block: block.astype(F32)
        else:
            sent, read = lax.optimization_barrier(encode(value)), decode
            value = decode(sent)
        if shares:
            (value, sent), made = make((value, sent))
        turns = sorted(masks, key=lambda k: (k != mask, -k))
        arrived = [swap(sent, "region", region_count, k) for k in turns]
        arrived, made = lax.optimization_barrier((arrived, made))
        arrived = [arrived[turns.index(k)] for k in masks]
        value = value + read(arrived[0])
        if len(masks) == 3:
            value = value + (read(arrived[1]) + read(arrived[2]))
        mask *= 1 + len(masks)
    grad_load, grad_bias = made
    return (value, grad_load[None], grad_bias)


def solution(mesh):
    placed = (
        P("region", "neuron", None),
        P(None, "neuron"),
        P("region", None, "neuron"),
        P("region", "neuron"),
        P("region", None),
        P("region"),
    )
    return jax.shard_map(
        functools.partial(per_device, mesh.shape["region"], mesh.shape["neuron"]),
        mesh=mesh,
        in_specs=placed,
        out_specs=(P(None, "neuron"), P("region", None, "neuron"), P("region", "neuron")),
        check_vma=False,
    )
```

```python
import functools

import jax
import jax.numpy as jnp
from jax import lax
from jax.experimental import pallas as pl
from jax.experimental.pallas import tpu as pltpu
from jax.sharding import PartitionSpec as P

LANES = 128
EXTRA = 16
F32 = jnp.float32
BF16 = jnp.bfloat16


def shift_tiles(tiles, delay, forward):
    lane = lax.broadcasted_iota(jnp.int32, delay.shape, 1)
    source = lane - delay if forward else lane + delay
    inside = source >= 0 if forward else source < LANES
    source = source & (LANES - 1)
    turned = [jnp.take_along_axis(tile, source, axis=1, mode="promise_in_bounds") for tile in tiles]
    nothing = [jnp.zeros_like(tiles[0])]
    others = nothing + turned[:-1] if forward else turned[1:] + nothing
    return [jnp.where(inside, tile, other) for tile, other in zip(turned, others)]


def expected(load_part, piece):
    eta = lax.dot_general(load_part, piece, (((0,), (0,)), ((), ())), preferred_element_type=F32)
    return jnp.exp(eta)


def shift_kernel(parts, order, axis, chunk, step, *refs):
    pack_ref, counts_hbm = refs[:2]
    arrived = refs[2 : 1 + parts]
    outs = refs[1 + parts : 1 + 2 * parts]
    load_ext, shifted, whole, counts_ref, held, resid_low, grad_shift, counts_sems = refs[1 + 2 * parts :]
    me = lax.axis_index(axis)
    lats, total = grad_shift.shape
    early = held.shape[0]
    neurons = counts_ref.shape[0]
    width = total // parts
    cut = 3 * chunk
    places = [pl.ds(0, cut), pl.ds(cut, neurons - cut)]
    copies = [
        pltpu.make_async_copy(counts_hbm.at[place], counts_ref.at[place], counts_sems.at[index])
        for index, place in enumerate(places)
    ]
    copies[0].start()

    for k in range(parts):
        start = pl.multiple_of((me ^ k) * width, width)
        whole[:, pl.ds(start, width)] = arrived[order.index(k)][...] if k else pack_ref[0:lats, neurons:].astype(BF16)
    diagonal = lax.broadcasted_iota(jnp.int32, (lats, LANES), 0) == lax.broadcasted_iota(jnp.int32, (lats, LANES), 1)
    spread = jnp.broadcast_to(pack_ref[lats + 1 : lats + 2, 0:LANES], (lats, LANES))
    column = jnp.sum(jnp.where(diagonal, spread, 0.0), axis=1, keepdims=True)
    delay = jnp.broadcast_to(column, (lats, LANES)).astype(jnp.int32)
    length = pack_ref[lats + 2 : lats + 3, 0:1].astype(jnp.int32)
    tiles = [whole[:, j * LANES : (j + 1) * LANES].astype(F32) for j in range(total // LANES)]
    for j, tile in enumerate(shift_tiles(tiles, delay, True)):
        shifted[0:lats, j * LANES : (j + 1) * LANES] = tile.astype(BF16)
    row = lax.broadcasted_iota(jnp.int32, (EXTRA, total), 0)
    shifted[lats:, :] = jnp.where(row < 3, 1.0, 0.0).astype(BF16)

    copies[1].start()

    load_ext[0:lats, :] = pack_ref[0:lats, 0:neurons].astype(BF16)
    bias = pack_ref[lats : lats + 1, 0:neurons]
    high = bias.astype(BF16).astype(F32)
    middle = (bias - high).astype(BF16).astype(F32)
    low = bias - high - middle
    row = lax.broadcasted_iota(jnp.int32, (EXTRA, neurons), 0)
    below = jnp.where(row == 0, high, jnp.where(row == 1, middle, jnp.where(row == 2, low, 0.0)))
    load_ext[lats:, :] = below.astype(BF16)

    blocks = [
        (slice(first, first + chunk), slice(begin, begin + step))
        for first in range(0, neurons, chunk)
        for begin in range(0, total, step)
    ]
    for rows, span in blocks:
        if rows.start < early:
            held[rows, span] = expected(load_ext[:, rows], shifted[:, span])
    spans = [slice(begin, begin + step) for begin in range(0, total, step)]
    for copy, place in zip(copies, [slice(0, cut), slice(cut, neurons)]):
        copy.wait()
        for rows, span in blocks:
            if place.start <= rows.start < place.stop:
                rate = held[rows, span] if rows.start < early else expected(load_ext[:, rows], shifted[:, span])
                resid_low[rows, span] = (rate - counts_ref[rows, span].astype(F32)).astype(BF16)
        for span in spans:
            part = jnp.dot(load_ext[0:lats, place], resid_low[place, span], preferred_element_type=F32)
            grad_shift[:, span] = grad_shift[:, span] + part if place.start else part

    bins = lax.broadcasted_iota(jnp.int32, (1, total), 1)
    tiles = []
    for j in range(total // LANES):
        span = slice(j * LANES, (j + 1) * LANES)
        tiles.append(jnp.where(bins[:, span] < length, grad_shift[:, span], 0.0))
    for j, tile in enumerate(shift_tiles(tiles, delay, False)):
        grad_shift[:, j * LANES : (j + 1) * LANES] = tile
    for k in range(parts):
        start = pl.multiple_of((me ^ k) * width, width)
        outs[k][...] = grad_shift[:, pl.ds(start, width)].astype(outs[k].dtype)


def load_kernel(lats, first, chunk, step, *refs):
    pack_ref, load_ext, shifted, counts_hbm = refs[:4]
    load_hbm, bias_hbm, counts_ref, held, load_ref, bias_ref, sems = refs[-7:]
    count, total = counts_ref.shape
    place = pl.ds(first, count)
    counts_copy = pltpu.make_async_copy(counts_hbm.at[place], counts_ref, sems.at[0])
    counts_copy.start()
    length = pack_ref[lats + 2 : lats + 3, 0:1].astype(jnp.int32)
    bins = lax.broadcasted_iota(jnp.int32, (1, total), 1)
    blocks = [(slice(begin, begin + chunk), range(0, total, step)) for begin in range(0, count, chunk)]

    def rate(rows, span):
        return expected(load_ext[:, first + rows.start : first + rows.stop], shifted[:, span])

    early = blocks[:-1] if len(blocks) > 2 else blocks
    for rows, starts in early:
        for at in starts:
            held[rows, at : at + step] = rate(rows, slice(at, at + step))
    counts_copy.wait()
    outward = []
    for index, (rows, starts) in enumerate(blocks):
        sums = jnp.zeros((chunk, LANES), F32)
        grad = jnp.zeros((chunk, lats), F32)
        for at in starts:
            span = slice(at, at + step)
            made = held[rows, span] if index < len(early) else rate(rows, span)
            resid = jnp.where(bins[:, span] < length, made - counts_ref[rows, span].astype(F32), 0.0)
            for j in range(step // LANES):
                sums = sums + resid[:, j * LANES : (j + 1) * LANES]
            grad = grad + lax.dot_general(
                resid.astype(BF16), shifted[0:lats, span], (((1,), (1,)), ((), ())), preferred_element_type=F32
            )
        load_ref[:, rows] = grad.T
        bias_ref[:, rows] = jnp.sum(sums.T, axis=0, keepdims=True)
        place = pl.ds(first + rows.start, chunk)
        outward.append(pltpu.make_async_copy(load_ref.at[:, rows], load_hbm.at[:, place], sems.at[2 * index + 1]))
        outward.append(pltpu.make_async_copy(bias_ref.at[:, rows], bias_hbm.at[:, place], sems.at[2 * index + 2]))
        for copy in outward[-2:]:
            copy.start()
    for copy in outward:
        copy.wait()


def encode(value):
    top = jnp.maximum(jnp.max(jnp.abs(value), axis=0, keepdims=True), 2.0**-100)
    power = jnp.ceil(jnp.log2(top)) - 14.0
    rows = jnp.broadcast_to(power, (8, value.shape[1]))
    return jnp.concatenate([value * jnp.exp2(-power), rows], axis=0).astype(jnp.float16)


def decode(code):
    power = code[-8:-7].astype(F32)
    return code[:-8].astype(F32) * jnp.exp2(power)


def per_device(region_count, neuron_count, counts, latents, loadings, bias, delays, recorded):
    neurons, total = counts.shape[1:]
    lats, width = latents.shape
    chunk, step = 256, 512
    vmem = pl.BlockSpec(memory_space=pltpu.VMEM)
    hbm = pl.BlockSpec(memory_space=pltpu.HBM)
    params = pltpu.CompilerParams(vmem_limit_bytes=52 * 1024 * 1024)

    def swap(value, axis, count, mask):
        return lax.ppermute(value, axis, [(i, i ^ mask) for i in range(count)])

    order = [1, *range(neuron_count - 1, 1, -1)]
    arrived = [swap(latents, "neuron", neuron_count, k) for k in order]
    row = lax.broadcasted_iota(jnp.int32, (lats + 8, neurons + width), 0)
    lines = jnp.pad(delays, ((lats + 1, 6), (0, neurons + width - lats)))
    lines = jnp.where(row == lats + 2, jnp.broadcast_to(recorded[:, None], lines.shape), lines)
    pack = jnp.pad(bias, ((lats, 7), (0, width))) + lines.astype(F32)
    pack = pack + jnp.pad(loadings[0], ((0, 8), (0, width))).astype(F32)
    pack = pack + jnp.pad(latents, ((0, 8), (neurons, 0))).astype(F32)

    *outs, load_ext, shifted = pl.pallas_call(
        functools.partial(shift_kernel, neuron_count, order, "neuron", chunk, step),
        out_shape=[jax.ShapeDtypeStruct((lats, width), BF16 if k > 1 else F32) for k in range(neuron_count)]
        + [jax.ShapeDtypeStruct((lats + EXTRA, neurons), BF16), jax.ShapeDtypeStruct((lats + EXTRA, total), BF16)],
        in_specs=[vmem, hbm] + [vmem] * (neuron_count - 1),
        out_specs=[vmem] * (neuron_count + 2),
        scratch_shapes=[
            pltpu.VMEM((lats, total), BF16),
            pltpu.VMEM((neurons, total), BF16),
            pltpu.VMEM((4 * chunk, total), F32),
            pltpu.VMEM((neurons, total), BF16),
            pltpu.VMEM((lats, total), F32),
            pltpu.SemaphoreType.DMA((2,)),
        ],
        compiler_params=params,
    )(pack, counts[0], *arrived)

    shares = [(0, 2 * chunk), (2 * chunk, neurons - 2 * chunk)]
    made = []

    def make(before):
        first, count = shares.pop(0)
        before, start_load = lax.optimization_barrier((before, load_ext))
        out = pl.pallas_call(
            functools.partial(load_kernel, lats, first, chunk, step),
            out_shape=[jax.ShapeDtypeStruct((lats, neurons), F32), jax.ShapeDtypeStruct((1, neurons), F32)],
            in_specs=[vmem, vmem, vmem, hbm] + [hbm] * len(made),
            out_specs=[hbm, hbm],
            scratch_shapes=[
                pltpu.VMEM((count, total), BF16),
                pltpu.VMEM((count, total), F32),
                pltpu.VMEM((lats, count), F32),
                pltpu.VMEM((1, count), F32),
                pltpu.SemaphoreType.DMA((1 + 2 * (count // chunk),)),
            ],
            input_output_aliases={4 + i: i for i in range(len(made))},
            compiler_params=params,
            cost_estimate=pl.CostEstimate(
                flops=4 * lats * count * total, bytes_accessed=2 * count * total, transcendentals=count * total
            ),
        )(pack, start_load, shifted, counts[0], *made)
        return before, out

    outs, made = make(outs)
    arrived = [swap(outs[k], "neuron", neuron_count, k) for k in [*range(2, neuron_count), 1]]
    arrived, made = lax.optimization_barrier((arrived, made))
    value = functools.reduce(jnp.add, [outs[0]] + [block.astype(F32) for block in arrived])
    mask = 1
    while mask < region_count:
        masks = [mask, 2 * mask, 3 * mask] if 2 * mask < region_count else [mask]
        if len(masks) == 3:
            value = lax.reduce_precision(value, 8, 7)
            sent, read = value.astype(BF16), lambda block: block.astype(F32)
        else:
            sent, read = lax.optimization_barrier(encode(value)), decode
            value = decode(sent)
        if shares:
            (value, sent), made = make((value, sent))
        turns = sorted(masks, key=lambda k: (k == 3 * mask, -k))
        arrived = [swap(sent, "region", region_count, k) for k in turns]
        arrived, made = lax.optimization_barrier((arrived, made))
        arrived = [arrived[turns.index(k)] for k in masks]
        value = value + read(arrived[0])
        if len(masks) == 3:
            value = value + (read(arrived[1]) + read(arrived[2]))
        mask *= 1 + len(masks)
    grad_load, grad_bias = made
    return (value, grad_load[None], grad_bias)


def solution(mesh):
    placed = (
        P("region", "neuron", None),
        P(None, "neuron"),
        P("region", None, "neuron"),
        P("region", "neuron"),
        P("region", None),
        P("region"),
    )
    return jax.shard_map(
        functools.partial(per_device, mesh.shape["region"], mesh.shape["neuron"]),
        mesh=mesh,
        in_specs=placed,
        out_specs=(P(None, "neuron"), P("region", None, "neuron"), P("region", "neuron")),
        check_vma=False,
    )
```
